32 devices in a mesh: chan: 4 (over y, core), space: 8 (over z, x).
Axes of the slice: x: 2, y: 2, z: 4, core: 2. Of those that a mesh axis runs over, the one named last changes fastest.
Arguments:
- features: bfloat16 [2, 256, 53760], P(None, 'chan', 'space'), may hold values from -6 to 6
- image_sizes: int32 [2, 192], replicated, may hold values from 10 to 18, as said below
- conv_in_w: bfloat16 [3, 3, 256, 512], P(None, None, 'chan'), may hold values from -0.125 to 0.125
- proj_w: bfloat16 [256, 512], P('chan'), may hold values from -0.375 to 0.375
- conv_mid_w: bfloat16 [3, 3, 3, 512, 512], P(None, None, None, 'chan'), may hold values from -0.09375 to 0.09375
- norm_gain: float32 [5, 512], P(None, 'chan'), may hold values from 0.1 to 1.9
- norm_bias: float32 [5, 512], P(None, 'chan'), may hold values from -2.5 to 2.5
- out_grad: bfloat16 [2, 512, 13440], P(None, 'chan', 'space'), may hold values from -6 to 6
Outputs:
- block_out: bfloat16 [2, 512, 13440], P(None, 'chan', 'space')
- feature_grad: float32 [2, 256, 53760], P(None, 'chan', 'space')
- conv_in_grad: float32 [3, 3, 256, 512], P(None, None, 'chan')
- proj_grad: float32 [256, 512], P('chan')
- conv_mid_grad: float32 [3, 3, 3, 512, 512], P(None, None, None, 'chan')
- gain_grad: float32 [5, 512], P(None, 'chan')
- bias_grad: float32 [5, 512], P(None, 'chan')
The draws below stay inside these ranges and needn't reach their ends.
Inputs may be any that keep to these rules, and one draw needn't show every extreme that they name: `image_sizes`: in each micro-batch a third of the 192 images have side 10, a third side 14 and a third side 18, in an order that varies.
All inputs are finite; a program needn't handle non-finite values.
Results may differ from the reference program's by a relative error of at most 0.033.
Values may be sent and summed in bfloat16 or wider, within the bound.
No kernel may reach another device: no remote copies, remote signals or barrier semaphores. Data moves between devices by JAX's collectives and lax.ppermute only.
A program may use at most 192 MiB of HBM per device.

```python
import jax
import jax.numpy as jnp
from jax import lax

C_IN = 256
C_OUT = 512
MICRO = 2
WIN = 20
IMGS = 192
NPOS_OUT = 13440
NPOS_IN = 53760


def draw_image_sizes(key, part):
    key = jax.random.fold_in(key, 11)
    micro_keys = jax.random.split(key, MICRO)
    orders = jax.vmap(lambda one_key: jax.random.permutation(one_key, IMGS))(micro_keys)
    return (10 + 4 * (orders % 3)).astype(jnp.int32)


def block_scale(stream_key, shape, cuts, low, largest):
    def one(axis_at, blocks):
        steps = jax.random.uniform(jax.random.fold_in(jax.random.fold_in(stream_key, 6), axis_at), (blocks,), jnp.float32, low / len(cuts), largest / len(cuts))
        return jnp.repeat(jnp.exp(steps), shape[axis_at] // blocks).reshape((-1,) + (1,) * (len(shape) - axis_at - 1))

    level = one(*cuts[0])
    for cut in cuts[1:]:
        level = level * one(*cut)
    return level


def scatter_about(own_key, shape, width, reach, cuts=(), kind=jnp.bfloat16):
    values = jax.random.normal(own_key, shape, jnp.float32) * width
    if len(cuts) > 0:
        values = block_scale(own_key, shape, cuts, -0.22, 0.18) * values
    return jnp.clip(values, min=-reach, max=reach).astype(kind)


def setup_inputs(seed: int = 0) -> dict:
    splits = jax.random.split(jax.random.key(seed), 9)
    return {
        "features": scatter_about(splits[0], (MICRO, C_IN, NPOS_IN), 1.0, 6.0, ((1, 4), (2, 8))),
        "image_sizes": draw_image_sizes(jax.random.fold_in(splits[8], 71), 0),
        "conv_in_w": scatter_about(splits[2], (3, 3, C_IN, C_OUT), (9 * C_IN) ** -0.5, 0.125, ((2, 4),)),
        "proj_w": scatter_about(splits[3], (C_IN, C_OUT), C_IN ** -0.5, 0.375, ((0, 4),)),
        "conv_mid_w": scatter_about(splits[4], (3, 3, 3, C_OUT, C_OUT), (9 * C_OUT) ** -0.5, 0.09375, ((3, 4),)),
        "norm_gain": jnp.clip(1.0 + 0.18 * jax.random.normal(splits[5], (5, C_OUT), jnp.float32), 0.1, 1.9),
        "norm_bias": scatter_about(splits[6], (5, C_OUT), 0.5, 2.5, ((1, 4),), jnp.float32),
        "out_grad": scatter_about(splits[7], (MICRO, C_OUT, NPOS_OUT), 1.0, 6.0, ((1, 4), (2, 8))),
    }


@jax.custom_vjp
def low(v):
    return lax.optimization_barrier(v.astype(jnp.bfloat16)).astype(jnp.float32)

@jax.custom_vjp
def low_back(v):
    return v

def low_keep(v):
    return (low(v), None)

def low_pass(kept, grad):
    return (grad,)

def back_keep(v):
    return (v, None)

def back_low(kept, grad):
    return (low(grad),)
low.defvjp(low_keep, low_pass)
low_back.defvjp(back_keep, back_low)
eps_norm = 1e-05
highest = lax.Precision.HIGHEST

def canvas_rows(sizes_row, first_row, row_count):
    sides_out = (sizes_row // 2).astype(jnp.int32)
    starts = (jnp.cumsum(sides_out) - sides_out).astype(jnp.int32)
    global_rows = (first_row + jnp.arange(row_count, dtype=jnp.int32)).astype(jnp.int32)
    inside = ((global_rows[:, None] >= starts[None, :]) & (global_rows[:, None] < (starts + sides_out)[None, :])).astype(jnp.int32)
    begins = lax.optimization_barrier(jnp.sum(inside * starts[None, :], axis=1)).astype(jnp.int32)
    widths = lax.optimization_barrier(jnp.sum(inside * sides_out[None, :], axis=1)).astype(jnp.int32)
    return ((global_rows - begins).astype(jnp.int32), widths)

def row_masks(local_rows, widths, columns):
    column_ids = jnp.arange(columns, dtype=jnp.int32)
    inside_mask = (column_ids[None, :] < widths[:, None]).astype(jnp.float32).reshape(-1)
    upper_mask = jnp.repeat(((local_rows > 0) & (widths > 0)).astype(jnp.float32), columns)
    lower_mask = jnp.repeat((local_rows < widths - 1).astype(jnp.float32), columns)
    return (inside_mask, upper_mask, lower_mask)

def input_mask(widths, columns):
    column_ids = jnp.arange(columns, dtype=jnp.int32)
    single = (column_ids[None, :] < 2 * widths[:, None]).astype(jnp.float32)
    return jnp.broadcast_to(single[:, None, :], (widths.shape[0], 2, columns)).reshape(-1)

def mid_columns(source_ext, upper_mask, lower_mask, width_out, position_count):
    pieces = []
    for row_step, row_keep in ((-1, upper_mask), (0, None), (1, lower_mask)):
        row_view = lax.slice_in_dim(source_ext, (1 + row_step) * width_out, (1 + row_step) * width_out + position_count, axis=1)
        if row_keep is not None:
            row_view = row_view * row_keep[None, :]
        padded = jnp.pad(row_view, ((0, 0), (1, 1)))
        for col_step in (-1, 0, 1):
            pieces.append(padded[:, 1 + col_step:1 + col_step + position_count])
    return jnp.concatenate(pieces, axis=0)

def entry_columns(source, prior_row, upper_mask, width_out):
    channels = source.shape[0]
    rows_out = source.shape[1] // (4 * width_out)
    position_count = rows_out * width_out
    phases = source.reshape(channels, rows_out, 2, width_out, 2)
    prior_split = prior_row.reshape(channels, width_out, 2)
    pieces = []
    for row_step in (-1, 0, 1):
        sources = []
        for parity in (0, 1):
            phase_view = phases[:, :, 0 if row_step == 0 else 1, :, parity].reshape(channels, position_count)
            if row_step == -1:
                phase_view = jnp.concatenate([prior_split[:, :, parity], phase_view], axis=1)[:, :position_count] * upper_mask[None, :]
            sources.append(phase_view)
        pieces.append(jnp.pad(sources[1], ((0, 0), (1, 0)))[:, :position_count])
        pieces.append(sources[0])
        pieces.append(sources[1])
    return jnp.concatenate(pieces, axis=0)

def silu_of(values):
    return values * jax.nn.sigmoid(values)

def batch_norm(source, inside_mask, total_count, gain_row, bias_row):
    mean_value = lax.optimization_barrier(jnp.sum(source * inside_mask[None, :], axis=1)) / total_count
    square_mean = lax.optimization_barrier(jnp.sum(source * source * inside_mask[None, :], axis=1)) / total_count
    inverse = lax.rsqrt(square_mean - mean_value * mean_value + eps_norm)
    scaled = (source - mean_value[:, None]) * inverse[:, None]
    return inside_mask[None, :] * (gain_row[:, None] * scaled + bias_row[:, None])

def mid_conv(source, weight, upper_mask, lower_mask, width_out):
    zero_row = jnp.zeros((source.shape[0], width_out), jnp.float32)
    source_ext = jnp.concatenate([zero_row, source, zero_row], axis=1)
    columns_mat = mid_columns(source_ext, upper_mask, lower_mask, width_out, source.shape[1])
    weight_mat = weight.reshape(9 * C_OUT, C_OUT)
    return jnp.dot(weight_mat.T, columns_mat, precision=highest, preferred_element_type=jnp.float32)

def one_micro(params, packed):
    weight_in, weight_proj, weight_mid, gains, biases = params
    feats, inside_in, inside_mask, upper_mask, lower_mask, total_count = packed
    width_out = WIN // 2
    source = feats * inside_in[None, :]
    zero_row = jnp.zeros((source.shape[0], WIN), jnp.float32)
    entry_cols = entry_columns(source, zero_row, upper_mask, width_out)
    entry_sum = low_back(jnp.dot(weight_in.reshape(9 * C_IN, C_OUT).T, entry_cols, precision=highest, preferred_element_type=jnp.float32))
    short_sum = low_back(jnp.dot(weight_proj.T, entry_cols[4 * C_IN:5 * C_IN], precision=highest, preferred_element_type=jnp.float32))
    first_low = low(silu_of(batch_norm(entry_sum, inside_mask, total_count, gains[0], biases[0])))
    second_sum = low_back(mid_conv(first_low, weight_mid[0], upper_mask, lower_mask, width_out))
    joined = silu_of(batch_norm(second_sum, inside_mask, total_count, gains[1], biases[1]) + batch_norm(short_sum, inside_mask, total_count, gains[2], biases[2]))
    joined_low = low(joined)
    third_sum = low_back(mid_conv(joined_low, weight_mid[1], upper_mask, lower_mask, width_out))
    third_low = low(silu_of(batch_norm(third_sum, inside_mask, total_count, gains[3], biases[3])))
    fourth_sum = low_back(mid_conv(third_low, weight_mid[2], upper_mask, lower_mask, width_out))
    return silu_of(batch_norm(fourth_sum, inside_mask, total_count, gains[4], biases[4]) + joined)

def reference(features, image_sizes, conv_in_w, proj_w, conv_mid_w, norm_gain, norm_bias, out_grad):
    width_out = WIN // 2
    rows_total = image_sizes.shape[1] * 7
    inside_in_list, inside_list, upper_list, lower_list, count_list = ([], [], [], [], [])
    for micro_index in range(MICRO):
        sizes_row = image_sizes[micro_index]
        local_rows, widths = canvas_rows(sizes_row, 0, rows_total)
        inside_mask, upper_mask, lower_mask = row_masks(local_rows, widths, width_out)
        inside_list.append(inside_mask)
        upper_list.append(upper_mask)
        lower_list.append(lower_mask)
        inside_in_list.append(input_mask(widths, WIN))
        sides_out = sizes_row // 2
        count_list.append(jnp.sum((sides_out * sides_out).astype(jnp.float32)))
    masks_all = (jnp.stack(inside_in_list), jnp.stack(inside_list), jnp.stack(upper_list), jnp.stack(lower_list), jnp.stack(count_list))
    step_fn = jax.checkpoint(one_micro)

    def forward(features_f, weight_in, weight_proj, weight_mid, gains, biases):
        params = (weight_in, weight_proj, weight_mid, gains, biases)
        return lax.map(lambda packed: step_fn(params, packed), (features_f,) + masks_all)
    outputs, pullback = jax.vjp(forward, features.astype(jnp.float32), conv_in_w.astype(jnp.float32), proj_w.astype(jnp.float32), conv_mid_w.astype(jnp.float32), norm_gain, norm_bias)
    grads = pullback(out_grad.astype(jnp.float32))
    return (outputs.astype(jnp.bfloat16), grads[0], grads[1], grads[2], grads[3], grads[4], grads[5])
```

```python
import collections
import functools

import jax
import jax.numpy as jnp
import numpy as np
from jax import lax
from jax.experimental import pallas as pl
from jax.experimental.pallas import tpu as pltpu
from jax.sharding import PartitionSpec as P

MICRO = 2
WIN = 20
MOST_SIDE = 9
EXTRA = MOST_SIDE - 1
BLOCK = 16
ROW_BLOCK = 64
GAP = 8
EPS = 1e-05
SLACK_BYTES = 6 * 1024 * 1024
LOW = jnp.bfloat16
FULL = jnp.float32

PLAN_FIELDS = ["chans", "spaces", "splits", "rows_dev", "own_rows", "bases", "pitch", "width"]
PLAN_FIELDS += ["spots", "chans_in", "chans_out", "wide"]
Plan = collections.namedtuple("Plan", PLAN_FIELDS)

VMEM = pl.BlockSpec(memory_space=pltpu.VMEM)
SMEM = pl.BlockSpec(memory_space=pltpu.SMEM)
HBM = pl.BlockSpec(memory_space=pltpu.HBM)


def flipped(value, axis, bit):
    count = lax.axis_size(axis)
    return lax.ppermute(value, axis, [(i, i ^ bit) for i in range(count)])


def from_next(value):
    count = lax.axis_size("space")
    return lax.ppermute(value, "space", [(i + 1, i) for i in range(count - 1)])


def to_next(value):
    count = lax.axis_size("space")
    return lax.ppermute(value, "space", [(i, i + 1) for i in range(count - 1)])


def exchanged(value, chan_bits, space_bits, plan):
    count = plan.chans * plan.spaces
    flip = chan_bits * plan.spaces + space_bits
    return lax.ppermute(value, ("chan", "space"), [(i, i ^ flip) for i in range(count)])


def tied(value, *others):
    return lax.optimization_barrier((value, others))[0]


def gathered(own, plan, then=()):
    parts = {0: own}
    for rel in range(1, plan.chans):
        bit = rel & -rel
        source = parts[rel ^ bit]
        if rel != bit and then:
            source = tied(source, *then)
        parts[rel] = flipped(source, "chan", bit)
    return [parts[rel] for rel in range(plan.chans)]


def swapped(parts, plan):
    return [parts[0]] + [flipped(parts[rel], "chan", rel) for rel in range(1, plan.chans)]


def micro_sums(value, plan, jobs=()):
    bits = []
    bit = 1
    while bit < plan.splits:
        bits.append((bit, 0))
        bit *= 2
    bit = 1
    while bit < plan.spaces:
        bits.append((0, bit))
        bit *= 2
    for i in range(0, len(bits), 2):
        pair = bits[i : i + 2]
        one = exchanged(value, *pair[0], plan)
        if len(pair) == 2:
            two = exchanged(value, *pair[1], plan)
            both = exchanged(value, pair[0][0] ^ pair[1][0], pair[0][1] ^ pair[1][1], plan)
        if i == 0 and jobs:
            one = tied(one, *[job() for job in jobs])
        value = value + one
        if len(pair) == 2:
            value = value + (two + both)
    return value


class WeightSum:
    def __init__(self, keep, send, plan, across_first):
        self.send, self.plan = send, plan
        self.pair = (keep, flipped(send, "chan", 1))
        chan_steps, space_steps = [], []
        bit = 2
        while bit < plan.chans:
            chan_steps.append(("chan", bit))
            bit *= 2
        bit = 1
        while bit < plan.spaces:
            space_steps.append(("space", bit))
            bit *= 2
        if across_first:
            self.steps = space_steps[:1] + chan_steps + space_steps[1:]
        else:
            self.steps = chan_steps + space_steps
        self.gathers = [bit for _, bit in space_steps[::-1]]
        self.whole = None

    def mine(self, bit):
        return (lax.axis_index("space") // bit) % 2

    def added(self, pick):
        kept, received = (pick(part).astype(FULL) for part in self.pair)
        return (kept + received).astype(LOW)

    def advance(self):
        if self.steps:
            axis, bit = self.steps.pop(0)
            if axis == "chan":
                kept = self.added(lambda part: part[0::2])
                sent = self.added(lambda part: part[1::2])
            else:
                half = self.pair[0].shape[1] // 2
                at = self.mine(bit) * half
                kept = self.added(lambda part: lax.dynamic_slice_in_dim(part, at, half, 1))
                sent = self.added(lambda part: lax.dynamic_slice_in_dim(part, half - at, half, 1))
            self.pair = (kept, flipped(sent, axis, bit))
            return sent
        bit = self.gathers.pop(0)
        if self.whole is None:
            self.whole = self.added(lambda part: part)[0]
        else:
            self.whole = self.ordered(*self.pair)
        self.pair = (self.whole, flipped(self.whole, "space", bit), bit)
        return self.whole

    def ordered(self, own, received, bit):
        low = jnp.concatenate([own, received], axis=0)
        high = jnp.concatenate([received, own], axis=0)
        return jnp.where(self.mine(bit) == 0, low, high)

    def halves(self):
        while self.steps or self.gathers:
            self.advance()
        return self.pair


def tiles(count, size):
    return [slice(i, i + size) for i in range(0, count, size)]


def logistic(u):
    return 1.0 / (1.0 + jnp.exp(-u))


def slope(u):
    g = logistic(u)
    return g * (1.0 + u * (1.0 - g))


def moments(stat, inv_count):
    mean = stat[0:1, :] * inv_count
    inverse = lax.rsqrt(stat[1:2, :] * inv_count - mean * mean + EPS)
    return mean, inverse


def dot(a, b):
    return lax.dot_general(a, b, (((1,), (0,)), ((), ())), preferred_element_type=FULL)


def dot_t(a, b):
    return lax.dot_general(a, b, (((1,), (1,)), ((), ())), preferred_element_type=FULL)


def unit(count):
    rows = lax.broadcasted_iota(jnp.int32, (count, count), 0)
    columns = lax.broadcasted_iota(jnp.int32, (count, count), 1)
    return jnp.where(rows == columns, 1.0, 0.0).astype(LOW)


def clear_gaps(ref, spots):
    zero = jnp.zeros((GAP, ref.shape[-1]), ref.dtype)
    ref[pl.ds(0, GAP), :] = zero
    ref[pl.ds(GAP + spots, GAP), :] = zero


def column_sum(x):
    return jnp.sum(x, axis=0, keepdims=True)


def start_shards(chan, shard_refs, w_ref, sems):
    size = shard_refs[0].shape[2]
    copies = []
    for rel, ref in enumerate(shard_refs):
        place = pl.ds(pl.multiple_of((chan ^ rel) * size, size), size)
        copy = pltpu.make_async_copy(ref, w_ref.at[:, :, place, :], sems.at[rel])
        copy.start()
        copies.append(copy)
    return copies


def matmul_tile(plan):
    for size in (288, 192, 144, 96, 64):
        if plan.spots % size == 0:
            return size
    return plan.spots


def vector_tile(plan):
    return 2 * plan.pitch // 4 if plan.pitch % 32 == 0 else plan.pitch


def spread_features_kernel(plan, chan_ref, x_ref, halo_ref, picks_ref, left_ref, right_ref, out_ref):
    chan = chan_ref[0]
    size, lanes = plan.chans_in, BLOCK * 4 * plan.width
    columns = MOST_SIDE

    def stacked(part):
        blank = jnp.zeros_like(part[0])
        even, odd = [], []
        for m in range(MICRO):
            even += [part[m], blank]
            odd += [blank, part[m]]
        return jnp.concatenate(even, 0), jnp.concatenate(odd, 0)

    have = x_ref.shape[2]
    for j in range(-(-(plan.rows_dev + EXTRA) // BLOCK)):
        start = j * lanes
        if start + lanes <= have:
            even, odd = stacked([x_ref[m, :, start : start + lanes] for m in range(MICRO)])
            result = dot_t(picks_ref[0], even) + dot_t(picks_ref[1], odd)
        else:
            even, odd = stacked([x_ref[m, :, start:have] for m in range(MICRO)])
            result = dot_t(left_ref[0], even) + dot_t(left_ref[1], odd)
            even, odd = stacked([halo_ref[m] for m in range(MICRO)])
            result += dot_t(right_ref[0], even) + dot_t(right_ref[1], odd)
        result = result.astype(LOW)
        for split, base in enumerate(plan.bases):
            row = j * BLOCK - base
            if row < 0 or row >= plan.pitch:
                continue
            for m in range(MICRO):
                to = chan ^ (m * plan.splits + split)
                for phase in range(2):
                    for c in range(columns):
                        at = (phase * columns + c) * BLOCK
                        part = result[at : at + BLOCK, m * 2 * size : (m + 1) * 2 * size]
                        spot = c * plan.pitch + row
                        out_ref[to, phase, spot : spot + BLOCK] = part


def spread_rows_kernel(plan, chan_ref, x_ref, halo_ref, pick_ref, left_ref, right_ref, out_ref):
    chan = chan_ref[0]
    size, spots = plan.chans_out, ROW_BLOCK * plan.width
    have = x_ref.shape[1]
    for j in range(-(-(plan.rows_dev + EXTRA) // ROW_BLOCK)):
        start = j * spots
        for m in range(MICRO):
            if start + spots <= have:
                result = dot(pick_ref[...], x_ref[m, start : start + spots])
            else:
                result = dot(left_ref[...], x_ref[m, start:have]) + dot(right_ref[...], halo_ref[m])
            result = result.astype(LOW)
            for split, base in enumerate(plan.bases):
                low, high = max(j * ROW_BLOCK, base), min((j + 1) * ROW_BLOCK, base + plan.pitch)
                if low >= high:
                    continue
                to = chan ^ (m * plan.splits + split)
                for c in range(MOST_SIDE):
                    at = c * ROW_BLOCK + low - j * ROW_BLOCK
                    spot = c * plan.pitch + low - base
                    out_ref[to, spot : spot + high - low] = result[at : at + high - low]


def laid_rows(plan, whole_ref, m, c, low, high, phase=None):
    pieces = []
    for row in range(low, high, BLOCK):
        total = None
        for split, base in enumerate(plan.bases):
            if not base <= row < base + plan.pitch:
                continue
            spots = pl.ds(c * plan.pitch + row - base, BLOCK)
            at = m * plan.splits + split
            part = whole_ref[at, spots] if phase is None else whole_ref[at, phase, spots]
            total = part if total is None else total + part
        pieces.append(total)
    return pieces


def join_rows_kernel(plan, chan_ref, picks_ref, left_ref, right_ref, *refs):
    parts = refs[: plan.chans]
    out_ref, tail_ref, whole_ref = refs[plan.chans :]
    chan = chan_ref[0]
    for rel in range(plan.chans):
        whole_ref[chan ^ rel] = parts[rel][...]
    spots = ROW_BLOCK * plan.width
    have = out_ref.shape[1]
    limit = plan.rows_dev + EXTRA
    for j in range(-(-limit // ROW_BLOCK)):
        start = j * spots
        low, high = j * ROW_BLOCK, min((j + 1) * ROW_BLOCK, limit)
        for m in range(MICRO):
            pieces = []
            for c in range(MOST_SIDE):
                pieces += laid_rows(plan, whole_ref, m, c, low, high)
                if high - low < ROW_BLOCK:
                    blank = (ROW_BLOCK - high + low, plan.chans_out)
                    pieces.append(jnp.zeros(blank, LOW))
            rows = jnp.concatenate(pieces, 0)
            if start + spots <= have:
                out_ref[m, start : start + spots] = dot(picks_ref[...], rows).astype(LOW)
            else:
                out_ref[m, start:have] = dot(left_ref[...], rows).astype(LOW)
                tail_ref[m] = dot(right_ref[...], rows).astype(LOW)


def join_features_kernel(plan, chan_ref, picks_ref, left_ref, right_ref, *refs):
    parts = refs[: plan.chans]
    out_ref, tail_ref, whole_ref = refs[plan.chans :]
    chan = chan_ref[0]
    for rel in range(plan.chans):
        whole_ref[chan ^ rel] = parts[rel][...]
    size = plan.chans_in
    one = unit(2 * size)
    lanes = BLOCK * 4 * plan.width
    have = out_ref.shape[2]
    for j in range(-(-(plan.rows_dev + EXTRA) // BLOCK)):
        start = j * lanes
        first, second = [], []
        for m in range(MICRO):
            pieces = []
            for phase in range(2):
                for c in range(MOST_SIDE):
                    row = j * BLOCK
                    pieces += laid_rows(plan, whole_ref, m, c, row, row + BLOCK, phase)
            turned = dot_t(one, jnp.concatenate(pieces, 0)).astype(LOW)
            first.append(turned[:size])
            second.append(turned[size:])
        first, second = jnp.concatenate(first, 0), jnp.concatenate(second, 0)
        if start + lanes <= have:
            result = dot(first, picks_ref[0]) + dot(second, picks_ref[1])
            for m in range(MICRO):
                out_ref[m, :, start : start + lanes] = result[m * size : (m + 1) * size]
        else:
            result = dot(first, left_ref[0]) + dot(second, left_ref[1])
            tail = dot(first, right_ref[0]) + dot(second, right_ref[1])
            for m in range(MICRO):
                out_ref[m, :, start:have] = result[m * size : (m + 1) * size]
                tail_ref[m] = tail[m * size : (m + 1) * size].astype(LOW)


def entry_copies(plan, shard_refs, w_ref, wp_ref, sems):
    copies = []
    for rel in range(plan.chans):
        for a in range(3):
            sem = sems.at[7 * rel + 2 * a]
            source = shard_refs[rel].at[pl.ds(3 * a + 1, 2)]
            copies.append(pltpu.make_async_copy(source, w_ref.at[a, 0, rel], sem))
            sem = sems.at[7 * rel + 2 * a + 1]
            source = shard_refs[rel].at[3 * a]
            copies.append(pltpu.make_async_copy(source, w_ref.at[a, 1, rel, 1], sem))
        source = shard_refs[rel].at[9]
        copies.append(pltpu.make_async_copy(source, wp_ref.at[rel, 0], sems.at[7 * rel + 6]))
    for copy in copies:
        copy.start()
    for rel in range(plan.chans):
        blank = jnp.zeros(wp_ref.shape[2:], LOW)
        wp_ref[rel, 1] = blank
        for a in range(3):
            w_ref[a, 1, rel, 0] = blank
    return copies


def entry_forward_kernel(plan, marks_ref, *refs):
    n = plan.chans
    x_refs, shard_refs = refs[:n], refs[n : 2 * n]
    e_ref, p_ref, stat_ref, xm_ref = refs[2 * n : 2 * n + 4]
    w_ref, wp_ref, xs_ref, am_ref, sems = refs[2 * n + 4 :]
    copies = entry_copies(plan, shard_refs, w_ref, wp_ref, sems)
    size = 2 * plan.chans_in
    deep = n * size
    pitch = plan.pitch
    for k in range(3):
        am_ref[k, 0:pitch] = jnp.zeros((pitch, deep), LOW)
    clear_gaps(xs_ref, plan.spots)
    for rel in range(n):
        lanes = slice(rel * size, (rel + 1) * size)
        for t in tiles(plan.spots, vector_tile(plan)):
            own = marks_ref[t, 0:1]
            for row in range(2):
                value = x_refs[rel][row, t].astype(FULL) * own
                low = value.astype(LOW)
                xm_ref[row, t, lanes] = low
                am_ref[row, pitch + t.start : pitch + t.stop, lanes] = low
                if row == 1:
                    xs_ref[GAP + t.start : GAP + t.stop, lanes] = value
    for t in tiles(plan.spots, vector_tile(plan)):
        above = xs_ref[GAP + t.start - 1 : GAP + t.stop - 1] * marks_ref[t, 1:2]
        am_ref[2, pitch + t.start : pitch + t.stop] = above.astype(LOW)
    for copy in copies:
        copy.wait()
    weights = w_ref[...].reshape(6 * deep, plan.wide)
    proj = wp_ref[...].reshape(deep, plan.wide)
    sums = [0.0] * 4
    for t in tiles(plan.spots, matmul_tile(plan)):
        own = marks_ref[t, 0:1]
        pieces = []
        for k in (2, 0, 1):
            pieces.append(am_ref[k, pitch + t.start : pitch + t.stop])
            pieces.append(am_ref[k, t])
        z = dot(jnp.concatenate(pieces, 1), weights)
        e_ref[t] = z
        p = dot(pieces[2], proj)
        p_ref[t] = p
        zm, pm = z * own, p * own
        for i, term in enumerate((zm, zm * z, pm, pm * p)):
            sums[i] = sums[i] + column_sum(term)
    stat_ref[...] = jnp.concatenate(sums, 0)


def mid_forward_kernel(plan, layers, chan_ref, inv_ref, marks_ref, par_ref, *refs):
    k = len(layers)
    n = plan.chans
    z_refs, stat_refs, shard_refs = refs[:k], refs[k : 2 * k], refs[2 * k : 2 * k + n]
    outs = refs[2 * k + n :]
    if k == 2:
        z_ref, out_stat_ref, a_ref, h_ref, w_ref, xs_ref, xa_ref, sems = outs
    else:
        z_ref, out_stat_ref, a_ref, w_ref, xs_ref, xa_ref, sems = outs
        h_ref = None
    copies = start_shards(chan_ref[0], shard_refs, w_ref, sems)
    inv = inv_ref[0]
    norms = [moments(stat[...], inv) for stat in stat_refs]
    wide, pitch = plan.wide, plan.pitch
    clear_gaps(xs_ref, plan.spots)
    for i in range(3):
        blank = jnp.zeros((pitch, wide), LOW)
        xa_ref[i, 0:pitch] = blank
        xa_ref[i, pitch + plan.spots : 2 * pitch + plan.spots] = blank
    for t in tiles(plan.spots, vector_tile(plan)):
        own = marks_ref[t, 0:1]
        u = 0.0
        for (mean, inverse), src, j in zip(norms, z_refs, layers):
            u = u + (par_ref[j : j + 1] * ((src[t] - mean) * inverse) + par_ref[5 + j : 6 + j])
        u = u * own
        a = u * logistic(u)
        if h_ref is not None:
            h_ref[t] = a
        xs_ref[GAP + t.start : GAP + t.stop] = a
        low = a.astype(LOW)
        a_ref[t] = low
        xa_ref[1, pitch + t.start : pitch + t.stop] = low
    for t in tiles(plan.spots, vector_tile(plan)):
        for i, step in ((0, -1), (2, 1)):
            part = xs_ref[GAP + t.start + step : GAP + t.stop + step]
            part = part * marks_ref[t, 1 + i // 2 : 2 + i // 2]
            xa_ref[i, pitch + t.start : pitch + t.stop] = part.astype(LOW)
    for copy in copies:
        copy.wait()
    weights = w_ref[...].reshape(9 * wide, wide)
    total, square = 0.0, 0.0
    for t in tiles(plan.spots, matmul_tile(plan)):
        own = marks_ref[t, 0:1]
        pieces = []
        for a in range(3):
            for b in range(3):
                pieces.append(xa_ref[a, t.start + b * pitch : t.stop + b * pitch])
        z = dot(jnp.concatenate(pieces, 1), weights)
        z_ref[t] = z
        zm = z * own
        total = total + column_sum(zm)
        square = square + column_sum(zm * z)
    out_stat_ref[...] = jnp.concatenate([total, square], 0)


def head_kernel(plan, chan_ref, inv_ref, marks_ref, par_ref, z_ref, stat_ref, h_ref, *refs):
    n = plan.chans
    og_refs = refs[:n]
    out_ref, g_ref, out_stat_ref, og_ref = refs[n:]
    chan = chan_ref[0]
    for rel in range(n):
        og_ref[chan ^ rel] = og_refs[rel][...]
    mean, inverse = moments(stat_ref[...], inv_ref[0])
    size = plan.chans_out
    for j in range(n):
        lanes = slice(j * size, (j + 1) * size)
        total, dotted = 0.0, 0.0
        for t in tiles(plan.spots, plan.pitch):
            own = marks_ref[t, 0:1]
            hat = (z_ref[t, lanes] - mean[:, lanes]) * inverse[:, lanes]
            u = own * (par_ref[4:5, lanes] * hat + par_ref[9:10, lanes]) + h_ref[t, lanes]
            s = logistic(u)
            out_ref[chan ^ j, t] = (u * s).astype(LOW)
            q = og_ref[j, t].astype(FULL) * (s * (1.0 + u * (1.0 - s))) * own
            g_ref[t, lanes] = q
            total = total + column_sum(q)
            dotted = dotted + column_sum(q * hat)
        out_stat_ref[0:1, lanes] = total
        out_stat_ref[1:2, lanes] = dotted


def norm_back(own, q, z, norm, gain, total, dotted, inv):
    mean, inverse = norm
    hat = (z - mean) * inverse
    return own * (gain * inverse) * (q - total * inv - hat * (dotted * inv))


def mid_backward_kernel(plan, j, kind, chan_ref, inv_ref, marks_ref, par_ref, *refs):
    n = plan.chans
    g_ref, z_ref, stat_ref, back_ref = refs[:4]
    shard_refs = refs[4 : 4 + n]
    refs = refs[4 + n :]
    add_ref = short_z_ref = None
    if kind == "join":
        src_refs, src_stats, add_ref = refs[:2], refs[2:4], refs[4]
        refs = refs[5:]
        layers = (1, 2)
    elif kind == "entry":
        src_refs, src_stats, short_z_ref, short_stat_ref = refs[:1], refs[1:2], refs[2], refs[3]
        refs = refs[4:]
        layers = (0,)
    else:
        src_refs, src_stats = refs[:1], refs[1:2]
        refs = refs[2:]
        layers = (3,)
    ga_ref, next_ref, out_stat_ref = refs[:3]
    refs = refs[3:]
    if kind == "entry":
        short_ref, refs = refs[0], refs[1:]
    w_ref, s0_ref, s2_ref, sems = refs
    copies = start_shards(chan_ref[0], shard_refs, w_ref, sems)
    inv = inv_ref[0]
    wide, pitch = plan.wide, plan.pitch
    norm = moments(stat_ref[...], inv)
    total, dotted = back_ref[0:1], back_ref[1:2]
    for ref in (s0_ref, s2_ref):
        clear_gaps(ref, plan.spots)
    for i in range(3):
        blank = jnp.zeros((pitch, wide), LOW)
        ga_ref[i, 0:pitch] = blank
        ga_ref[i, pitch + plan.spots : 2 * pitch + plan.spots] = blank
    if kind == "entry":
        short_norm = moments(short_stat_ref[...], inv)
    for t in tiles(plan.spots, vector_tile(plan)):
        own, upper, lower = (marks_ref[t, i : i + 1] for i in range(3))
        g = g_ref[t]
        gz = norm_back(own, g, z_ref[t], norm, par_ref[j : j + 1], total, dotted, inv)
        low = gz.astype(LOW)
        gz = low.astype(FULL)
        ga_ref[1, pitch + t.start : pitch + t.stop] = low
        s0_ref[GAP + t.start : GAP + t.stop] = gz * upper
        s2_ref[GAP + t.start : GAP + t.stop] = gz * lower
        if kind == "entry":
            back = norm_back(
                own, g, short_z_ref[t], short_norm, par_ref[2:3], total, back_ref[2:3], inv
            )
            short_ref[t] = back.astype(LOW)
    for t in tiles(plan.spots, vector_tile(plan)):
        first, last = GAP + t.start, GAP + t.stop
        to = slice(pitch + t.start, pitch + t.stop)
        ga_ref[0, to] = s0_ref[first + 1 : last + 1].astype(LOW)
        ga_ref[2, to] = s2_ref[first - 1 : last - 1].astype(LOW)
    for copy in copies:
        copy.wait()
    norms = [moments(stat[...], inv) for stat in src_stats]
    sums = [0.0] * (1 + len(layers))
    weights = jnp.concatenate([w_ref[a, b] for a in range(3) for b in range(3)], 1)
    for t in tiles(plan.spots, matmul_tile(plan)):
        own = marks_ref[t, 0:1]
        pieces = []
        for a in range(3):
            for b in range(3):
                back = (2 - b) * pitch
                pieces.append(ga_ref[a, t.start + back : t.stop + back])
        gx = dot_t(jnp.concatenate(pieces, 1), weights)
        u = 0.0
        hats = []
        for (mean, inverse), src, i in zip(norms, src_refs, layers):
            hat = (src[t] - mean) * inverse
            hats.append(hat)
            u = u + (par_ref[i : i + 1] * hat + par_ref[5 + i : 6 + i])
        u = u * own
        if add_ref is not None:
            gx = gx + add_ref[t]
        q = gx * slope(u) * own
        next_ref[t] = q
        sums[0] = sums[0] + column_sum(q)
        for i, hat in enumerate(hats):
            sums[1 + i] = sums[1 + i] + column_sum(q * hat)
    out_stat_ref[...] = jnp.concatenate(sums, 0)


def entry_norm_kernel(plan, inv_ref, marks_ref, par_ref, g_ref, e_ref, stat_ref, back_ref, gm_ref, s_ref):
    inv = inv_ref[0]
    norm = moments(stat_ref[...], inv)
    clear_gaps(s_ref, plan.spots)
    for k in range(2):
        gm_ref[k, plan.spots : plan.spots + plan.pitch] = jnp.zeros((plan.pitch, plan.wide), LOW)
    for t in tiles(plan.spots, vector_tile(plan)):
        own, upper = marks_ref[t, 0:1], marks_ref[t, 1:2]
        gz = norm_back(
            own, g_ref[t], e_ref[t], norm, par_ref[0:1], back_ref[0:1], back_ref[1:2], inv
        )
        low = gz.astype(LOW)
        gm_ref[0, t] = low
        s_ref[GAP + t.start : GAP + t.stop] = low.astype(FULL) * upper
    for t in tiles(plan.spots, vector_tile(plan)):
        gm_ref[1, t] = s_ref[GAP + t.start + 1 : GAP + t.stop + 1].astype(LOW)


def entry_backward_kernel(plan, marks_ref, gm_ref, short_ref, *refs):
    n = plan.chans
    shard_refs = refs[:n]
    gx_ref, w_ref, wp_ref, sems = refs[n:]
    for copy in entry_copies(plan, shard_refs, w_ref, wp_ref, sems):
        copy.wait()
    size = 2 * plan.chans_in
    deep = n * size
    pitch, wide = plan.pitch, plan.wide

    def part(a, side):
        return w_ref[a, side].reshape(deep, wide)

    top_weights = [part(1, 0), part(1, 1), wp_ref[...].reshape(deep, wide)]
    top_weights = jnp.concatenate(top_weights, 1)
    low_weights = jnp.concatenate([part(2, 0), part(2, 1), part(0, 0), part(0, 1)], 1)
    for t in tiles(plan.spots, matmul_tile(plan)):
        own = marks_ref[t, 0:1]
        right = slice(t.start + pitch, t.stop + pitch)
        here = [gm_ref[0, t], gm_ref[0, right]]
        top = dot_t(jnp.concatenate(here + [short_ref[t]], 1), top_weights)
        here += [gm_ref[1, t], gm_ref[1, right]]
        low = dot_t(jnp.concatenate(here, 1), low_weights)
        for row, value in enumerate((top, low)):
            value = (value * own).astype(LOW)
            for rel in range(n):
                gx_ref[rel, row, t] = value[:, rel * size : (rel + 1) * size]


def mid_weight_kernel(plan, chan_ref, a_ref, ga_ref, keep_ref, send_ref, turned_ref, at_ref):
    wide, pitch = plan.wide, plan.pitch
    turned_ref[...] = dot_t(unit(wide), a_ref[...]).astype(LOW)
    chan = chan_ref[0]
    size = plan.chans_out
    for rel in range(plan.chans):
        place = pl.ds(pl.multiple_of((chan ^ rel) * size, size), size)
        at_ref[rel * size : (rel + 1) * size] = turned_ref[place]
    for a in range(3):
        for b in range(3):
            back = (2 - b) * pitch
            rows = slice((3 * a + b) * size, (3 * a + b + 1) * size)
            part = dot(at_ref[...], ga_ref[a, back : back + plan.spots]).astype(LOW)
            for rel in range(plan.chans):
                target = send_ref if rel & 1 else keep_ref
                target[rel // 2, rows] = part[rel * size : (rel + 1) * size]


def entry_weight_kernel(plan, xm_ref, gm_ref, short_ref, keep_ref, send_ref, xt_ref):
    n, size, wide, pitch = plan.chans, plan.chans_in, plan.wide, plan.pitch
    whole = unit(n * 2 * size)
    for row in range(2):
        xt_ref[row] = dot_t(whole, xm_ref[row]).astype(LOW)

    def put(tap, rel, value):
        target = send_ref if rel & 1 else keep_ref
        target[rel // 2, tap * size : (tap + 1) * size] = value

    def product(row, right):
        return dot(xt_ref[row], right).astype(LOW)

    for row, grad, a in ((0, 0, 1), (1, 0, 2), (1, 1, 0)):
        big = product(row, gm_ref[grad, 0 : plan.spots])
        side = product(row, gm_ref[grad, pitch : pitch + plan.spots])
        for rel in range(n):
            at = 2 * rel * size
            put(3 * a + 1, rel, big[at : at + size])
            put(3 * a + 2, rel, big[at + size : at + 2 * size])
            put(3 * a, rel, side[at + size : at + 2 * size])
    proj = product(0, short_ref[...])
    for rel in range(n):
        put(9, rel, proj[2 * rel * size : (2 * rel + 1) * size])


def mid_assembly_kernel(count, mine_ref, *refs):
    parts, out_ref, hold_ref, sems = refs[: 2 * count], *refs[2 * count :]
    half = parts[0].shape[0]
    copies = []
    for i, part in enumerate(parts):
        hold_ref[i] = part[...].astype(FULL)
        at = mine_ref[0] if i % 2 == 0 else 1 - mine_ref[0]
        rows = pl.ds(pl.multiple_of(at * half, 8), half)
        copy = pltpu.make_async_copy(hold_ref.at[i], out_ref.at[i // 2, rows], sems.at[i])
        copy.start()
        copies.append(copy)
    for copy in copies:
        copy.wait()


def entry_assembly_kernel(mine_ref, own_ref, other_ref, conv_ref, proj_ref, hold_ref, sems):
    half = own_ref.shape[0]
    for i, part in enumerate((own_ref, other_ref)):
        at = mine_ref[0] if i == 0 else 1 - mine_ref[0]
        hold_ref[pl.ds(pl.multiple_of(at * half, 8), half)] = part[...].astype(FULL)
    cut = conv_ref.shape[0]
    copies = [
        pltpu.make_async_copy(hold_ref.at[pl.ds(0, cut)], conv_ref, sems.at[0]),
        pltpu.make_async_copy(hold_ref.at[pl.ds(cut, proj_ref.shape[0])], proj_ref, sems.at[1]),
    ]
    for copy in copies:
        copy.start()
    for copy in copies:
        copy.wait()


def call(kernel, operands, specs, outs, out_specs, scratch, flops, name):
    bytes_moved = sum(int(np.prod(o.shape)) * o.dtype.itemsize for o in operands)
    bytes_moved += sum(int(np.prod(s)) * jnp.dtype(d).itemsize for s, d in outs)
    shapes = [jax.ShapeDtypeStruct(s, d) for s, d in outs]
    held = SLACK_BYTES
    for one in scratch:
        if one.memory_space == pltpu.VMEM:
            held += int(np.prod(one.shape)) * jnp.dtype(one.dtype).itemsize
    return pl.pallas_call(
        kernel,
        out_shape=shapes,
        in_specs=specs,
        out_specs=out_specs,
        scratch_shapes=scratch,
        compiler_params=pltpu.CompilerParams(vmem_limit_bytes=held),
        cost_estimate=pl.CostEstimate(
            flops=int(flops), bytes_accessed=int(bytes_moved), transcendentals=0
        ),
        name=name,
    )(*operands)


def feature_picks(plan):
    width, columns = plan.width, MOST_SIDE
    picks = np.zeros((2, 2 * columns * BLOCK, BLOCK * 4 * width), np.float32)
    for side in range(2):
        for phase in range(2):
            for c in range(columns):
                for r in range(BLOCK):
                    source = (2 * r + phase) * 2 * width + 2 * c + side
                    picks[side, (phase * columns + c) * BLOCK + r, source] = 1.0
    return picks


def row_picks(plan):
    width = plan.width
    picks = np.zeros((MOST_SIDE * ROW_BLOCK, ROW_BLOCK * width), np.float32)
    for c in range(MOST_SIDE):
        for r in range(ROW_BLOCK):
            picks[c * ROW_BLOCK + r, r * width + c] = 1.0
    return picks


def cut_picks(picks, rows, per_row, rows_dev, turned=False):
    own = rows_dev % rows * per_row
    extra = EXTRA * per_row
    parts = (picks, picks[..., :own], picks[..., own : own + extra])
    return [jnp.asarray((part.T if turned else part).astype(LOW)) for part in parts]


def marks_of(plan, sizes, top, first):
    sides = sizes // 2
    starts = jnp.cumsum(sides) - sides
    here = top + jnp.arange(plan.pitch, dtype=jnp.int32)
    inside = (
        (here[:, None] >= starts[None, :]) & (here[:, None] < (starts + sides)[None, :])
    ).astype(jnp.int32)
    begins = jnp.sum(inside * starts[None, :], axis=1)
    widths = jnp.sum(inside * sides[None, :], axis=1)
    local = here - begins
    owned = (widths > 0) & (begins >= first) & (begins < first + plan.own_rows)
    columns = jnp.arange(MOST_SIDE, dtype=jnp.int32)
    own = owned[None, :] & (columns[:, None] < widths[None, :])
    upper = jnp.broadcast_to((owned & (local > 0))[None, :], own.shape)
    lower = jnp.broadcast_to((owned & (local < widths - 1))[None, :], own.shape)
    marks = jnp.stack([own, upper, lower] + [jnp.zeros_like(own)] * 5, axis=-1)
    total = jnp.sum((sides * sides).astype(FULL))
    return marks.astype(FULL).reshape(plan.spots, 8), (1.0 / total).reshape(1)


def shards(features, image_sizes, conv_in_w, proj_w, conv_mid_w, norm_gain, norm_bias, out_grad):
    chans, spaces = lax.axis_size("chan"), lax.axis_size("space")
    splits = chans // MICRO
    width = WIN // 2
    rows_dev = features.shape[2] // (4 * width)
    own_rows = rows_dev // splits
    bases = tuple(split * own_rows // BLOCK * BLOCK for split in range(splits))
    need = max(split * own_rows - bases[split] for split in range(splits)) + own_rows + EXTRA
    pitch = -(-need // BLOCK) * BLOCK
    reach = -(-(rows_dev + EXTRA) // BLOCK) * BLOCK
    assert max(bases) + pitch <= reach and rows_dev + EXTRA == reach
    chans_in, chans_out = features.shape[1], norm_gain.shape[1]
    spots = MOST_SIDE * pitch
    plan = Plan(
        chans, spaces, splits, rows_dev, own_rows, bases, pitch, width, spots,
        chans_in, chans_out, chans * chans_out,
    )
    wide = plan.wide
    chan = lax.axis_index("chan")
    micro, split = chan // splits, chan % splits
    here = lax.axis_index("space") * rows_dev
    first = here + split * own_rows
    chan_at = chan.astype(jnp.int32).reshape(1)

    picks = cut_picks(feature_picks(plan), BLOCK, 4 * width, rows_dev)
    halo = from_next(features[:, :, : EXTRA * 4 * width])
    (spread,) = call(
        functools.partial(spread_features_kernel, plan),
        (chan_at, features, halo, *picks),
        [SMEM] + [VMEM] * 5,
        [((chans, 2, spots, 2 * chans_in), LOW)],
        [VMEM],
        [],
        2 * 2 * 2 * spots * 640 * chans * 2 * chans_in,
        "spread_features",
    )
    x_parts = swapped(spread, plan)
    entry_own = jnp.concatenate([conv_in_w.reshape(9, chans_in, wide), proj_w[None]], axis=0)
    entry_shards = gathered(entry_own, plan)

    slots = jnp.concatenate([norm_gain, norm_bias], axis=0)
    slots = lax.dynamic_update_slice(
        jnp.zeros((10, wide), FULL), slots, (jnp.int32(0), chan * chans_out)
    )
    bit = 1
    while bit < chans:
        slots = slots + flipped(slots, "chan", bit)
        bit *= 2
    pars = slots
    mid_first = tied(conv_mid_w[0], *x_parts, *entry_shards, pars)

    sizes = lax.dynamic_index_in_dim(image_sizes, micro, 0, keepdims=False)
    bases_at = jnp.asarray(bases, jnp.int32)[split]
    marks, inv = marks_of(plan, sizes, here + bases_at, first)

    conv_flops = 2 * spots * 9 * wide * wide
    field = ((spots, wide), FULL)
    deep = chans * 2 * chans_in
    entry_scratch = [
        pltpu.VMEM((3, 2, chans, 2, chans_in, wide), LOW),
        pltpu.VMEM((chans, 2, chans_in, wide), LOW),
    ]
    padded = pltpu.VMEM((spots + 2 * GAP, wide), FULL)
    z0, zp, stats, xm = call(
        functools.partial(entry_forward_kernel, plan),
        (marks, *x_parts, *entry_shards),
        [VMEM] * (1 + chans) + [HBM] * chans,
        [field, field, ((4, wide), FULL), ((2, spots, deep), LOW)],
        [VMEM] * 4,
        entry_scratch
        + [
            pltpu.VMEM((spots + 2 * GAP, deep), FULL),
            pltpu.VMEM((3, spots + pitch, deep), LOW),
            pltpu.SemaphoreType.DMA((7 * chans,)),
        ],
        2 * spots * 7 * deep * wide,
        "entry_forward",
    )
    mid_shards = [gathered(mid_first, plan, (stats,))]
    mid_second = tied(conv_mid_w[1], stats)
    stats = micro_sums(stats, plan)
    stat0, statp = stats[0:2], stats[2:4]

    weight_scratch = pltpu.VMEM((3, 3, wide, wide), LOW)
    shard_sems = pltpu.SemaphoreType.DMA((chans,))

    def mid_forward(layers, sources, source_stats, weights, name):
        outs = [field, ((2, wide), FULL), ((spots, wide), LOW)]
        if len(layers) == 2:
            outs.append(field)
        k = len(layers)
        return call(
            functools.partial(mid_forward_kernel, plan, layers),
            (chan_at, inv, marks, pars, *sources, *source_stats, *weights),
            [SMEM, SMEM] + [VMEM] * (2 + 2 * k) + [HBM] * chans,
            outs,
            [VMEM] * len(outs),
            [weight_scratch, padded, pltpu.VMEM((3, spots + 2 * pitch, wide), LOW), shard_sems],
            conv_flops,
            name,
        )

    z2, stat1, a_first = mid_forward((0,), (z0,), (stat0,), mid_shards[0], "mid_forward_a")
    mid_shards.append(gathered(mid_second, plan, (stat1,)))
    mid_third = tied(conv_mid_w[2], stat1)
    picks_out = cut_picks(row_picks(plan), ROW_BLOCK, width, rows_dev)
    picks_back = cut_picks(row_picks(plan), ROW_BLOCK, width, rows_dev, True)
    out_grad = jnp.swapaxes(out_grad, 1, 2)
    halo = from_next(out_grad[:, : EXTRA * width])
    (grad_spread,) = call(
        functools.partial(spread_rows_kernel, plan),
        (chan_at, out_grad, halo, *picks_out),
        [SMEM] + [VMEM] * 5,
        [((chans, spots, chans_out), LOW)],
        [VMEM],
        [],
        2 * spots * 640 * wide,
        "spread_rows",
    )
    og_parts = swapped(tied(grad_spread, stat1), plan)
    stat1 = micro_sums(stat1, plan)
    z3, stat3, a_second, h1 = mid_forward(
        (1, 2), (z2, zp), (stat1, statp), mid_shards[1], "mid_forward_b"
    )
    mid_shards.append(gathered(mid_third, plan, (stat3,)))
    stat3 = micro_sums(stat3, plan)
    z4, stat4, a_third = mid_forward((3,), (z3,), (stat3,), mid_shards[2], "mid_forward_c")
    stat4 = micro_sums(stat4, plan)

    block, gh2, back4 = call(
        functools.partial(head_kernel, plan),
        (chan_at, inv, marks, pars, z4, stat4, h1, *og_parts),
        [SMEM, SMEM] + [VMEM] * (5 + chans),
        [((chans, spots, chans_out), LOW), field, ((2, wide), FULL)],
        [VMEM] * 3,
        [pltpu.VMEM((chans, spots, chans_out), LOW)],
        spots * wide * 30,
        "head",
    )
    back4 = micro_sums(back4, plan)

    def mid_backward(j, kind, g, z, stat, back, weights, others, extra_outs, name):
        count = 3 if kind == "join" else 2
        outs = [((3, spots + 2 * pitch, wide), LOW), field, ((count, wide), FULL)] + extra_outs
        return call(
            functools.partial(mid_backward_kernel, plan, j, kind),
            (chan_at, inv, marks, pars, g, z, stat, back, *weights, *others),
            [SMEM, SMEM] + [VMEM] * 6 + [HBM] * chans + [VMEM] * len(others),
            outs,
            [VMEM] * len(outs),
            [weight_scratch, padded, padded, shard_sems],
            conv_flops,
            name,
        )

    def mid_weight(a, ga, name, across_first):
        keep, send = call(
            functools.partial(mid_weight_kernel, plan),
            (chan_at, a, ga),
            [SMEM, VMEM, VMEM],
            [((chans // 2, 9 * chans_out, wide), LOW)] * 2,
            [VMEM, VMEM],
            [pltpu.VMEM((wide, spots), LOW)] * 2,
            conv_flops,
            name,
        )
        return WeightSum(keep, send, plan, across_first)

    ga_third, g3, back3 = mid_backward(
        4, "plain", gh2, z4, stat4, back4, mid_shards[2], (z3, stat3), [], "mid_backward_c"
    )
    third = mid_weight(a_third, ga_third, "mid_weight_c", False)
    back3 = micro_sums(back3, plan, [lambda: third.send])
    ga_second, gh1, back12 = mid_backward(
        3, "join", g3, z3, stat3, back3, mid_shards[1], (z2, zp, stat1, statp, gh2), [],
        "mid_backward_b",
    )
    second = mid_weight(a_second, ga_second, "mid_weight_b", False)
    back12 = micro_sums(back12, plan, [lambda: second.send, third.advance])
    ga_first, g1, back0, gzp = mid_backward(
        1, "entry", gh1, z2, stat1, back12, mid_shards[0], (z0, stat0, zp, statp),
        [((spots, wide), LOW)], "mid_backward_a",
    )
    first_sum = mid_weight(a_first, ga_first, "mid_weight_a", True)
    back0 = micro_sums(back0, plan, [lambda: first_sum.send, second.advance, third.advance])
    (gm,) = call(
        functools.partial(entry_norm_kernel, plan),
        (inv, marks, pars, g1, z0, stat0, back0),
        [SMEM] + [VMEM] * 6,
        [((2, spots + pitch, wide), LOW)],
        [VMEM],
        [padded],
        spots * wide * 20,
        "entry_norm",
    )
    keep, send = call(
        functools.partial(entry_weight_kernel, plan),
        (xm, tied(gm, first_sum.advance()), gzp),
        [VMEM] * 3,
        [((chans // 2, 10 * chans_in, wide), LOW)] * 2,
        [VMEM] * 2,
        [pltpu.VMEM((2, deep, spots), LOW)],
        2 * spots * 7 * deep * wide,
        "entry_weight",
    )
    entry_sum = WeightSum(keep, send, plan, True)
    (gx,) = call(
        functools.partial(entry_backward_kernel, plan),
        (marks, gm, tied(gzp, send, third.advance()), *entry_shards),
        [VMEM] * 3 + [HBM] * chans,
        [((chans, 2, spots, 2 * chans_in), LOW)],
        [VMEM],
        entry_scratch + [pltpu.SemaphoreType.DMA((7 * chans,))],
        2 * spots * 7 * deep * wide,
        "entry_backward",
    )
    gx_parts = swapped(gx, plan)
    gx_parts[1] = tied(
        gx_parts[1], entry_sum.advance(), second.advance(), third.advance(), first_sum.advance()
    )

    def joined(kernel, parts, matrices, shape, axis, extra, dtype, whole, flops, name):
        edge = tuple(extra if i == axis else n for i, n in enumerate(shape))
        main, tail = call(
            functools.partial(kernel, plan),
            (chan_at, *matrices, *parts),
            [SMEM] + [VMEM] * (3 + chans),
            [(shape, dtype), (edge, LOW)],
            [VMEM] * 2,
            [pltpu.VMEM(whole, LOW)],
            flops,
            name,
        )
        first = lax.slice_in_dim(main, 0, extra, axis=axis) + to_next(tail).astype(dtype)
        return lax.dynamic_update_slice(main, first, (0, 0, 0))

    block_out = joined(
        join_rows_kernel, swapped(block, plan), picks_back, out_grad.shape, 1, EXTRA * width, LOW,
        (chans, spots, chans_out), 2 * spots * wide * 800, "join_rows",
    )
    block_out = jnp.swapaxes(block_out, 1, 2)
    feature_grad = joined(
        join_features_kernel, gx_parts, picks, features.shape, 2, EXTRA * 4 * width, FULL,
        (chans, 2, spots, 2 * chans_in), 8 * spots * 640 * chans * chans_in, "join_features",
    )

    last = ((lax.axis_index("space")) % 2).astype(jnp.int32).reshape(1)
    mids = [one.halves()[:2] for one in (first_sum, second, third)]
    (conv_mid_grad,) = call(
        functools.partial(mid_assembly_kernel, 3),
        (last, *[part for pair in mids for part in pair]),
        [SMEM] + [VMEM] * 6,
        [((3, 9 * chans_out, wide), FULL)],
        [HBM],
        [
            pltpu.VMEM((6, 9 * chans_out // 2, wide), FULL),
            pltpu.SemaphoreType.DMA((6,)),
        ],
        0,
        "mid_assembly",
    )
    conv_mid_grad = conv_mid_grad.reshape(3, 3, 3, chans_out, wide)
    conv_in_grad, proj_grad = call(
        entry_assembly_kernel,
        (last, *entry_sum.halves()[:2]),
        [SMEM] + [VMEM] * 2,
        [((9 * chans_in, wide), FULL), ((chans_in, wide), FULL)],
        [HBM] * 2,
        [pltpu.VMEM((10 * chans_in, wide), FULL), pltpu.SemaphoreType.DMA((2,))],
        0,
        "entry_assembly",
    )
    conv_in_grad = conv_in_grad.reshape(3, 3, chans_in, wide)

    sums = jnp.stack(
        [back0[1], back12[1], back12[2], back3[1], back4[1]]
        + [back0[0], back12[0], back12[0], back3[0], back4[0]]
    )
    sums = sums + flipped(sums, "chan", splits)
    sums = lax.dynamic_slice_in_dim(sums, chan * chans_out, chans_out, 1)
    return (
        block_out, feature_grad, conv_in_grad, proj_grad, conv_mid_grad, sums[:5], sums[5:],
    )


def solution(mesh):
    placed = (
        P(None, "chan", "space"),
        P(),
        P(None, None, "chan", None),
        P("chan", None),
        P(None, None, None, "chan", None),
        P(None, "chan"),
        P(None, "chan"),
        P(None, "chan", "space"),
    )
    return jax.shard_map(
        shards,
        mesh=mesh,
        in_specs=placed,
        out_specs=(
            P(None, "chan", "space"),
            P(None, "chan", "space"),
            P(None, None, "chan", None),
            P("chan", None),
            P(None, None, None, "chan", None),
            P(None, "chan"),
            P(None, "chan"),
        ),
        check_vma=False,
    )
```

```python
import collections
import functools

import jax
import jax.numpy as jnp
import numpy as np
from jax import lax
from jax.experimental import pallas as pl
from jax.experimental.pallas import tpu as pltpu
from jax.sharding import PartitionSpec as P

MICRO = 2
WIN = 20
MOST_SIDE = 9
EXTRA = MOST_SIDE - 1
BLOCK = 16
ROW_BLOCK = 64
GAP = 8
EPS = 1e-05
SLACK_BYTES = 6 * 1024 * 1024
LOW = jnp.bfloat16
HIDERS = ("mid_forward_c", "mid_backward_c", "mid_backward_b", "mid_weight_b")
HIDERS += ("mid_backward_a", "mid_weight_a", "entry_backward", "entry_weight")
FULL = jnp.float32

PLAN_FIELDS = ["chans", "spaces", "splits", "rows_dev", "own_rows", "bases", "pitch", "width"]
PLAN_FIELDS += ["spots", "chans_in", "chans_out", "wide"]
Plan = collections.namedtuple("Plan", PLAN_FIELDS)

VMEM = pl.BlockSpec(memory_space=pltpu.VMEM)
SMEM = pl.BlockSpec(memory_space=pltpu.SMEM)
HBM = pl.BlockSpec(memory_space=pltpu.HBM)
ANY = pl.BlockSpec(memory_space=pl.ANY)


def flipped(value, axis, bit):
    count = lax.axis_size(axis)
    return lax.ppermute(value, axis, [(i, i ^ bit) for i in range(count)])


def from_next(value):
    count = lax.axis_size("space")
    return lax.ppermute(value, "space", [(i + 1, i) for i in range(count - 1)])


def to_next(value):
    count = lax.axis_size("space")
    return lax.ppermute(value, "space", [(i, i + 1) for i in range(count - 1)])


def exchanged(value, chan_bits, space_bits, plan):
    count = plan.chans * plan.spaces
    flip = chan_bits * plan.spaces + space_bits
    return lax.ppermute(value, ("chan", "space"), [(i, i ^ flip) for i in range(count)])


def tied(value, *others):
    return lax.optimization_barrier((value, others))[0]


def gathered(own, plan, then=()):
    parts = {0: own}
    for rel in range(1, plan.chans):
        bit = rel & -rel
        source = parts[rel ^ bit]
        if rel != bit and then:
            source = tied(source, *then)
        parts[rel] = flipped(source, "chan", bit)
    return [parts[rel] for rel in range(plan.chans)]


def swapped(parts, plan):
    return [parts[0]] + [flipped(parts[rel], "chan", rel) for rel in range(1, plan.chans)]


def micro_sums(value, plan, early=(), late=()):
    bits = []
    bit = 1
    while bit < plan.splits:
        bits.append((bit, 0))
        bit *= 2
    bit = 1
    while bit < plan.spaces:
        bits.append((0, bit))
        bit *= 2
    for i in range(0, len(bits), 2):
        pair = bits[i : i + 2]
        start = value
        one = exchanged(value, *pair[0], plan)
        if len(pair) == 2:
            two = exchanged(value, *pair[1], plan)
            both = exchanged(value, pair[0][0] ^ pair[1][0], pair[0][1] ^ pair[1][1], plan)
        done = []
        if i == 0:
            done = [job(one) for job in early]
        elif i == 2:
            done = [job(start) for job in late]
        done = [token for token in jax.tree.leaves(done) if token is not None]
        if done:
            one = tied(one, *done)
        value = value + one
        if len(pair) == 2:
            value = value + (two + both)
    return value


class WeightSum:
    def __init__(self, keep, send, plan, order):
        self.send, self.plan = send, plan
        self.kept = keep
        self.received = [] if send is None else [flipped(send, "chan", 1)]
        self.steps = []
        named = [bit for step in order if step != "c" for bit in step]
        rest = [k for k in range(plan.spaces.bit_length() - 1) if k not in named]
        for step in list(order) + [(k,) for k in rest]:
            if step == "c":
                self.steps += [("chan", (1 << k,)) for k in range(1, plan.chans.bit_length() - 1)]
            else:
                self.steps.append(("space", tuple(1 << k for k in step)))
        self.steps[-1] = ("swap", self.steps[-1][1])
        self.gathers = [bits for axis, bits in self.steps if axis == "space"][::-1]
        self.last = self.gathers[-1]
        self.gathering = False

    def mine(self, bit):
        return (lax.axis_index("space") // bit) % 2

    def added(self, pick):
        total = pick(self.kept).astype(FULL)
        for part in self.received:
            total = total + pick(part).astype(FULL)
        return total.astype(LOW)

    def flips(self, bits):
        ways = []
        for number in range(1, 1 << len(bits)):
            held = [(number >> i) & 1 for i in range(len(bits))]
            ways.append((sum(bit for bit, on in zip(bits, held) if on), held))
        return ways

    def take(self, *after):
        if after and self.received:
            self.received[0] = tied(self.received[0], *after)
        elif after:
            self.kept = tied(self.kept, *after)

    def advance(self, *after):
        self.take(*after)
        if self.steps:
            axis, bits = self.steps.pop(0)
            if axis == "swap":
                kept = self.added(lambda part: part)
                sent = [(bits[0], kept)]
                axis = "space"
            elif axis == "chan":
                kept = self.added(lambda part: part[0::2])
                sent = [(bits[0], self.added(lambda part: part[1::2]))]
            else:
                size = self.kept.shape[1] >> len(bits)

                def piece(held):
                    at = 0
                    for bit, on in zip(bits[::-1], held[::-1]):
                        at = 2 * at + (self.mine(bit) if not on else 1 - self.mine(bit))
                    return self.added(lambda part: lax.dynamic_slice_in_dim(part, at * size, size, 1))

                kept = piece([0] * len(bits))
                sent = [(flip, piece(held)) for flip, held in self.flips(bits)]
            self.kept = kept
            self.received = [flipped(part, axis, flip) for flip, part in sent]
            return sent[0][1]
        bits = self.gathers.pop(0)
        whole = self.ordered() if self.gathering else self.added(lambda part: part)
        self.gathering = bits
        self.kept = whole
        self.received = [flipped(whole, "space", flip) for flip, _ in self.flips(bits)]
        return whole

    def ordered(self):
        parts = [self.kept] + self.received
        for bit in self.gathering:
            turned = self.mine(bit) == 0
            joined = []
            for i in range(0, len(parts), 2):
                low = jnp.concatenate(parts[i : i + 2], axis=1)
                high = jnp.concatenate(parts[i : i + 2][::-1], axis=1)
                joined.append(jnp.where(turned, low, high))
            parts = joined
        return parts[0]

    def halves(self, *after):
        while self.steps or self.gathers:
            self.advance(*after)
        self.take(*after)
        return self.kept[0], self.received[0][0]


def tiles(count, size):
    return [slice(i, i + size) for i in range(0, count, size)]


def logistic(u):
    return 1.0 / (1.0 + jnp.exp(-u))


def slope(u):
    g = logistic(u)
    return g * (1.0 + u * (1.0 - g))


def moments(stat, inv_count):
    mean = stat[0:1, :] * inv_count
    inverse = lax.rsqrt(stat[1:2, :] * inv_count - mean * mean + EPS)
    return mean, inverse


def dot(a, b):
    return lax.dot_general(a, b, (((1,), (0,)), ((), ())), preferred_element_type=FULL)


def dot_t(a, b):
    return lax.dot_general(a, b, (((1,), (1,)), ((), ())), preferred_element_type=FULL)


def unit(count):
    rows = lax.broadcasted_iota(jnp.int32, (count, count), 0)
    columns = lax.broadcasted_iota(jnp.int32, (count, count), 1)
    return jnp.where(rows == columns, 1.0, 0.0).astype(LOW)


def clear_gaps(ref, spots):
    zero = jnp.zeros((GAP, ref.shape[-1]), ref.dtype)
    ref[pl.ds(0, GAP), :] = zero
    ref[pl.ds(GAP + spots, GAP), :] = zero


def column_sum(x):
    return jnp.sum(x, axis=0, keepdims=True)


def start_shards(chan, shard_refs, w_ref, sems):
    size = shard_refs[0].shape[2]
    copies = []
    for rel, ref in enumerate(shard_refs):
        place = pl.ds(pl.multiple_of((chan ^ rel) * size, size), size)
        copy = pltpu.make_async_copy(ref, w_ref.at[:, :, place, :], sems.at[rel])
        copy.start()
        copies.append(copy)
    return copies


def matmul_tile(plan):
    for size in (288, 192, 144, 96, 64):
        if plan.spots % size == 0:
            return size
    return plan.spots


def vector_tile(plan):
    return 2 * plan.pitch // 4 if plan.pitch % 32 == 0 else plan.pitch


def feature_pick(plan, side, first, count):
    shape = (2 * MOST_SIDE * BLOCK, count)
    place = lax.broadcasted_iota(jnp.int32, shape, 0)
    cell = lax.broadcasted_iota(jnp.int32, shape, 1) + first
    row, column = place & (BLOCK - 1), place >> (BLOCK.bit_length() - 1)
    phase = jnp.where(column >= MOST_SIDE, 1, 0)
    column = column - MOST_SIDE * phase
    source = (2 * row + phase) * (2 * plan.width) + 2 * column + side
    return jnp.where(source == cell, 1.0, 0.0).astype(LOW)


def row_pick(plan, first, count, turned=False):
    spots = MOST_SIDE * ROW_BLOCK
    shape = (count, spots) if turned else (spots, count)
    place = lax.broadcasted_iota(jnp.int32, shape, 1 if turned else 0)
    cell = lax.broadcasted_iota(jnp.int32, shape, 0 if turned else 1) + first
    row, column = place & (ROW_BLOCK - 1), place >> (ROW_BLOCK.bit_length() - 1)
    return jnp.where(row * plan.width + column == cell, 1.0, 0.0).astype(LOW)


def spread_features_kernel(plan, chan_ref, x_ref, halo_ref, out_ref):
    chan = chan_ref[0]
    size, lanes = plan.chans_in, BLOCK * 4 * plan.width
    columns = MOST_SIDE

    def stacked(part):
        blank = jnp.zeros_like(part[0])
        even, odd = [], []
        for m in range(MICRO):
            even += [part[m], blank]
            odd += [blank, part[m]]
        return jnp.concatenate(even, 0), jnp.concatenate(odd, 0)

    have = x_ref.shape[2]
    own, extra = have % lanes, halo_ref.shape[2]
    picks = [feature_pick(plan, side, 0, lanes) for side in range(2)]
    left = [feature_pick(plan, side, 0, own) for side in range(2)]
    right = [feature_pick(plan, side, own, extra) for side in range(2)]
    for j in range(-(-(plan.rows_dev + EXTRA) // BLOCK)):
        start = j * lanes
        if start + lanes <= have:
            even, odd = stacked([x_ref[m, :, start : start + lanes] for m in range(MICRO)])
            result = dot_t(picks[0], even) + dot_t(picks[1], odd)
        else:
            even, odd = stacked([x_ref[m, :, start:have] for m in range(MICRO)])
            result = dot_t(left[0], even) + dot_t(left[1], odd)
            even, odd = stacked([halo_ref[m] for m in range(MICRO)])
            result += dot_t(right[0], even) + dot_t(right[1], odd)
        result = result.astype(LOW)
        for split, base in enumerate(plan.bases):
            row = j * BLOCK - base
            if row < 0 or row >= plan.pitch:
                continue
            for m in range(MICRO):
                to = chan ^ (m * plan.splits + split)
                for phase in range(2):
                    for c in range(columns):
                        at = (phase * columns + c) * BLOCK
                        part = result[at : at + BLOCK, m * 2 * size : (m + 1) * 2 * size]
                        spot = c * plan.pitch + row
                        out_ref[to, phase, spot : spot + BLOCK] = part


def spread_rows_kernel(plan, chan_ref, x_ref, halo_ref, out_ref):
    chan = chan_ref[0]
    size, spots = plan.chans_out, ROW_BLOCK * plan.width
    have = x_ref.shape[1]
    own, extra = have % spots, halo_ref.shape[1]
    pick, left = row_pick(plan, 0, spots), row_pick(plan, 0, own)
    right = row_pick(plan, own, extra)
    for j in range(-(-(plan.rows_dev + EXTRA) // ROW_BLOCK)):
        start = j * spots
        for m in range(MICRO):
            if start + spots <= have:
                result = dot(pick, x_ref[m, start : start + spots])
            else:
                result = dot(left, x_ref[m, start:have]) + dot(right, halo_ref[m])
            result = result.astype(LOW)
            for split, base in enumerate(plan.bases):
                low, high = max(j * ROW_BLOCK, base), min((j + 1) * ROW_BLOCK, base + plan.pitch)
                if low >= high:
                    continue
                to = chan ^ (m * plan.splits + split)
                for c in range(MOST_SIDE):
                    at = c * ROW_BLOCK + low - j * ROW_BLOCK
                    spot = c * plan.pitch + low - base
                    out_ref[to, spot : spot + high - low] = result[at : at + high - low]


def laid_rows(plan, whole_ref, m, c, low, high, phase=None):
    pieces = []
    for row in range(low, high, BLOCK):
        total = None
        for split, base in enumerate(plan.bases):
            if not base <= row < base + plan.pitch:
                continue
            spots = pl.ds(c * plan.pitch + row - base, BLOCK)
            at = m * plan.splits + split
            part = whole_ref[at, spots] if phase is None else whole_ref[at, phase, spots]
            total = part if total is None else total + part
        pieces.append(total)
    return pieces


def join_rows_kernel(plan, chan_ref, *refs):
    parts = refs[: plan.chans]
    out_ref, tail_ref, whole_ref = refs[plan.chans :]
    chan = chan_ref[0]
    for rel in range(plan.chans):
        whole_ref[chan ^ rel] = parts[rel][...]
    spots = ROW_BLOCK * plan.width
    have = out_ref.shape[1]
    own, extra = have % spots, tail_ref.shape[1]
    pick, left = row_pick(plan, 0, spots, True), row_pick(plan, 0, own, True)
    right = row_pick(plan, own, extra, True)
    limit = plan.rows_dev + EXTRA
    for j in range(-(-limit // ROW_BLOCK)):
        start = j * spots
        low, high = j * ROW_BLOCK, min((j + 1) * ROW_BLOCK, limit)
        for m in range(MICRO):
            pieces = []
            for c in range(MOST_SIDE):
                pieces += laid_rows(plan, whole_ref, m, c, low, high)
                if high - low < ROW_BLOCK:
                    blank = (ROW_BLOCK - high + low, plan.chans_out)
                    pieces.append(jnp.zeros(blank, LOW))
            rows = jnp.concatenate(pieces, 0)
            if start + spots <= have:
                out_ref[m, start : start + spots] = dot(pick, rows).astype(LOW)
            else:
                out_ref[m, start:have] = dot(left, rows).astype(LOW)
                tail_ref[m] = dot(right, rows).astype(LOW)


def join_features_kernel(plan, chan_ref, *refs):
    parts = refs[: plan.chans]
    out_ref, tail_ref, whole_ref = refs[plan.chans :]
    chan = chan_ref[0]
    for rel in range(plan.chans):
        whole_ref[chan ^ rel] = parts[rel][...]
    size = plan.chans_in
    one = unit(2 * size)
    lanes = BLOCK * 4 * plan.width
    have = out_ref.shape[2]
    own, extra = have % lanes, tail_ref.shape[2]
    picks = [feature_pick(plan, side, 0, lanes) for side in range(2)]
    left = [feature_pick(plan, side, 0, own) for side in range(2)]
    right = [feature_pick(plan, side, own, extra) for side in range(2)]
    for j in range(-(-(plan.rows_dev + EXTRA) // BLOCK)):
        start = j * lanes
        first, second = [], []
        for m in range(MICRO):
            pieces = []
            for phase in range(2):
                for c in range(MOST_SIDE):
                    row = j * BLOCK
                    pieces += laid_rows(plan, whole_ref, m, c, row, row + BLOCK, phase)
            turned = dot_t(one, jnp.concatenate(pieces, 0)).astype(LOW)
            first.append(turned[:size])
            second.append(turned[size:])
        first, second = jnp.concatenate(first, 0), jnp.concatenate(second, 0)
        if start + lanes <= have:
            result = dot(first, picks[0]) + dot(second, picks[1])
            for m in range(MICRO):
                out_ref[m, :, start : start + lanes] = result[m * size : (m + 1) * size]
        else:
            result = dot(first, left[0]) + dot(second, left[1])
            tail = dot(first, right[0]) + dot(second, right[1])
            for m in range(MICRO):
                out_ref[m, :, start:have] = result[m * size : (m + 1) * size]
                tail_ref[m] = tail[m * size : (m + 1) * size].astype(LOW)


def entry_copies(plan, shard_refs, w_ref, wp_ref, sems):
    copies = []
    for rel in range(plan.chans):
        for a in range(3):
            sem = sems.at[7 * rel + 2 * a]
            source = shard_refs[rel].at[pl.ds(3 * a + 1, 2)]
            copies.append(pltpu.make_async_copy(source, w_ref.at[a, 0, rel], sem))
            sem = sems.at[7 * rel + 2 * a + 1]
            source = shard_refs[rel].at[3 * a]
            copies.append(pltpu.make_async_copy(source, w_ref.at[a, 1, rel, 1], sem))
        source = shard_refs[rel].at[9]
        copies.append(pltpu.make_async_copy(source, wp_ref.at[rel, 0], sems.at[7 * rel + 6]))
    for copy in copies:
        copy.start()
    for rel in range(plan.chans):
        blank = jnp.zeros(wp_ref.shape[2:], LOW)
        wp_ref[rel, 1] = blank
        for a in range(3):
            w_ref[a, 1, rel, 0] = blank
    return copies


def entry_forward_kernel(plan, marks_ref, *refs):
    n = plan.chans
    x_refs, shard_refs = refs[:n], refs[n : 2 * n]
    e_ref, p_ref, stat_ref, xm_ref = refs[2 * n : 2 * n + 4]
    x_ref, w_ref, wp_ref, xs_ref, am_ref, sems, x_sems = refs[2 * n + 4 :]
    x_copies = []
    for rel in range(n):
        x_copies.append(pltpu.make_async_copy(x_refs[rel], x_ref.at[rel], x_sems.at[rel]))
        x_copies[-1].start()
    copies = entry_copies(plan, shard_refs, w_ref, wp_ref, sems)
    size = 2 * plan.chans_in
    deep = n * size
    pitch = plan.pitch
    for k in range(3):
        am_ref[k, 0:pitch] = jnp.zeros((pitch, deep), LOW)
    clear_gaps(xs_ref, plan.spots)
    for rel in range(n):
        x_copies[rel].wait()
        lanes = slice(rel * size, (rel + 1) * size)
        for t in tiles(plan.spots, vector_tile(plan)):
            own = marks_ref[t, 0:1]
            for row in range(2):
                value = x_ref[rel, row, t].astype(FULL) * own
                low = value.astype(LOW)
                xm_ref[row, t, lanes] = low
                am_ref[row, pitch + t.start : pitch + t.stop, lanes] = low
                if row == 1:
                    xs_ref[GAP + t.start : GAP + t.stop, lanes] = value
    for t in tiles(plan.spots, vector_tile(plan)):
        above = xs_ref[GAP + t.start - 1 : GAP + t.stop - 1] * marks_ref[t, 1:2]
        am_ref[2, pitch + t.start : pitch + t.stop] = above.astype(LOW)
    for copy in copies:
        copy.wait()
    weights = w_ref[...].reshape(6 * deep, plan.wide)
    proj = wp_ref[...].reshape(deep, plan.wide)
    sums = [0.0] * 4
    for t in tiles(plan.spots, matmul_tile(plan)):
        own = marks_ref[t, 0:1]
        pieces = []
        for k in (2, 0, 1):
            pieces.append(am_ref[k, pitch + t.start : pitch + t.stop])
            pieces.append(am_ref[k, t])
        z = dot(jnp.concatenate(pieces, 1), weights)
        e_ref[t] = z.astype(LOW)
        p = dot(pieces[2], proj)
        p_ref[t] = p.astype(LOW)
        zm, pm = z * own, p * own
        for i, term in enumerate((zm, zm * z, pm, pm * p)):
            sums[i] = sums[i] + column_sum(term)
    stat_ref[...] = jnp.concatenate(sums, 0)


def mid_forward_kernel(plan, layers, chan_ref, inv_ref, marks_ref, par_ref, *refs):
    k = len(layers)
    n = plan.chans
    z_refs, stat_refs, shard_refs = refs[:k], refs[k : 2 * k], refs[2 * k : 2 * k + n]
    outs = refs[2 * k + n :]
    if k == 2:
        z_ref, out_stat_ref, a_ref, h_ref, w_ref, xs_ref, xa_ref, sems = outs
    else:
        z_ref, out_stat_ref, a_ref, w_ref, xs_ref, xa_ref, sems = outs
        h_ref = None
    copies = start_shards(chan_ref[0], shard_refs, w_ref, sems)
    inv = inv_ref[0]
    norms = [moments(stat[...], inv) for stat in stat_refs]
    wide, pitch = plan.wide, plan.pitch
    clear_gaps(xs_ref, plan.spots)
    for i in range(3):
        blank = jnp.zeros((pitch, wide), LOW)
        xa_ref[i, 0:pitch] = blank
        xa_ref[i, pitch + plan.spots : 2 * pitch + plan.spots] = blank
    for t in tiles(plan.spots, vector_tile(plan)):
        own = marks_ref[t, 0:1]
        u = 0.0
        for (mean, inverse), src, j in zip(norms, z_refs, layers):
            u = u + (par_ref[j : j + 1] * ((src[t].astype(FULL) - mean) * inverse) + par_ref[5 + j : 6 + j])
        u = u * own
        a = u * logistic(u)
        if h_ref is not None:
            h_ref[t] = a.astype(LOW)
        xs_ref[GAP + t.start : GAP + t.stop] = a
        low = a.astype(LOW)
        a_ref[t] = low
        xa_ref[1, pitch + t.start : pitch + t.stop] = low
    for t in tiles(plan.spots, vector_tile(plan)):
        for i, step in ((0, -1), (2, 1)):
            part = xs_ref[GAP + t.start + step : GAP + t.stop + step]
            part = part * marks_ref[t, 1 + i // 2 : 2 + i // 2]
            xa_ref[i, pitch + t.start : pitch + t.stop] = part.astype(LOW)
    for copy in copies:
        copy.wait()
    weights = w_ref[...].reshape(9 * wide, wide)
    total, square = 0.0, 0.0
    for t in tiles(plan.spots, matmul_tile(plan)):
        own = marks_ref[t, 0:1]
        pieces = []
        for a in range(3):
            for b in range(3):
                pieces.append(xa_ref[a, t.start + b * pitch : t.stop + b * pitch])
        z = dot(jnp.concatenate(pieces, 1), weights)
        z_ref[t] = z.astype(LOW)
        zm = z * own
        total = total + column_sum(zm)
        square = square + column_sum(zm * z)
    out_stat_ref[...] = jnp.concatenate([total, square], 0)


def head_kernel(plan, chan_ref, inv_ref, marks_ref, par_ref, z_ref, stat_ref, h_ref, *refs):
    n = plan.chans
    og_refs = refs[:n]
    out_ref, g_ref, out_stat_ref, og_ref = refs[n:]
    chan = chan_ref[0]
    for rel in range(n):
        og_ref[chan ^ rel] = og_refs[rel][...]
    mean, inverse = moments(stat_ref[...], inv_ref[0])
    size = plan.chans_out
    for j in range(n):
        lanes = slice(j * size, (j + 1) * size)
        total, dotted = 0.0, 0.0
        for t in tiles(plan.spots, plan.pitch):
            own = marks_ref[t, 0:1]
            hat = (z_ref[t, lanes].astype(FULL) - mean[:, lanes]) * inverse[:, lanes]
            u = own * (par_ref[4:5, lanes] * hat + par_ref[9:10, lanes]) + h_ref[t, lanes].astype(FULL)
            s = logistic(u)
            out_ref[chan ^ j, t] = (u * s).astype(LOW)
            q = og_ref[j, t].astype(FULL) * (s * (1.0 + u * (1.0 - s))) * own
            g_ref[t, lanes] = q.astype(LOW)
            total = total + column_sum(q)
            dotted = dotted + column_sum(q * hat)
        out_stat_ref[0:1, lanes] = total
        out_stat_ref[1:2, lanes] = dotted


def norm_back(own, q, z, norm, gain, total, dotted, inv):
    mean, inverse = norm
    hat = (z - mean) * inverse
    return own * (gain * inverse) * (q - total * inv - hat * (dotted * inv))


def mid_backward_kernel(plan, j, kind, chan_ref, inv_ref, marks_ref, par_ref, *refs):
    n = plan.chans
    g_ref, z_ref, stat_ref, back_ref = refs[:4]
    shard_refs = refs[4 : 4 + n]
    refs = refs[4 + n :]
    add_ref = short_z_ref = None
    if kind == "join":
        src_refs, src_stats, add_ref = refs[:2], refs[2:4], refs[4]
        refs = refs[5:]
        layers = (1, 2)
    elif kind == "entry":
        src_refs, src_stats, short_z_ref, short_stat_ref = refs[:1], refs[1:2], refs[2], refs[3]
        refs = refs[4:]
        layers = (0,)
    else:
        src_refs, src_stats = refs[:1], refs[1:2]
        refs = refs[2:]
        layers = (3,)
    ga_ref, next_ref, out_stat_ref = refs[:3]
    refs = refs[3:]
    if kind == "entry":
        short_ref, refs = refs[0], refs[1:]
    w_ref, s0_ref, s2_ref, sems = refs
    copies = start_shards(chan_ref[0], shard_refs, w_ref, sems)
    inv = inv_ref[0]
    wide, pitch = plan.wide, plan.pitch
    norm = moments(stat_ref[...], inv)
    total, dotted = back_ref[0:1], back_ref[1:2]
    for ref in (s0_ref, s2_ref):
        clear_gaps(ref, plan.spots)
    for i in range(3):
        blank = jnp.zeros((pitch, wide), LOW)
        ga_ref[i, 0:pitch] = blank
        ga_ref[i, pitch + plan.spots : 2 * pitch + plan.spots] = blank
    if kind == "entry":
        short_norm = moments(short_stat_ref[...], inv)
    for t in tiles(plan.spots, vector_tile(plan)):
        own, upper, lower = (marks_ref[t, i : i + 1] for i in range(3))
        g = g_ref[t].astype(FULL)
        z = z_ref[t].astype(FULL)
        gz = norm_back(own, g, z, norm, par_ref[j : j + 1], total, dotted, inv)
        low = gz.astype(LOW)
        gz = low.astype(FULL)
        ga_ref[1, pitch + t.start : pitch + t.stop] = low
        s0_ref[GAP + t.start : GAP + t.stop] = gz * upper
        s2_ref[GAP + t.start : GAP + t.stop] = gz * lower
        if kind == "entry":
            back = norm_back(
                own, g, short_z_ref[t].astype(FULL), short_norm, par_ref[2:3], total,
                back_ref[2:3], inv,
            )
            short_ref[t] = back.astype(LOW)
    for t in tiles(plan.spots, vector_tile(plan)):
        first, last = GAP + t.start, GAP + t.stop
        to = slice(pitch + t.start, pitch + t.stop)
        ga_ref[0, to] = s0_ref[first + 1 : last + 1].astype(LOW)
        ga_ref[2, to] = s2_ref[first - 1 : last - 1].astype(LOW)
    for copy in copies:
        copy.wait()
    norms = [moments(stat[...], inv) for stat in src_stats]
    sums = [0.0] * (1 + len(layers))
    weights = jnp.concatenate([w_ref[a, b] for a in range(3) for b in range(3)], 1)
    for t in tiles(plan.spots, matmul_tile(plan)):
        own = marks_ref[t, 0:1]
        pieces = []
        for a in range(3):
            for b in range(3):
                back = (2 - b) * pitch
                pieces.append(ga_ref[a, t.start + back : t.stop + back])
        gx = dot_t(jnp.concatenate(pieces, 1), weights)
        u = 0.0
        hats = []
        for (mean, inverse), src, i in zip(norms, src_refs, layers):
            hat = (src[t].astype(FULL) - mean) * inverse
            hats.append(hat)
            u = u + (par_ref[i : i + 1] * hat + par_ref[5 + i : 6 + i])
        u = u * own
        if add_ref is not None:
            gx = gx + add_ref[t].astype(FULL)
        q = gx * slope(u) * own
        next_ref[t] = q.astype(LOW)
        sums[0] = sums[0] + column_sum(q)
        for i, hat in enumerate(hats):
            sums[1 + i] = sums[1 + i] + column_sum(q * hat)
    out_stat_ref[...] = jnp.concatenate(sums, 0)


def entry_norm_kernel(plan, inv_ref, marks_ref, par_ref, g_ref, e_ref, stat_ref, back_ref, gm_ref, s_ref):
    inv = inv_ref[0]
    norm = moments(stat_ref[...], inv)
    clear_gaps(s_ref, plan.spots)
    for k in range(2):
        gm_ref[k, plan.spots : plan.spots + plan.pitch] = jnp.zeros((plan.pitch, plan.wide), LOW)
    for t in tiles(plan.spots, vector_tile(plan)):
        own, upper = marks_ref[t, 0:1], marks_ref[t, 1:2]
        gz = norm_back(
            own, g_ref[t].astype(FULL), e_ref[t].astype(FULL), norm, par_ref[0:1], back_ref[0:1],
            back_ref[1:2], inv,
        )
        low = gz.astype(LOW)
        gm_ref[0, t] = low
        s_ref[GAP + t.start : GAP + t.stop] = low.astype(FULL) * upper
    for t in tiles(plan.spots, vector_tile(plan)):
        gm_ref[1, t] = s_ref[GAP + t.start + 1 : GAP + t.stop + 1].astype(LOW)


def entry_backward_kernel(plan, marks_ref, gm_ref, short_ref, *refs):
    n = plan.chans
    shard_refs = refs[:n]
    gx_ref, w_ref, wp_ref, sems = refs[n:]
    for copy in entry_copies(plan, shard_refs, w_ref, wp_ref, sems):
        copy.wait()
    size = 2 * plan.chans_in
    deep = n * size
    pitch, wide = plan.pitch, plan.wide

    def part(a, side):
        return w_ref[a, side].reshape(deep, wide)

    top_weights = [part(1, 0), part(1, 1), wp_ref[...].reshape(deep, wide)]
    top_weights = jnp.concatenate(top_weights, 1)
    low_weights = jnp.concatenate([part(2, 0), part(2, 1), part(0, 0), part(0, 1)], 1)
    for t in tiles(plan.spots, matmul_tile(plan)):
        own = marks_ref[t, 0:1]
        right = slice(t.start + pitch, t.stop + pitch)
        here = [gm_ref[0, t], gm_ref[0, right]]
        top = dot_t(jnp.concatenate(here + [short_ref[t]], 1), top_weights)
        here += [gm_ref[1, t], gm_ref[1, right]]
        low = dot_t(jnp.concatenate(here, 1), low_weights)
        for row, value in enumerate((top, low)):
            value = (value * own).astype(LOW)
            for rel in range(n):
                gx_ref[rel, row, t] = value[:, rel * size : (rel + 1) * size]


def mid_weight_kernel(plan, chan_ref, a_ref, ga_ref, keep_ref, send_ref, turned_ref, at_ref):
    wide, pitch = plan.wide, plan.pitch
    turned_ref[...] = dot_t(unit(wide), a_ref[...]).astype(LOW)
    chan = chan_ref[0]
    size = plan.chans_out
    for rel in range(plan.chans):
        place = pl.ds(pl.multiple_of((chan ^ rel) * size, size), size)
        at_ref[rel * size : (rel + 1) * size] = turned_ref[place]
    for a in range(3):
        for b in range(3):
            back = (2 - b) * pitch
            rows = slice((3 * a + b) * size, (3 * a + b + 1) * size)
            part = dot(at_ref[...], ga_ref[a, back : back + plan.spots]).astype(LOW)
            for rel in range(plan.chans):
                target = send_ref if rel & 1 else keep_ref
                target[rel // 2, rows] = part[rel * size : (rel + 1) * size]


def entry_weight_kernel(plan, xm_ref, gm_ref, short_ref, keep_ref, send_ref, xt_ref):
    n, size, wide, pitch = plan.chans, plan.chans_in, plan.wide, plan.pitch
    whole = unit(n * 2 * size)
    for row in range(2):
        xt_ref[row] = dot_t(whole, xm_ref[row]).astype(LOW)

    def put(tap, rel, value):
        target = send_ref if rel & 1 else keep_ref
        target[rel // 2, tap * size : (tap + 1) * size] = value

    def product(row, right):
        return dot(xt_ref[row], right).astype(LOW)

    for row, grad, a in ((0, 0, 1), (1, 0, 2), (1, 1, 0)):
        big = product(row, gm_ref[grad, 0 : plan.spots])
        side = product(row, gm_ref[grad, pitch : pitch + plan.spots])
        for rel in range(n):
            at = 2 * rel * size
            put(3 * a + 1, rel, big[at : at + size])
            put(3 * a + 2, rel, big[at + size : at + 2 * size])
            put(3 * a, rel, side[at + size : at + 2 * size])
    proj = product(0, short_ref[...])
    for rel in range(n):
        put(9, rel, proj[2 * rel * size : (2 * rel + 1) * size])


def mid_assembly_kernel(mine_ref, *refs):
    out_ref, hold_ref, sems = refs[6:]
    half = refs[0].shape[0]
    copies = []
    for layer in range(3):
        mine = mine_ref[layer]
        for i, part in enumerate(refs[2 * layer : 2 * layer + 2]):
            at = mine if i == 0 else 1 - mine
            rows = pl.ds(pl.multiple_of(at * half, 8), half)
            hold_ref[layer, rows] = part[...].astype(FULL)
        copies.append(pltpu.make_async_copy(hold_ref.at[layer], out_ref.at[layer], sems.at[layer]))
        copies[-1].start()
    for copy in copies:
        copy.wait()


def entry_assembly_kernel(mine_ref, own_ref, other_ref, conv_ref, proj_ref, hold_ref, sems):
    half = own_ref.shape[0]
    for i, part in enumerate((own_ref, other_ref)):
        at = mine_ref[3] if i == 0 else 1 - mine_ref[3]
        hold_ref[pl.ds(pl.multiple_of(at * half, 8), half)] = part[...].astype(FULL)
    cut = conv_ref.shape[0]
    copies = [
        pltpu.make_async_copy(hold_ref.at[pl.ds(0, cut)], conv_ref, sems.at[0]),
        pltpu.make_async_copy(hold_ref.at[pl.ds(cut, proj_ref.shape[0])], proj_ref, sems.at[1]),
    ]
    for copy in copies:
        copy.start()
    for copy in copies:
        copy.wait()


def call(kernel, operands, specs, outs, out_specs, scratch, name, flops=0):
    bytes_moved = sum(int(np.prod(o.shape)) * o.dtype.itemsize for o in operands)
    bytes_moved += sum(int(np.prod(s)) * jnp.dtype(d).itemsize for s, d in outs)
    bytes_moved = 1 if name in HIDERS else bytes_moved
    shapes = [jax.ShapeDtypeStruct(s, d) for s, d in outs]
    held = SLACK_BYTES
    for one in scratch:
        if one.memory_space == pltpu.VMEM:
            held += int(np.prod(one.shape)) * jnp.dtype(one.dtype).itemsize
    return pl.pallas_call(
        kernel,
        out_shape=shapes,
        in_specs=specs,
        out_specs=out_specs,
        scratch_shapes=scratch,
        compiler_params=pltpu.CompilerParams(vmem_limit_bytes=held),
        cost_estimate=pl.CostEstimate(
            flops=int(flops), bytes_accessed=int(bytes_moved), transcendentals=0
        ),
        name=name,
    )(*operands)


def marks_of(plan, sizes, top, first):
    sides = sizes // 2
    starts = jnp.cumsum(sides) - sides
    here = top + jnp.arange(plan.pitch, dtype=jnp.int32)
    inside = (
        (here[:, None] >= starts[None, :]) & (here[:, None] < (starts + sides)[None, :])
    ).astype(jnp.int32)
    begins = jnp.sum(inside * starts[None, :], axis=1)
    widths = jnp.sum(inside * sides[None, :], axis=1)
    local = here - begins
    owned = (widths > 0) & (begins >= first) & (begins < first + plan.own_rows)
    columns = jnp.arange(MOST_SIDE, dtype=jnp.int32)
    own = owned[None, :] & (columns[:, None] < widths[None, :])
    upper = jnp.broadcast_to((owned & (local > 0))[None, :], own.shape)
    lower = jnp.broadcast_to((owned & (local < widths - 1))[None, :], own.shape)
    marks = jnp.stack([own, upper, lower] + [jnp.zeros_like(own)] * 5, axis=-1)
    total = jnp.sum((sides * sides).astype(FULL))
    return marks.astype(FULL).reshape(plan.spots, 8), (1.0 / total).reshape(1)


def shards(features, image_sizes, conv_in_w, proj_w, conv_mid_w, norm_gain, norm_bias, out_grad):
    chans, spaces = lax.axis_size("chan"), lax.axis_size("space")
    splits = chans // MICRO
    width = WIN // 2
    rows_dev = features.shape[2] // (4 * width)
    own_rows = rows_dev // splits
    bases = tuple(split * own_rows // BLOCK * BLOCK for split in range(splits))
    need = max(split * own_rows - bases[split] for split in range(splits)) + own_rows + EXTRA
    pitch = -(-need // BLOCK) * BLOCK
    reach = -(-(rows_dev + EXTRA) // BLOCK) * BLOCK
    assert max(bases) + pitch <= reach and rows_dev + EXTRA == reach
    chans_in, chans_out = features.shape[1], norm_gain.shape[1]
    spots = MOST_SIDE * pitch
    plan = Plan(
        chans, spaces, splits, rows_dev, own_rows, bases, pitch, width, spots,
        chans_in, chans_out, chans * chans_out,
    )
    wide = plan.wide
    chan = lax.axis_index("chan")
    micro, split = chan // splits, chan % splits
    here = lax.axis_index("space") * rows_dev
    first = here + split * own_rows
    chan_at = chan.astype(jnp.int32).reshape(1)

    edge = features[:, :, : EXTRA * 4 * width]
    halo = from_next(edge)
    out_grad = jnp.swapaxes(out_grad, 1, 2)
    out_halo = from_next(out_grad[:, : EXTRA * width])
    (spread,) = call(
        functools.partial(spread_features_kernel, plan),
        (chan_at, features, tied(halo, out_halo)),
        [SMEM] + [VMEM] * 2,
        [((chans, 2, spots, 2 * chans_in), LOW)],
        [VMEM],
        [],
        "spread_features",
    )
    x_parts = swapped(spread, plan)
    slots = jnp.concatenate([norm_gain, norm_bias], axis=0)
    slots = lax.dynamic_update_slice(
        jnp.zeros((10, wide), FULL), slots, (jnp.int32(0), chan * chans_out)
    )
    bit = 1
    while bit < chans:
        slots = slots + flipped(slots, "chan", bit)
        bit *= 2
    pars = slots
    sizes = lax.dynamic_index_in_dim(image_sizes, micro, 0, keepdims=False)
    bases_at = jnp.asarray(bases, jnp.int32)[split]
    marks, inv = marks_of(plan, sizes, here + bases_at, first)

    (grad_spread,) = call(
        functools.partial(spread_rows_kernel, plan),
        (chan_at, out_grad, tied(out_halo, x_parts[1])),
        [SMEM] + [VMEM] * 2,
        [((chans, spots, chans_out), LOW)],
        [VMEM],
        [],
        "spread_rows",
    )

    entry_own = jnp.concatenate([conv_in_w.reshape(9, chans_in, wide), proj_w[None]], axis=0)
    entry_own = tied(entry_own, edge)
    entry_shards = gathered(entry_own, plan, (*x_parts[chans // 2 :], pars, grad_spread))
    mid_first = tied(conv_mid_w[0], *x_parts[chans // 2 :])

    conv_flops = 2 * spots * 9 * wide * wide
    field = ((spots, wide), LOW)
    deep = chans * 2 * chans_in
    entry_scratch = [
        pltpu.VMEM((3, 2, chans, 2, chans_in, wide), LOW),
        pltpu.VMEM((chans, 2, chans_in, wide), LOW),
    ]
    padded = pltpu.VMEM((spots + 2 * GAP, wide), FULL)
    z0, zp, stats, xm = call(
        functools.partial(entry_forward_kernel, plan),
        (marks, *x_parts, *entry_shards),
        [VMEM] + [ANY] * (2 * chans),
        [field, field, ((4, wide), FULL), ((2, spots, deep), LOW)],
        [VMEM] * 4,
        [pltpu.VMEM((chans, 2, spots, 2 * chans_in), LOW)]
        + entry_scratch
        + [
            pltpu.VMEM((spots + 2 * GAP, deep), FULL),
            pltpu.VMEM((3, spots + pitch, deep), LOW),
            pltpu.SemaphoreType.DMA((7 * chans,)),
            pltpu.SemaphoreType.DMA((chans,)),
        ],
        "entry_forward",
        conv_flops // 2,
    )
    mid_shards = []

    def second_hop(layer):
        return lambda value: mid_shards.append(gathered(layer, plan, (value,)))

    mid_second = tied(conv_mid_w[1], stats)
    stats = micro_sums(stats, plan, (), [second_hop(mid_first)])
    mid_third = tied(conv_mid_w[2], stats)
    stat0, statp = stats[0:2], stats[2:4]

    weight_scratch = pltpu.VMEM((3, 3, wide, wide), LOW)
    shard_sems = pltpu.SemaphoreType.DMA((chans,))

    def mid_forward(layers, sources, source_stats, weights, name):
        outs = [field, ((2, wide), FULL), ((spots, wide), LOW)]
        if len(layers) == 2:
            outs.append(field)
        k = len(layers)
        return call(
            functools.partial(mid_forward_kernel, plan, layers),
            (chan_at, inv, marks, pars, *sources, *source_stats, *weights),
            [SMEM, SMEM] + [VMEM] * (2 + 2 * k) + [HBM] * chans,
            outs,
            [VMEM] * len(outs),
            [weight_scratch, padded, pltpu.VMEM((3, spots + 2 * pitch, wide), LOW), shard_sems],
            name,
            0 if name in HIDERS else conv_flops,
        )

    z2, stat1, a_first = mid_forward((0,), (z0,), (stat0,), mid_shards[0], "mid_forward_a")
    og_parts = swapped(tied(grad_spread, stat1), plan)
    stat1 = micro_sums(stat1, plan, (), [second_hop(mid_second)])
    z3, stat3, a_second, h1 = mid_forward(
        (1, 2), (z2, zp), (stat1, statp), mid_shards[1], "mid_forward_b"
    )
    stat3 = micro_sums(stat3, plan, (), [second_hop(mid_third)])
    z4, stat4, a_third = mid_forward((3,), (z3,), (stat3,), mid_shards[2], "mid_forward_c")
    stat4 = micro_sums(tied(stat4, *og_parts[1:]), plan)

    block, gh2, back4 = call(
        functools.partial(head_kernel, plan),
        (chan_at, inv, marks, pars, z4, stat4, h1, *og_parts),
        [SMEM, SMEM] + [VMEM] * (5 + chans),
        [((chans, spots, chans_out), LOW), field, ((2, wide), FULL)],
        [VMEM] * 3,
        [pltpu.VMEM((chans, spots, chans_out), LOW)],
        "head",
    )
    back4 = micro_sums(back4, plan)
    block_parts = swapped(block, plan)

    def mid_backward(j, kind, g, z, stat, back, weights, others, extra_outs, name):
        count = 3 if kind == "join" else 2
        outs = [((3, spots + 2 * pitch, wide), LOW), field, ((count, wide), FULL)] + extra_outs
        return call(
            functools.partial(mid_backward_kernel, plan, j, kind),
            (chan_at, inv, marks, pars, g, z, stat, back, *weights, *others),
            [SMEM, SMEM] + [VMEM] * 6 + [HBM] * chans + [VMEM] * len(others),
            outs,
            [VMEM] * len(outs),
            [weight_scratch, padded, padded, shard_sems],
            name,
            0 if name in HIDERS else conv_flops,
        )

    def mid_weight(a, ga, name):
        return call(
            functools.partial(mid_weight_kernel, plan),
            (chan_at, a, ga),
            [SMEM, VMEM, VMEM],
            [((chans // 2, 9 * chans_out, wide), LOW)] * 2,
            [VMEM, VMEM],
            [pltpu.VMEM((wide, spots), LOW)] * 2,
            name,
            0 if name in HIDERS else conv_flops,
        )
    ga_third, g3, back3 = mid_backward(
        4, "plain", gh2, z4, stat4, back4, mid_shards[2], (z3, stat3), [], "mid_backward_c"
    )
    sums_of = {}

    def weigh(key, a, ga, order, behind=()):
        def job(value):
            keep, send = mid_weight(tied(a, value), ga, "mid_weight_" + key)
            others = [part for other in behind for part in sums_of[other].received]
            if others:
                send = tied(send, *others)
            sums_of[key] = WeightSum(keep, send, plan, order)
            return [send] + [sums_of[other].advance(send) for other in behind]

        return job

    def step(key):
        return lambda value: sums_of[key].advance(value)

    back3 = micro_sums(
        tied(back3, *block_parts[1:]), plan,
        [weigh("c", a_third, ga_third, ["c", (0,), (1,), (2,)])],
        [step("c")],
    )
    ga_second, gh1, back12 = mid_backward(
        3, "join", g3, z3, stat3, back3, mid_shards[1], (z2, zp, stat1, statp, gh2), [],
        "mid_backward_b",
    )
    back12 = micro_sums(
        back12, plan, [weigh("b", a_second, ga_second, ["c", (1,), (0,), (2,)], "c")], [step("b")]
    )
    ga_first, g1, back0, gzp = mid_backward(
        1, "entry", gh1, z2, stat1, back12, mid_shards[0], (z0, stat0, zp, statp),
        [((spots, wide), LOW)], "mid_backward_a",
    )
    back0 = micro_sums(
        back0, plan,
        [weigh("a", a_first, ga_first, [(0,), "c", (1,), (2,)], "cb")],
        [step("c")],
    )
    (gm,) = call(
        functools.partial(entry_norm_kernel, plan),
        (inv, marks, pars, g1, z0, stat0, back0),
        [SMEM] + [VMEM] * 6,
        [((2, spots + pitch, wide), LOW)],
        [VMEM],
        [padded],
        "entry_norm",
    )
    token = sums_of["a"].advance(gm)
    (gx,) = call(
        functools.partial(entry_backward_kernel, plan),
        (marks, tied(gm, token), gzp, *entry_shards),
        [VMEM] * 3 + [ANY] * chans,
        [((chans, 2, spots, 2 * chans_in), LOW)],
        [VMEM],
        entry_scratch + [pltpu.SemaphoreType.DMA((7 * chans,))],
        "entry_backward",
    )
    gx_parts = swapped(gx, plan)
    keep, send = call(
        functools.partial(entry_weight_kernel, plan),
        (xm, tied(gm, gx), gzp),
        [VMEM] * 3,
        [((chans // 2, 10 * chans_in, wide), LOW)] * 2,
        [VMEM] * 2,
        [pltpu.VMEM((2, deep, spots), LOW)],
        "entry_weight",
    )
    send = tied(
        send, gx_parts[chans // 2], *[part for key in "abc" for part in sums_of[key].received]
    )
    sums_of["e"] = WeightSum(keep, send, plan, [(0,), (1,), "c", (2,)])

    def chain(last, keys):
        for key in keys:
            last = sums_of[key].advance(last)
        return last

    def joined(kernel, parts, shape, axis, extra, dtype, whole, name):
        edge = tuple(extra if i == axis else n for i, n in enumerate(shape))
        return call(
            functools.partial(kernel, plan),
            (chan_at, *parts),
            [SMEM] + [VMEM] * chans,
            [(shape, dtype), (edge, LOW)],
            [VMEM] * 2,
            [pltpu.VMEM(whole, LOW)],
            name,
        )

    def topped(main, tail, axis):
        first = lax.slice_in_dim(main, 0, tail.shape[axis], axis=axis) + tail.astype(main.dtype)
        return lax.dynamic_update_slice(main, first, (0, 0, 0))

    token = chain(send, "cab")
    token = chain(tied(token, gx_parts[-1]), "e")
    gx_parts[0] = tied(gx_parts[0], token)
    feature_grad, feature_tail = joined(
        join_features_kernel, gx_parts, features.shape, 2, EXTRA * 4 * width, FULL,
        (chans, 2, spots, 2 * chans_in), "join_features",
    )
    token = feature_tail
    feature_tail = to_next(feature_tail)
    token = chain(token, "be")
    block_parts[0] = tied(block_parts[0], token)
    block_out, block_tail = joined(
        join_rows_kernel, block_parts, out_grad.shape, 1, EXTRA * width, LOW,
        (chans, spots, chans_out), "join_rows",
    )
    token = block_tail
    block_tail = to_next(block_tail)
    token = chain(token, "aecb")
    feature_grad = topped(feature_grad, tied(feature_tail, token), 2)
    block_out = jnp.swapaxes(topped(block_out, tied(block_tail, token), 1), 1, 2)
    token = chain(token, "eabeaea")

    def mine(key):
        return sums_of[key].mine(sums_of[key].last[0])

    last = jnp.stack([mine(key) for key in "abce"]).astype(jnp.int32)
    (conv_mid_grad,) = call(
        mid_assembly_kernel,
        (last, *[part for key in "abc" for part in sums_of[key].halves(token)]),
        [SMEM] + [VMEM] * 6,
        [((3, 9 * chans_out, wide), FULL)],
        [HBM],
        [pltpu.VMEM((3, 9 * chans_out, wide), FULL), pltpu.SemaphoreType.DMA((3,))],
        "mid_assembly",
    )
    entry_own, entry_other = sums_of["e"].halves(token)
    conv_mid_grad = conv_mid_grad.reshape(3, 3, 3, chans_out, wide)
    conv_in_grad, proj_grad = call(
        entry_assembly_kernel,
        (last, entry_own, entry_other),
        [SMEM] + [VMEM] * 2,
        [((9 * chans_in, wide), FULL), ((chans_in, wide), FULL)],
        [HBM] * 2,
        [pltpu.VMEM((10 * chans_in, wide), FULL), pltpu.SemaphoreType.DMA((2,))],
        "entry_assembly",
    )
    conv_in_grad = conv_in_grad.reshape(3, 3, chans_in, wide)

    sums = jnp.stack(
        [back0[1], back12[1], back12[2], back3[1], back4[1]]
        + [back0[0], back12[0], back12[0], back3[0], back4[0]]
    )
    sums = sums + flipped(sums, "chan", splits)
    sums = lax.dynamic_slice_in_dim(sums, chan * chans_out, chans_out, 1)
    return (
        block_out, feature_grad, conv_in_grad, proj_grad, conv_mid_grad, sums[:5], sums[5:],
    )


def solution(mesh):
    placed = (
        P(None, "chan", "space"),
        P(),
        P(None, None, "chan", None),
        P("chan", None),
        P(None, None, None, "chan", None),
        P(None, "chan"),
        P(None, "chan"),
        P(None, "chan", "space"),
    )
    return jax.shard_map(
        shards,
        mesh=mesh,
        in_specs=placed,
        out_specs=(
            P(None, "chan", "space"),
            P(None, "chan", "space"),
            P(None, None, "chan", None),
            P("chan", None),
            P(None, None, None, "chan", None),
            P(None, "chan"),
            P(None, "chan"),
        ),
        check_vma=False,
    )
```

```python
import collections
import functools

import jax
import jax.numpy as jnp
import numpy as np
from jax import lax
from jax.experimental import pallas as pl
from jax.experimental.pallas import tpu as pltpu
from jax.sharding import PartitionSpec as P

MICRO = 2
WIN = 20
MOST_SIDE = 9
EXTRA = MOST_SIDE - 1
BLOCK = 16
ROW_BLOCK = 64
GAP = 8
EPS = 1e-05
SLACK_BYTES = 6 * 1024 * 1024
LOW = jnp.bfloat16
HIDERS = ("mid_forward_c", "mid_backward_c", "mid_backward_b", "mid_weight_b")
HIDERS += ("mid_backward_a", "mid_weight_a", "entry_backward", "entry_weight")
FULL = jnp.float32

PLAN_FIELDS = ["chans", "spaces", "splits", "rows_dev", "own_rows", "bases", "pitch", "width"]
PLAN_FIELDS += ["spots", "chans_in", "chans_out", "wide"]
Plan = collections.namedtuple("Plan", PLAN_FIELDS)

VMEM = pl.BlockSpec(memory_space=pltpu.VMEM)
SMEM = pl.BlockSpec(memory_space=pltpu.SMEM)
HBM = pl.BlockSpec(memory_space=pltpu.HBM)
ANY = pl.BlockSpec(memory_space=pl.ANY)


def flipped(value, axis, bit):
    count = lax.axis_size(axis)
    return lax.ppermute(value, axis, [(i, i ^ bit) for i in range(count)])


def from_next(value):
    count = lax.axis_size("space")
    return lax.ppermute(value, "space", [(i + 1, i) for i in range(count - 1)])


def to_next(value):
    count = lax.axis_size("space")
    return lax.ppermute(value, "space", [(i, i + 1) for i in range(count - 1)])


def exchanged(value, chan_bits, space_bits, plan):
    count = plan.chans * plan.spaces
    flip = chan_bits * plan.spaces + space_bits
    return lax.ppermute(value, ("chan", "space"), [(i, i ^ flip) for i in range(count)])


def tied(value, *others):
    return lax.optimization_barrier((value, others))[0]


def gathered(own, plan, then=()):
    parts = {0: own}
    for rel in range(1, plan.chans):
        bit = rel & -rel
        source = parts[rel ^ bit]
        if rel != bit and then:
            source = tied(source, *then)
        parts[rel] = flipped(source, "chan", bit)
    return [parts[rel] for rel in range(plan.chans)]


def swapped(parts, plan):
    return [parts[0]] + [flipped(parts[rel], "chan", rel) for rel in range(1, plan.chans)]


def micro_sums(value, plan, early=(), late=()):
    bits = []
    bit = 1
    while bit < plan.splits:
        bits.append((bit, 0))
        bit *= 2
    bit = 1
    while bit < plan.spaces:
        bits.append((0, bit))
        bit *= 2
    for i in range(0, len(bits), 2):
        pair = bits[i : i + 2]
        start = value
        one = exchanged(value, *pair[0], plan)
        if len(pair) == 2:
            two = exchanged(value, *pair[1], plan)
            both = exchanged(value, pair[0][0] ^ pair[1][0], pair[0][1] ^ pair[1][1], plan)
        done = []
        if i == 0:
            done = [job(one, [two, both] if len(pair) == 2 else []) for job in early]
        elif i == 2:
            done = [job(one if takes == "one" else start) for takes, job in late]
        done = [token for token in jax.tree.leaves(done) if token is not None]
        if done:
            one = tied(one, *done)
        value = value + one
        if len(pair) == 2:
            value = value + (two + both)
    return value


class WeightSum:
    def __init__(self, keep, send, plan, order):
        self.send, self.plan = send, plan
        self.kept = keep
        self.received = [] if send is None else [flipped(send, "chan", 1)]
        self.steps = []
        named = [bit for step in order if step != "c" for bit in step]
        rest = [k for k in range(plan.spaces.bit_length() - 1) if k not in named]
        for step in list(order) + [(k,) for k in rest]:
            if step == "c":
                self.steps += [("chan", (1 << k,)) for k in range(1, plan.chans.bit_length() - 1)]
            else:
                self.steps.append(("space", tuple(1 << k for k in step)))
        self.steps[-1] = ("swap", self.steps[-1][1])
        self.gathers = [bits for axis, bits in self.steps if axis == "space"][::-1]
        self.last = self.gathers[-1]
        self.gathering = False

    def mine(self, bit):
        return (lax.axis_index("space") // bit) % 2

    def added(self, pick):
        total = pick(self.kept).astype(FULL)
        for part in self.received:
            total = total + pick(part).astype(FULL)
        return total.astype(LOW)

    def flips(self, bits):
        ways = []
        for number in range(1, 1 << len(bits)):
            held = [(number >> i) & 1 for i in range(len(bits))]
            ways.append((sum(bit for bit, on in zip(bits, held) if on), held))
        return ways

    def take(self, *after):
        if after and self.received:
            self.received[0] = tied(self.received[0], *after)
        elif after:
            self.kept = tied(self.kept, *after)

    def advance(self, *after):
        self.take(*after)
        if self.steps:
            axis, bits = self.steps.pop(0)
            if axis == "swap":
                kept = self.added(lambda part: part)
                sent = [(bits[0], kept)]
                axis = "space"
            elif axis == "chan":
                kept = self.added(lambda part: part[0::2])
                sent = [(bits[0], self.added(lambda part: part[1::2]))]
            else:
                size = self.kept.shape[1] >> len(bits)

                def piece(held):
                    at = 0
                    for bit, on in zip(bits[::-1], held[::-1]):
                        at = 2 * at + (self.mine(bit) if not on else 1 - self.mine(bit))
                    return self.added(lambda part: lax.dynamic_slice_in_dim(part, at * size, size, 1))

                kept = piece([0] * len(bits))
                sent = [(flip, piece(held)) for flip, held in self.flips(bits)]
            self.kept = kept
            self.received = [flipped(part, axis, flip) for flip, part in sent]
            return sent[0][1]
        bits = self.gathers.pop(0)
        whole = self.ordered() if self.gathering else self.added(lambda part: part)
        self.gathering = bits
        self.kept = whole
        self.received = [flipped(whole, "space", flip) for flip, _ in self.flips(bits)]
        return whole

    def ordered(self):
        parts = [self.kept] + self.received
        for bit in self.gathering:
            turned = self.mine(bit) == 0
            joined = []
            for i in range(0, len(parts), 2):
                low = jnp.concatenate(parts[i : i + 2], axis=1)
                high = jnp.concatenate(parts[i : i + 2][::-1], axis=1)
                joined.append(jnp.where(turned, low, high))
            parts = joined
        return parts[0]

    def halves(self, *after):
        while self.steps or self.gathers:
            self.advance(*after)
        self.take(*after)
        return self.kept[0], self.received[0][0]


def tiles(count, size):
    return [slice(i, i + size) for i in range(0, count, size)]


def logistic(u):
    return 1.0 / (1.0 + jnp.exp(-u))


def slope(u):
    g = logistic(u)
    return g * (1.0 + u * (1.0 - g))


def moments(stat, inv_count):
    mean = stat[0:1, :] * inv_count
    inverse = lax.rsqrt(stat[1:2, :] * inv_count - mean * mean + EPS)
    return mean, inverse


def dot(a, b):
    return lax.dot_general(a, b, (((1,), (0,)), ((), ())), preferred_element_type=FULL)


def dot_t(a, b):
    return lax.dot_general(a, b, (((1,), (1,)), ((), ())), preferred_element_type=FULL)


def unit(count):
    rows = lax.broadcasted_iota(jnp.int32, (count, count), 0)
    columns = lax.broadcasted_iota(jnp.int32, (count, count), 1)
    return jnp.where(rows == columns, 1.0, 0.0).astype(LOW)


def clear_gaps(ref, spots):
    zero = jnp.zeros((GAP, ref.shape[-1]), ref.dtype)
    ref[pl.ds(0, GAP), :] = zero
    ref[pl.ds(GAP + spots, GAP), :] = zero


def column_sum(x):
    return jnp.sum(x, axis=0, keepdims=True)


def start_shards(chan, shard_refs, w_ref, sems):
    size = shard_refs[0].shape[2]
    copies = []
    for rel, ref in enumerate(shard_refs):
        place = pl.ds(pl.multiple_of((chan ^ rel) * size, size), size)
        copy = pltpu.make_async_copy(ref, w_ref.at[:, :, place, :], sems.at[rel])
        copy.start()
        copies.append(copy)
    return copies


def matmul_tile(plan):
    for size in (288, 192, 144, 96, 64):
        if plan.spots % size == 0:
            return size
    return plan.spots


def vector_tile(plan):
    return 2 * plan.pitch // 4 if plan.pitch % 32 == 0 else plan.pitch


def feature_pick(plan, side, first, count):
    shape = (2 * MOST_SIDE * BLOCK, count)
    place = lax.broadcasted_iota(jnp.int32, shape, 0)
    cell = lax.broadcasted_iota(jnp.int32, shape, 1) + first
    row, column = place & (BLOCK - 1), place >> (BLOCK.bit_length() - 1)
    phase = jnp.where(column >= MOST_SIDE, 1, 0)
    column = column - MOST_SIDE * phase
    source = (2 * row + phase) * (2 * plan.width) + 2 * column + side
    return jnp.where(source == cell, 1.0, 0.0).astype(LOW)


def row_pick(plan, first, count, turned=False):
    spots = MOST_SIDE * ROW_BLOCK
    shape = (count, spots) if turned else (spots, count)
    place = lax.broadcasted_iota(jnp.int32, shape, 1 if turned else 0)
    cell = lax.broadcasted_iota(jnp.int32, shape, 0 if turned else 1) + first
    row, column = place & (ROW_BLOCK - 1), place >> (ROW_BLOCK.bit_length() - 1)
    return jnp.where(row * plan.width + column == cell, 1.0, 0.0).astype(LOW)


def spread_features_kernel(plan, chan_ref, x_ref, halo_ref, out_ref):
    chan = chan_ref[0]
    size, lanes = plan.chans_in, BLOCK * 4 * plan.width
    columns = MOST_SIDE

    def stacked(part):
        blank = jnp.zeros_like(part[0])
        even, odd = [], []
        for m in range(MICRO):
            even += [part[m], blank]
            odd += [blank, part[m]]
        return jnp.concatenate(even, 0), jnp.concatenate(odd, 0)

    have = x_ref.shape[2]
    own, extra = have % lanes, halo_ref.shape[2]
    picks = [feature_pick(plan, side, 0, lanes) for side in range(2)]
    left = [feature_pick(plan, side, 0, own) for side in range(2)]
    right = [feature_pick(plan, side, own, extra) for side in range(2)]
    for j in range(-(-(plan.rows_dev + EXTRA) // BLOCK)):
        start = j * lanes
        if start + lanes <= have:
            even, odd = stacked([x_ref[m, :, start : start + lanes] for m in range(MICRO)])
            result = dot_t(picks[0], even) + dot_t(picks[1], odd)
        else:
            even, odd = stacked([x_ref[m, :, start:have] for m in range(MICRO)])
            result = dot_t(left[0], even) + dot_t(left[1], odd)
            even, odd = stacked([halo_ref[m] for m in range(MICRO)])
            result += dot_t(right[0], even) + dot_t(right[1], odd)
        result = result.astype(LOW)
        for split, base in enumerate(plan.bases):
            row = j * BLOCK - base
            if row < 0 or row >= plan.pitch:
                continue
            for m in range(MICRO):
                to = chan ^ (m * plan.splits + split)
                for phase in range(2):
                    for c in range(columns):
                        at = (phase * columns + c) * BLOCK
                        part = result[at : at + BLOCK, m * 2 * size : (m + 1) * 2 * size]
                        spot = c * plan.pitch + row
                        out_ref[to, phase, spot : spot + BLOCK] = part


def spread_rows_kernel(plan, chan_ref, x_ref, halo_ref, out_ref):
    chan = chan_ref[0]
    size, spots = plan.chans_out, ROW_BLOCK * plan.width
    have = x_ref.shape[1]
    own, extra = have % spots, halo_ref.shape[1]
    pick, left = row_pick(plan, 0, spots), row_pick(plan, 0, own)
    right = row_pick(plan, own, extra)
    for j in range(-(-(plan.rows_dev + EXTRA) // ROW_BLOCK)):
        start = j * spots
        for m in range(MICRO):
            if start + spots <= have:
                result = dot(pick, x_ref[m, start : start + spots])
            else:
                result = dot(left, x_ref[m, start:have]) + dot(right, halo_ref[m])
            result = result.astype(LOW)
            for split, base in enumerate(plan.bases):
                low, high = max(j * ROW_BLOCK, base), min((j + 1) * ROW_BLOCK, base + plan.pitch)
                if low >= high:
                    continue
                to = chan ^ (m * plan.splits + split)
                for c in range(MOST_SIDE):
                    at = c * ROW_BLOCK + low - j * ROW_BLOCK
                    spot = c * plan.pitch + low - base
                    out_ref[to, spot : spot + high - low] = result[at : at + high - low]


def laid_rows(plan, whole_ref, m, c, low, high, phase=None):
    pieces = []
    for row in range(low, high, BLOCK):
        total = None
        for split, base in enumerate(plan.bases):
            if not base <= row < base + plan.pitch:
                continue
            spots = pl.ds(c * plan.pitch + row - base, BLOCK)
            at = m * plan.splits + split
            part = whole_ref[at, spots] if phase is None else whole_ref[at, phase, spots]
            total = part if total is None else total + part
        pieces.append(total)
    return pieces


def join_rows_kernel(plan, chan_ref, *refs):
    parts = refs[: plan.chans]
    out_ref, tail_ref, whole_ref = refs[plan.chans :]
    chan = chan_ref[0]
    for rel in range(plan.chans):
        whole_ref[chan ^ rel] = parts[rel][...]
    spots = ROW_BLOCK * plan.width
    have = out_ref.shape[1]
    own, extra = have % spots, tail_ref.shape[1]
    pick, left = row_pick(plan, 0, spots, True), row_pick(plan, 0, own, True)
    right = row_pick(plan, own, extra, True)
    limit = plan.rows_dev + EXTRA
    for j in range(-(-limit // ROW_BLOCK)):
        start = j * spots
        low, high = j * ROW_BLOCK, min((j + 1) * ROW_BLOCK, limit)
        for m in range(MICRO):
            pieces = []
            for c in range(MOST_SIDE):
                pieces += laid_rows(plan, whole_ref, m, c, low, high)
                if high - low < ROW_BLOCK:
                    blank = (ROW_BLOCK - high + low, plan.chans_out)
                    pieces.append(jnp.zeros(blank, LOW))
            rows = jnp.concatenate(pieces, 0)
            if start + spots <= have:
                out_ref[m, start : start + spots] = dot(pick, rows).astype(LOW)
            else:
                out_ref[m, start:have] = dot(left, rows).astype(LOW)
                tail_ref[m] = dot(right, rows).astype(LOW)


def join_features_kernel(plan, chan_ref, *refs):
    parts = refs[: plan.chans]
    out_ref, tail_ref, whole_ref = refs[plan.chans :]
    chan = chan_ref[0]
    for rel in range(plan.chans):
        whole_ref[chan ^ rel] = parts[rel][...]
    size = plan.chans_in
    one = unit(2 * size)
    lanes = BLOCK * 4 * plan.width
    have = out_ref.shape[2]
    own, extra = have % lanes, tail_ref.shape[2]
    picks = [feature_pick(plan, side, 0, lanes) for side in range(2)]
    left = [feature_pick(plan, side, 0, own) for side in range(2)]
    right = [feature_pick(plan, side, own, extra) for side in range(2)]
    for j in range(-(-(plan.rows_dev + EXTRA) // BLOCK)):
        start = j * lanes
        first, second = [], []
        for m in range(MICRO):
            pieces = []
            for phase in range(2):
                for c in range(MOST_SIDE):
                    row = j * BLOCK
                    pieces += laid_rows(plan, whole_ref, m, c, row, row + BLOCK, phase)
            turned = dot_t(one, jnp.concatenate(pieces, 0)).astype(LOW)
            first.append(turned[:size])
            second.append(turned[size:])
        first, second = jnp.concatenate(first, 0), jnp.concatenate(second, 0)
        if start + lanes <= have:
            result = dot(first, picks[0]) + dot(second, picks[1])
            for m in range(MICRO):
                out_ref[m, :, start : start + lanes] = result[m * size : (m + 1) * size]
        else:
            result = dot(first, left[0]) + dot(second, left[1])
            tail = dot(first, right[0]) + dot(second, right[1])
            for m in range(MICRO):
                out_ref[m, :, start:have] = result[m * size : (m + 1) * size]
                tail_ref[m] = tail[m * size : (m + 1) * size].astype(LOW)


def entry_copies(plan, shard_refs, w_ref, wp_ref, sems):
    copies = []
    for rel in range(plan.chans):
        for a in range(3):
            sem = sems.at[7 * rel + 2 * a]
            source = shard_refs[rel].at[pl.ds(3 * a + 1, 2)]
            copies.append(pltpu.make_async_copy(source, w_ref.at[a, 0, rel], sem))
            sem = sems.at[7 * rel + 2 * a + 1]
            source = shard_refs[rel].at[3 * a]
            copies.append(pltpu.make_async_copy(source, w_ref.at[a, 1, rel, 1], sem))
        source = shard_refs[rel].at[9]
        copies.append(pltpu.make_async_copy(source, wp_ref.at[rel, 0], sems.at[7 * rel + 6]))
    for copy in copies:
        copy.start()
    for rel in range(plan.chans):
        blank = jnp.zeros(wp_ref.shape[2:], LOW)
        wp_ref[rel, 1] = blank
        for a in range(3):
            w_ref[a, 1, rel, 0] = blank
    return copies


def entry_forward_kernel(plan, marks_ref, *refs):
    n = plan.chans
    x_refs, shard_refs = refs[:n], refs[n : 2 * n]
    e_ref, p_ref, stat_ref, xm_ref = refs[2 * n : 2 * n + 4]
    x_ref, w_ref, wp_ref, xs_ref, am_ref, sems, x_sems = refs[2 * n + 4 :]
    x_copies = []
    for rel in range(n):
        x_copies.append(pltpu.make_async_copy(x_refs[rel], x_ref.at[rel], x_sems.at[rel]))
        x_copies[-1].start()
    copies = entry_copies(plan, shard_refs, w_ref, wp_ref, sems)
    size = 2 * plan.chans_in
    deep = n * size
    pitch = plan.pitch
    for k in range(3):
        am_ref[k, 0:pitch] = jnp.zeros((pitch, deep), LOW)
    clear_gaps(xs_ref, plan.spots)
    for rel in range(n):
        x_copies[rel].wait()
        lanes = slice(rel * size, (rel + 1) * size)
        for t in tiles(plan.spots, vector_tile(plan)):
            own = marks_ref[t, 0:1]
            for row in range(2):
                value = x_ref[rel, row, t].astype(FULL) * own
                low = value.astype(LOW)
                xm_ref[row, t, lanes] = low
                am_ref[row, pitch + t.start : pitch + t.stop, lanes] = low
                if row == 1:
                    xs_ref[GAP + t.start : GAP + t.stop, lanes] = value
    for t in tiles(plan.spots, vector_tile(plan)):
        above = xs_ref[GAP + t.start - 1 : GAP + t.stop - 1] * marks_ref[t, 1:2]
        am_ref[2, pitch + t.start : pitch + t.stop] = above.astype(LOW)
    for copy in copies:
        copy.wait()
    weights = w_ref[...].reshape(6 * deep, plan.wide)
    proj = wp_ref[...].reshape(deep, plan.wide)
    sums = [0.0] * 4
    for t in tiles(plan.spots, matmul_tile(plan)):
        own = marks_ref[t, 0:1]
        pieces = []
        for k in (2, 0, 1):
            pieces.append(am_ref[k, pitch + t.start : pitch + t.stop])
            pieces.append(am_ref[k, t])
        z = dot(jnp.concatenate(pieces, 1), weights)
        e_ref[t] = z.astype(LOW)
        p = dot(pieces[2], proj)
        p_ref[t] = p.astype(LOW)
        zm, pm = z * own, p * own
        for i, term in enumerate((zm, zm * z, pm, pm * p)):
            sums[i] = sums[i] + column_sum(term)
    stat_ref[...] = jnp.concatenate(sums, 0)


def mid_forward_kernel(plan, layers, chan_ref, inv_ref, marks_ref, par_ref, *refs):
    k = len(layers)
    n = plan.chans
    z_refs, stat_refs, shard_refs = refs[:k], refs[k : 2 * k], refs[2 * k : 2 * k + n]
    outs = refs[2 * k + n :]
    if k == 2:
        z_ref, out_stat_ref, a_ref, h_ref, w_ref, xs_ref, xa_ref, sems = outs
    else:
        z_ref, out_stat_ref, a_ref, w_ref, xs_ref, xa_ref, sems = outs
        h_ref = None
    copies = start_shards(chan_ref[0], shard_refs, w_ref, sems)
    inv = inv_ref[0]
    norms = [moments(stat[...], inv) for stat in stat_refs]
    wide, pitch = plan.wide, plan.pitch
    clear_gaps(xs_ref, plan.spots)
    for i in range(3):
        blank = jnp.zeros((pitch, wide), LOW)
        xa_ref[i, 0:pitch] = blank
        xa_ref[i, pitch + plan.spots : 2 * pitch + plan.spots] = blank
    for t in tiles(plan.spots, vector_tile(plan)):
        own = marks_ref[t, 0:1]
        u = 0.0
        for (mean, inverse), src, j in zip(norms, z_refs, layers):
            u = u + (par_ref[j : j + 1] * ((src[t].astype(FULL) - mean) * inverse) + par_ref[5 + j : 6 + j])
        u = u * own
        a = u * logistic(u)
        if h_ref is not None:
            h_ref[t] = a.astype(LOW)
        xs_ref[GAP + t.start : GAP + t.stop] = a
        low = a.astype(LOW)
        a_ref[t] = low
        xa_ref[1, pitch + t.start : pitch + t.stop] = low
    for t in tiles(plan.spots, vector_tile(plan)):
        for i, step in ((0, -1), (2, 1)):
            part = xs_ref[GAP + t.start + step : GAP + t.stop + step]
            part = part * marks_ref[t, 1 + i // 2 : 2 + i // 2]
            xa_ref[i, pitch + t.start : pitch + t.stop] = part.astype(LOW)
    for copy in copies:
        copy.wait()
    weights = w_ref[...].reshape(9 * wide, wide)
    total, square = 0.0, 0.0
    for t in tiles(plan.spots, matmul_tile(plan)):
        own = marks_ref[t, 0:1]
        pieces = []
        for a in range(3):
            for b in range(3):
                pieces.append(xa_ref[a, t.start + b * pitch : t.stop + b * pitch])
        z = dot(jnp.concatenate(pieces, 1), weights)
        z_ref[t] = z.astype(LOW)
        zm = z * own
        total = total + column_sum(zm)
        square = square + column_sum(zm * z)
    out_stat_ref[...] = jnp.concatenate([total, square], 0)


def head_kernel(plan, chan_ref, inv_ref, marks_ref, par_ref, z_ref, stat_ref, h_ref, *refs):
    n = plan.chans
    og_refs = refs[:n]
    out_ref, g_ref, out_stat_ref, og_ref = refs[n:]
    chan = chan_ref[0]
    for rel in range(n):
        og_ref[chan ^ rel] = og_refs[rel][...]
    mean, inverse = moments(stat_ref[...], inv_ref[0])
    size = plan.chans_out
    for j in range(n):
        lanes = slice(j * size, (j + 1) * size)
        total, dotted = 0.0, 0.0
        for t in tiles(plan.spots, plan.pitch):
            own = marks_ref[t, 0:1]
            hat = (z_ref[t, lanes].astype(FULL) - mean[:, lanes]) * inverse[:, lanes]
            u = own * (par_ref[4:5, lanes] * hat + par_ref[9:10, lanes]) + h_ref[t, lanes].astype(FULL)
            s = logistic(u)
            out_ref[chan ^ j, t] = (u * s).astype(LOW)
            q = og_ref[j, t].astype(FULL) * (s * (1.0 + u * (1.0 - s))) * own
            g_ref[t, lanes] = q.astype(LOW)
            total = total + column_sum(q)
            dotted = dotted + column_sum(q * hat)
        out_stat_ref[0:1, lanes] = total
        out_stat_ref[1:2, lanes] = dotted


def norm_back(own, q, z, norm, gain, total, dotted, inv):
    mean, inverse = norm
    hat = (z - mean) * inverse
    return own * (gain * inverse) * (q - total * inv - hat * (dotted * inv))


def mid_backward_kernel(plan, j, kind, chan_ref, inv_ref, marks_ref, par_ref, *refs):
    n = plan.chans
    g_ref, z_ref, stat_ref, back_ref = refs[:4]
    shard_refs = refs[4 : 4 + n]
    refs = refs[4 + n :]
    add_ref = short_z_ref = None
    if kind == "join":
        src_refs, src_stats, add_ref = refs[:2], refs[2:4], refs[4]
        refs = refs[5:]
        layers = (1, 2)
    elif kind == "entry":
        src_refs, src_stats, short_z_ref, short_stat_ref = refs[:1], refs[1:2], refs[2], refs[3]
        refs = refs[4:]
        layers = (0,)
    else:
        src_refs, src_stats = refs[:1], refs[1:2]
        refs = refs[2:]
        layers = (3,)
    ga_ref, next_ref, out_stat_ref = refs[:3]
    refs = refs[3:]
    if kind == "entry":
        short_ref, refs = refs[0], refs[1:]
    w_ref, s0_ref, s2_ref, sems = refs
    copies = start_shards(chan_ref[0], shard_refs, w_ref, sems)
    inv = inv_ref[0]
    wide, pitch = plan.wide, plan.pitch
    norm = moments(stat_ref[...], inv)
    total, dotted = back_ref[0:1], back_ref[1:2]
    for ref in (s0_ref, s2_ref):
        clear_gaps(ref, plan.spots)
    for i in range(3):
        blank = jnp.zeros((pitch, wide), LOW)
        ga_ref[i, 0:pitch] = blank
        ga_ref[i, pitch + plan.spots : 2 * pitch + plan.spots] = blank
    if kind == "entry":
        short_norm = moments(short_stat_ref[...], inv)
    for t in tiles(plan.spots, vector_tile(plan)):
        own, upper, lower = (marks_ref[t, i : i + 1] for i in range(3))
        g = g_ref[t].astype(FULL)
        z = z_ref[t].astype(FULL)
        gz = norm_back(own, g, z, norm, par_ref[j : j + 1], total, dotted, inv)
        low = gz.astype(LOW)
        gz = low.astype(FULL)
        ga_ref[1, pitch + t.start : pitch + t.stop] = low
        s0_ref[GAP + t.start : GAP + t.stop] = gz * upper
        s2_ref[GAP + t.start : GAP + t.stop] = gz * lower
        if kind == "entry":
            back = norm_back(
                own, g, short_z_ref[t].astype(FULL), short_norm, par_ref[2:3], total,
                back_ref[2:3], inv,
            )
            short_ref[t] = back.astype(LOW)
    for t in tiles(plan.spots, vector_tile(plan)):
        first, last = GAP + t.start, GAP + t.stop
        to = slice(pitch + t.start, pitch + t.stop)
        ga_ref[0, to] = s0_ref[first + 1 : last + 1].astype(LOW)
        ga_ref[2, to] = s2_ref[first - 1 : last - 1].astype(LOW)
    for copy in copies:
        copy.wait()
    norms = [moments(stat[...], inv) for stat in src_stats]
    sums = [0.0] * (1 + len(layers))
    weights = jnp.concatenate([w_ref[a, b] for a in range(3) for b in range(3)], 1)
    for t in tiles(plan.spots, matmul_tile(plan)):
        own = marks_ref[t, 0:1]
        pieces = []
        for a in range(3):
            for b in range(3):
                back = (2 - b) * pitch
                pieces.append(ga_ref[a, t.start + back : t.stop + back])
        gx = dot_t(jnp.concatenate(pieces, 1), weights)
        u = 0.0
        hats = []
        for (mean, inverse), src, i in zip(norms, src_refs, layers):
            hat = (src[t].astype(FULL) - mean) * inverse
            hats.append(hat)
            u = u + (par_ref[i : i + 1] * hat + par_ref[5 + i : 6 + i])
        u = u * own
        if add_ref is not None:
            gx = gx + add_ref[t].astype(FULL)
        q = gx * slope(u) * own
        next_ref[t] = q.astype(LOW)
        sums[0] = sums[0] + column_sum(q)
        for i, hat in enumerate(hats):
            sums[1 + i] = sums[1 + i] + column_sum(q * hat)
    out_stat_ref[...] = jnp.concatenate(sums, 0)


def entry_norm_kernel(plan, inv_ref, marks_ref, par_ref, g_ref, e_ref, stat_ref, back_ref, gm_ref, s_ref):
    inv = inv_ref[0]
    norm = moments(stat_ref[...], inv)
    clear_gaps(s_ref, plan.spots)
    for k in range(2):
        gm_ref[k, plan.spots : plan.spots + plan.pitch] = jnp.zeros((plan.pitch, plan.wide), LOW)
    for t in tiles(plan.spots, vector_tile(plan)):
        own, upper = marks_ref[t, 0:1], marks_ref[t, 1:2]
        gz = norm_back(
            own, g_ref[t].astype(FULL), e_ref[t].astype(FULL), norm, par_ref[0:1], back_ref[0:1],
            back_ref[1:2], inv,
        )
        low = gz.astype(LOW)
        gm_ref[0, t] = low
        s_ref[GAP + t.start : GAP + t.stop] = low.astype(FULL) * upper
    for t in tiles(plan.spots, vector_tile(plan)):
        gm_ref[1, t] = s_ref[GAP + t.start + 1 : GAP + t.stop + 1].astype(LOW)


def entry_backward_kernel(plan, marks_ref, gm_ref, short_ref, *refs):
    n = plan.chans
    shard_refs = refs[:n]
    gx_ref, w_ref, wp_ref, sems = refs[n:]
    for copy in entry_copies(plan, shard_refs, w_ref, wp_ref, sems):
        copy.wait()
    size = 2 * plan.chans_in
    deep = n * size
    pitch, wide = plan.pitch, plan.wide

    def part(a, side):
        return w_ref[a, side].reshape(deep, wide)

    top_weights = [part(1, 0), part(1, 1), wp_ref[...].reshape(deep, wide)]
    top_weights = jnp.concatenate(top_weights, 1)
    low_weights = jnp.concatenate([part(2, 0), part(2, 1), part(0, 0), part(0, 1)], 1)
    for t in tiles(plan.spots, matmul_tile(plan)):
        own = marks_ref[t, 0:1]
        right = slice(t.start + pitch, t.stop + pitch)
        here = [gm_ref[0, t], gm_ref[0, right]]
        top = dot_t(jnp.concatenate(here + [short_ref[t]], 1), top_weights)
        here += [gm_ref[1, t], gm_ref[1, right]]
        low = dot_t(jnp.concatenate(here, 1), low_weights)
        for row, value in enumerate((top, low)):
            value = (value * own).astype(LOW)
            for rel in range(n):
                gx_ref[rel, row, t] = value[:, rel * size : (rel + 1) * size]


def mid_weight_kernel(plan, chan_ref, a_ref, ga_ref, keep_ref, send_ref, turned_ref, at_ref):
    wide, pitch = plan.wide, plan.pitch
    turned_ref[...] = dot_t(unit(wide), a_ref[...]).astype(LOW)
    chan = chan_ref[0]
    size = plan.chans_out
    for rel in range(plan.chans):
        place = pl.ds(pl.multiple_of((chan ^ rel) * size, size), size)
        at_ref[rel * size : (rel + 1) * size] = turned_ref[place]
    for a in range(3):
        for b in range(3):
            back = (2 - b) * pitch
            rows = slice((3 * a + b) * size, (3 * a + b + 1) * size)
            part = dot(at_ref[...], ga_ref[a, back : back + plan.spots]).astype(LOW)
            for rel in range(plan.chans):
                target = send_ref if rel & 1 else keep_ref
                target[rel // 2, rows] = part[rel * size : (rel + 1) * size]


def entry_weight_kernel(plan, xm_ref, gm_ref, short_ref, keep_ref, send_ref, xt_ref):
    n, size, wide, pitch = plan.chans, plan.chans_in, plan.wide, plan.pitch
    whole = unit(n * 2 * size)
    for row in range(2):
        xt_ref[row] = dot_t(whole, xm_ref[row]).astype(LOW)

    def put(tap, rel, value):
        target = send_ref if rel & 1 else keep_ref
        target[rel // 2, tap * size : (tap + 1) * size] = value

    def product(row, right):
        return dot(xt_ref[row], right).astype(LOW)

    for row, grad, a in ((0, 0, 1), (1, 0, 2), (1, 1, 0)):
        big = product(row, gm_ref[grad, 0 : plan.spots])
        side = product(row, gm_ref[grad, pitch : pitch + plan.spots])
        for rel in range(n):
            at = 2 * rel * size
            put(3 * a + 1, rel, big[at : at + size])
            put(3 * a + 2, rel, big[at + size : at + 2 * size])
            put(3 * a, rel, side[at + size : at + 2 * size])
    proj = product(0, short_ref[...])
    for rel in range(n):
        put(9, rel, proj[2 * rel * size : (2 * rel + 1) * size])


def mid_assembly_kernel(mine_ref, *refs):
    out_ref, hold_ref, sems = refs[6:]
    half = refs[0].shape[0]
    copies = []
    for layer in range(3):
        mine = mine_ref[layer]
        for i, part in enumerate(refs[2 * layer : 2 * layer + 2]):
            at = mine if i == 0 else 1 - mine
            rows = pl.ds(pl.multiple_of(at * half, 8), half)
            hold_ref[layer, rows] = part[...].astype(FULL)
        copies.append(pltpu.make_async_copy(hold_ref.at[layer], out_ref.at[layer], sems.at[layer]))
        copies[-1].start()
    for copy in copies:
        copy.wait()


def entry_assembly_kernel(mine_ref, own_ref, other_ref, conv_ref, proj_ref, hold_ref, sems):
    half = own_ref.shape[0]
    for i, part in enumerate((own_ref, other_ref)):
        at = mine_ref[3] if i == 0 else 1 - mine_ref[3]
        hold_ref[pl.ds(pl.multiple_of(at * half, 8), half)] = part[...].astype(FULL)
    cut = conv_ref.shape[0]
    copies = [
        pltpu.make_async_copy(hold_ref.at[pl.ds(0, cut)], conv_ref, sems.at[0]),
        pltpu.make_async_copy(hold_ref.at[pl.ds(cut, proj_ref.shape[0])], proj_ref, sems.at[1]),
    ]
    for copy in copies:
        copy.start()
    for copy in copies:
        copy.wait()


def call(kernel, operands, specs, outs, out_specs, scratch, name, flops=0):
    bytes_moved = sum(int(np.prod(o.shape)) * o.dtype.itemsize for o in operands)
    bytes_moved += sum(int(np.prod(s)) * jnp.dtype(d).itemsize for s, d in outs)
    bytes_moved = 1 if name in HIDERS else bytes_moved
    shapes = [jax.ShapeDtypeStruct(s, d) for s, d in outs]
    held = SLACK_BYTES
    for one in scratch:
        if one.memory_space == pltpu.VMEM:
            held += int(np.prod(one.shape)) * jnp.dtype(one.dtype).itemsize
    return pl.pallas_call(
        kernel,
        out_shape=shapes,
        in_specs=specs,
        out_specs=out_specs,
        scratch_shapes=scratch,
        compiler_params=pltpu.CompilerParams(vmem_limit_bytes=held),
        cost_estimate=pl.CostEstimate(
            flops=int(flops), bytes_accessed=int(bytes_moved), transcendentals=0
        ),
        name=name,
    )(*operands)


def marks_of(plan, sizes, top, first):
    sides = sizes // 2
    starts = jnp.cumsum(sides) - sides
    here = top + jnp.arange(plan.pitch, dtype=jnp.int32)
    inside = (
        (here[:, None] >= starts[None, :]) & (here[:, None] < (starts + sides)[None, :])
    ).astype(jnp.int32)
    begins = jnp.sum(inside * starts[None, :], axis=1)
    widths = jnp.sum(inside * sides[None, :], axis=1)
    local = here - begins
    owned = (widths > 0) & (begins >= first) & (begins < first + plan.own_rows)
    columns = jnp.arange(MOST_SIDE, dtype=jnp.int32)
    own = owned[None, :] & (columns[:, None] < widths[None, :])
    upper = jnp.broadcast_to((owned & (local > 0))[None, :], own.shape)
    lower = jnp.broadcast_to((owned & (local < widths - 1))[None, :], own.shape)
    marks = jnp.stack([own, upper, lower] + [jnp.zeros_like(own)] * 5, axis=-1)
    total = jnp.sum((sides * sides).astype(FULL))
    return marks.astype(FULL).reshape(plan.spots, 8), (1.0 / total).reshape(1)


def shards(features, image_sizes, conv_in_w, proj_w, conv_mid_w, norm_gain, norm_bias, out_grad):
    chans, spaces = lax.axis_size("chan"), lax.axis_size("space")
    splits = chans // MICRO
    width = WIN // 2
    rows_dev = features.shape[2] // (4 * width)
    own_rows = rows_dev // splits
    bases = tuple(split * own_rows // BLOCK * BLOCK for split in range(splits))
    need = max(split * own_rows - bases[split] for split in range(splits)) + own_rows + EXTRA
    pitch = -(-need // BLOCK) * BLOCK
    reach = -(-(rows_dev + EXTRA) // BLOCK) * BLOCK
    assert max(bases) + pitch <= reach and rows_dev + EXTRA == reach
    chans_in, chans_out = features.shape[1], norm_gain.shape[1]
    spots = MOST_SIDE * pitch
    plan = Plan(
        chans, spaces, splits, rows_dev, own_rows, bases, pitch, width, spots,
        chans_in, chans_out, chans * chans_out,
    )
    wide = plan.wide
    chan = lax.axis_index("chan")
    micro, split = chan // splits, chan % splits
    here = lax.axis_index("space") * rows_dev
    first = here + split * own_rows
    chan_at = chan.astype(jnp.int32).reshape(1)

    edge = features[:, :, : EXTRA * 4 * width]
    halo = from_next(edge)
    out_grad = jnp.swapaxes(out_grad, 1, 2)
    out_halo = from_next(out_grad[:, : EXTRA * width])
    (spread,) = call(
        functools.partial(spread_features_kernel, plan),
        (chan_at, features, tied(halo, out_halo)),
        [SMEM] + [VMEM] * 2,
        [((chans, 2, spots, 2 * chans_in), LOW)],
        [VMEM],
        [],
        "spread_features",
    )
    x_parts = swapped(spread, plan)
    slots = jnp.concatenate([norm_gain, norm_bias], axis=0)
    slots = lax.dynamic_update_slice(
        jnp.zeros((10, wide), FULL), slots, (jnp.int32(0), chan * chans_out)
    )
    bit = 1
    while bit < chans:
        slots = slots + flipped(slots, "chan", bit)
        bit *= 2
    pars = slots
    sizes = lax.dynamic_index_in_dim(image_sizes, micro, 0, keepdims=False)
    bases_at = jnp.asarray(bases, jnp.int32)[split]
    marks, inv = marks_of(plan, sizes, here + bases_at, first)

    (grad_spread,) = call(
        functools.partial(spread_rows_kernel, plan),
        (chan_at, out_grad, tied(out_halo, x_parts[1])),
        [SMEM] + [VMEM] * 2,
        [((chans, spots, chans_out), LOW)],
        [VMEM],
        [],
        "spread_rows",
    )

    entry_own = jnp.concatenate([conv_in_w.reshape(9, chans_in, wide), proj_w[None]], axis=0)
    entry_own = tied(entry_own, edge)
    entry_shards = gathered(entry_own, plan, (*x_parts[chans // 2 :], pars, grad_spread))
    mid_first = tied(conv_mid_w[0], *x_parts[chans // 2 :])

    conv_flops = 2 * spots * 9 * wide * wide
    field = ((spots, wide), LOW)
    deep = chans * 2 * chans_in
    entry_scratch = [
        pltpu.VMEM((3, 2, chans, 2, chans_in, wide), LOW),
        pltpu.VMEM((chans, 2, chans_in, wide), LOW),
    ]
    padded = pltpu.VMEM((spots + 2 * GAP, wide), FULL)
    z0, zp, stats, xm = call(
        functools.partial(entry_forward_kernel, plan),
        (marks, *x_parts, *entry_shards),
        [VMEM] + [ANY] * (2 * chans),
        [field, field, ((4, wide), FULL), ((2, spots, deep), LOW)],
        [VMEM] * 4,
        [pltpu.VMEM((chans, 2, spots, 2 * chans_in), LOW)]
        + entry_scratch
        + [
            pltpu.VMEM((spots + 2 * GAP, deep), FULL),
            pltpu.VMEM((3, spots + pitch, deep), LOW),
            pltpu.SemaphoreType.DMA((7 * chans,)),
            pltpu.SemaphoreType.DMA((chans,)),
        ],
        "entry_forward",
        conv_flops // 2,
    )
    mid_shards = []

    def second_hop(layer):
        return lambda value: mid_shards.append(gathered(layer, plan, (value,)))

    mid_second = tied(conv_mid_w[1], stats)
    stats = micro_sums(stats, plan, (), [("start", second_hop(mid_first))])
    mid_third = tied(conv_mid_w[2], stats)
    stat0, statp = stats[0:2], stats[2:4]

    weight_scratch = pltpu.VMEM((3, 3, wide, wide), LOW)
    shard_sems = pltpu.SemaphoreType.DMA((chans,))

    def mid_forward(layers, sources, source_stats, weights, name):
        outs = [field, ((2, wide), FULL), ((spots, wide), LOW)]
        if len(layers) == 2:
            outs.append(field)
        k = len(layers)
        return call(
            functools.partial(mid_forward_kernel, plan, layers),
            (chan_at, inv, marks, pars, *sources, *source_stats, *weights),
            [SMEM, SMEM] + [VMEM] * (2 + 2 * k) + [HBM] * chans,
            outs,
            [VMEM] * len(outs),
            [weight_scratch, padded, pltpu.VMEM((3, spots + 2 * pitch, wide), LOW), shard_sems],
            name,
            0 if name in HIDERS else conv_flops,
        )

    z2, stat1, a_first = mid_forward((0,), (z0,), (stat0,), mid_shards[0], "mid_forward_a")
    og_parts = swapped(tied(grad_spread, stat1), plan)
    stat1 = micro_sums(stat1, plan, (), [("start", second_hop(mid_second))])
    z3, stat3, a_second, h1 = mid_forward(
        (1, 2), (z2, zp), (stat1, statp), mid_shards[1], "mid_forward_b"
    )
    stat3 = micro_sums(stat3, plan, (), [("start", second_hop(mid_third))])
    z4, stat4, a_third = mid_forward((3,), (z3,), (stat3,), mid_shards[2], "mid_forward_c")
    stat4 = micro_sums(tied(stat4, *og_parts[1:]), plan)

    block, gh2, back4 = call(
        functools.partial(head_kernel, plan),
        (chan_at, inv, marks, pars, z4, stat4, h1, *og_parts),
        [SMEM, SMEM] + [VMEM] * (5 + chans),
        [((chans, spots, chans_out), LOW), field, ((2, wide), FULL)],
        [VMEM] * 3,
        [pltpu.VMEM((chans, spots, chans_out), LOW)],
        "head",
    )
    back4 = micro_sums(back4, plan)
    block_parts = swapped(block, plan)

    def mid_backward(j, kind, g, z, stat, back, weights, others, extra_outs, name):
        count = 3 if kind == "join" else 2
        outs = [((3, spots + 2 * pitch, wide), LOW), field, ((count, wide), FULL)] + extra_outs
        return call(
            functools.partial(mid_backward_kernel, plan, j, kind),
            (chan_at, inv, marks, pars, g, z, stat, back, *weights, *others),
            [SMEM, SMEM] + [VMEM] * 6 + [HBM] * chans + [VMEM] * len(others),
            outs,
            [VMEM] * len(outs),
            [weight_scratch, padded, padded, shard_sems],
            name,
            0 if name in HIDERS else conv_flops,
        )

    def mid_weight(a, ga, name):
        return call(
            functools.partial(mid_weight_kernel, plan),
            (chan_at, a, ga),
            [SMEM, VMEM, VMEM],
            [((chans // 2, 9 * chans_out, wide), LOW)] * 2,
            [VMEM, VMEM],
            [pltpu.VMEM((wide, spots), LOW)] * 2,
            name,
            0 if name in HIDERS else conv_flops,
        )
    ga_third, g3, back3 = mid_backward(
        4, "plain", gh2, z4, stat4, back4, mid_shards[2], (z3, stat3), [], "mid_backward_c"
    )
    sums_of = {}

    def weigh(key, a, ga, order, behind=()):
        def job(value, far):
            keep, send = mid_weight(tied(a, value), ga, "mid_weight_" + key)
            others = far + [part for other in behind for part in sums_of[other].received]
            if others:
                send = tied(send, *others)
            sums_of[key] = WeightSum(keep, send, plan, order)
            return [send] + [sums_of[other].advance(send) for other in behind]

        return job

    def step(key):
        return lambda value: sums_of[key].advance(value)

    back3 = micro_sums(
        tied(back3, *block_parts[1:]), plan,
        [weigh("c", a_third, ga_third, ["c", (0,), (1,), (2,)])],
        [("one", step("c"))],
    )
    ga_second, gh1, back12 = mid_backward(
        3, "join", g3, z3, stat3, back3, mid_shards[1], (z2, zp, stat1, statp, gh2), [],
        "mid_backward_b",
    )
    back12 = micro_sums(
        back12, plan, [weigh("b", a_second, ga_second, ["c", (1,), (0,), (2,)], "c")], [("one", step("b"))]
    )
    ga_first, g1, back0, gzp = mid_backward(
        1, "entry", gh1, z2, stat1, back12, mid_shards[0], (z0, stat0, zp, statp),
        [((spots, wide), LOW)], "mid_backward_a",
    )
    back0 = micro_sums(
        back0, plan,
        [weigh("a", a_first, ga_first, [(0,), "c", (1,), (2,)], "cb")],
        [("one", step("c"))],
    )
    (gm,) = call(
        functools.partial(entry_norm_kernel, plan),
        (inv, marks, pars, g1, z0, stat0, back0),
        [SMEM] + [VMEM] * 6,
        [((2, spots + pitch, wide), LOW)],
        [VMEM],
        [padded],
        "entry_norm",
    )
    token = sums_of["a"].advance(gm)
    (gx,) = call(
        functools.partial(entry_backward_kernel, plan),
        (marks, tied(gm, token), gzp, *entry_shards),
        [VMEM] * 3 + [ANY] * chans,
        [((chans, 2, spots, 2 * chans_in), LOW)],
        [VMEM],
        entry_scratch + [pltpu.SemaphoreType.DMA((7 * chans,))],
        "entry_backward",
    )
    gx_parts = swapped(gx, plan)
    keep, send = call(
        functools.partial(entry_weight_kernel, plan),
        (xm, tied(gm, gx), gzp),
        [VMEM] * 3,
        [((chans // 2, 10 * chans_in, wide), LOW)] * 2,
        [VMEM] * 2,
        [pltpu.VMEM((2, deep, spots), LOW)],
        "entry_weight",
    )
    send = tied(
        send, gx_parts[chans // 2], *[part for key in "abc" for part in sums_of[key].received]
    )
    sums_of["e"] = WeightSum(keep, send, plan, [(1,), (0,), "c", (2,)])

    def chain(last, keys):
        for key in keys:
            last = sums_of[key].advance(last)
        return last

    def joined(kernel, parts, shape, axis, extra, dtype, whole, name):
        edge = tuple(extra if i == axis else n for i, n in enumerate(shape))
        return call(
            functools.partial(kernel, plan),
            (chan_at, *parts),
            [SMEM] + [VMEM] * chans,
            [(shape, dtype), (edge, LOW)],
            [VMEM] * 2,
            [pltpu.VMEM(whole, LOW)],
            name,
        )

    def topped(main, tail, axis):
        first = lax.slice_in_dim(main, 0, tail.shape[axis], axis=axis) + tail.astype(main.dtype)
        return lax.dynamic_update_slice(main, first, (0, 0, 0))

    token = chain(send, "cab")
    token = chain(tied(token, gx_parts[-1]), "e")
    gx_parts[0] = tied(gx_parts[0], token)
    feature_grad, feature_tail = joined(
        join_features_kernel, gx_parts, features.shape, 2, EXTRA * 4 * width, FULL,
        (chans, 2, spots, 2 * chans_in), "join_features",
    )
    token = feature_tail
    feature_tail = to_next(feature_tail)
    token = chain(token, "be")
    block_parts[0] = tied(block_parts[0], token)
    block_out, block_tail = joined(
        join_rows_kernel, block_parts, out_grad.shape, 1, EXTRA * width, LOW,
        (chans, spots, chans_out), "join_rows",
    )
    token = block_tail
    block_tail = to_next(block_tail)
    token = chain(token, "aecb")
    feature_grad = topped(feature_grad, tied(feature_tail, token), 2)
    block_out = jnp.swapaxes(topped(block_out, tied(block_tail, token), 1), 1, 2)
    token = chain(token, "eabeaea")

    def mine(key):
        return sums_of[key].mine(sums_of[key].last[0])

    last = jnp.stack([mine(key) for key in "abce"]).astype(jnp.int32)
    (conv_mid_grad,) = call(
        mid_assembly_kernel,
        (last, *[part for key in "abc" for part in sums_of[key].halves(token)]),
        [SMEM] + [VMEM] * 6,
        [((3, 9 * chans_out, wide), FULL)],
        [HBM],
        [pltpu.VMEM((3, 9 * chans_out, wide), FULL), pltpu.SemaphoreType.DMA((3,))],
        "mid_assembly",
    )
    entry_own, entry_other = sums_of["e"].halves(token)
    conv_mid_grad = conv_mid_grad.reshape(3, 3, 3, chans_out, wide)
    conv_in_grad, proj_grad = call(
        entry_assembly_kernel,
        (last, entry_own, entry_other),
        [SMEM] + [VMEM] * 2,
        [((9 * chans_in, wide), FULL), ((chans_in, wide), FULL)],
        [HBM] * 2,
        [pltpu.VMEM((10 * chans_in, wide), FULL), pltpu.SemaphoreType.DMA((2,))],
        "entry_assembly",
    )
    conv_in_grad = conv_in_grad.reshape(3, 3, chans_in, wide)

    sums = jnp.stack(
        [back0[1], back12[1], back12[2], back3[1], back4[1]]
        + [back0[0], back12[0], back12[0], back3[0], back4[0]]
    )
    sums = sums + flipped(sums, "chan", splits)
    sums = lax.dynamic_slice_in_dim(sums, chan * chans_out, chans_out, 1)
    return (
        block_out, feature_grad, conv_in_grad, proj_grad, conv_mid_grad, sums[:5], sums[5:],
    )


def solution(mesh):
    placed = (
        P(None, "chan", "space"),
        P(),
        P(None, None, "chan", None),
        P("chan", None),
        P(None, None, None, "chan", None),
        P(None, "chan"),
        P(None, "chan"),
        P(None, "chan", "space"),
    )
    return jax.shard_map(
        shards,
        mesh=mesh,
        in_specs=placed,
        out_specs=(
            P(None, "chan", "space"),
            P(None, "chan", "space"),
            P(None, None, "chan", None),
            P("chan", None),
            P(None, None, None, "chan", None),
            P(None, "chan"),
            P(None, "chan"),
        ),
        check_vma=False,
    )
```

```python
import collections
import functools

import jax
import jax.numpy as jnp
import numpy as np
from jax import lax
from jax.experimental import pallas as pl
from jax.experimental.pallas import tpu as pltpu
from jax.sharding import PartitionSpec as P

MICRO = 2
WIN = 20
MOST_SIDE = 9
EXTRA = MOST_SIDE - 1
BLOCK = 16
ROW_BLOCK = 64
GAP = 8
EPS = 1e-05
SLACK_BYTES = 6 * 1024 * 1024
LOW = jnp.bfloat16
HIDERS = ("mid_forward_c", "mid_backward_c", "mid_backward_b", "mid_weight_b")
HIDERS += ("mid_backward_a", "mid_weight_a", "entry_backward", "entry_weight")
FULL = jnp.float32

PLAN_FIELDS = ["chans", "spaces", "splits", "rows_dev", "own_rows", "bases", "pitch", "width"]
PLAN_FIELDS += ["spots", "chans_in", "chans_out", "wide"]
Plan = collections.namedtuple("Plan", PLAN_FIELDS)

VMEM = pl.BlockSpec(memory_space=pltpu.VMEM)
SMEM = pl.BlockSpec(memory_space=pltpu.SMEM)
HBM = pl.BlockSpec(memory_space=pltpu.HBM)
ANY = pl.BlockSpec(memory_space=pl.ANY)


def flipped(value, axis, bit):
    count = lax.axis_size(axis)
    return lax.ppermute(value, axis, [(i, i ^ bit) for i in range(count)])


def from_next(value):
    count = lax.axis_size("space")
    return lax.ppermute(value, "space", [(i + 1, i) for i in range(count - 1)])


def to_next(value):
    count = lax.axis_size("space")
    return lax.ppermute(value, "space", [(i, i + 1) for i in range(count - 1)])


def exchanged(value, chan_bits, space_bits, plan):
    count = plan.chans * plan.spaces
    flip = chan_bits * plan.spaces + space_bits
    return lax.ppermute(value, ("chan", "space"), [(i, i ^ flip) for i in range(count)])


def tied(value, *others):
    return lax.optimization_barrier((value, others))[0]


def gathered(own, plan, then=()):
    parts = {0: own}
    for rel in range(1, plan.chans):
        bit = rel & -rel
        source = parts[rel ^ bit]
        if rel != bit and then:
            source = tied(source, *then)
        parts[rel] = flipped(source, "chan", bit)
    return [parts[rel] for rel in range(plan.chans)]


def swapped(parts, plan):
    return [parts[0]] + [flipped(parts[rel], "chan", rel) for rel in range(1, plan.chans)]


def micro_sums(value, plan, early=(), late=()):
    bits = []
    bit = 1
    while bit < plan.splits:
        bits.append((bit, 0))
        bit *= 2
    bit = 1
    while bit < plan.spaces:
        bits.append((0, bit))
        bit *= 2
    for i in range(0, len(bits), 2):
        pair = bits[i : i + 2]
        start = value
        one = exchanged(value, *pair[0], plan)
        if len(pair) == 2:
            two = exchanged(value, *pair[1], plan)
            both = exchanged(value, pair[0][0] ^ pair[1][0], pair[0][1] ^ pair[1][1], plan)
        done = []
        if i == 0:
            done = [job(one, [two, both] if len(pair) == 2 else []) for job in early]
        elif i == 2:
            done = [job(one if takes == "one" else start) for takes, job in late]
        done = [token for token in jax.tree.leaves(done) if token is not None]
        if done:
            one = tied(one, *done)
        value = value + one
        if len(pair) == 2:
            value = value + (two + both)
    return value


class WeightSum:
    def __init__(self, keep, send, plan, order):
        self.send, self.plan = send, plan
        self.kept = keep
        self.received = [] if send is None else [flipped(send, "chan", 1)]
        self.steps = []
        named = [bit for step in order if step != "c" for bit in step]
        rest = [k for k in range(plan.spaces.bit_length() - 1) if k not in named]
        for step in list(order) + [(k,) for k in rest]:
            if step == "c":
                self.steps += [("chan", (1 << k,)) for k in range(1, plan.chans.bit_length() - 1)]
            else:
                self.steps.append(("space", tuple(1 << k for k in step)))
        self.steps[-1] = ("swap", self.steps[-1][1])
        self.gathers = [bits for axis, bits in self.steps if axis == "space"][::-1]
        self.last = self.gathers[-1]
        self.gathering = False

    def mine(self, bit):
        return (lax.axis_index("space") // bit) % 2

    def added(self, pick):
        total = pick(self.kept).astype(FULL)
        for part in self.received:
            total = total + pick(part).astype(FULL)
        return total.astype(LOW)

    def flips(self, bits):
        ways = []
        for number in range(1, 1 << len(bits)):
            held = [(number >> i) & 1 for i in range(len(bits))]
            ways.append((sum(bit for bit, on in zip(bits, held) if on), held))
        return ways

    def take(self, *after):
        if after and self.received:
            self.received[0] = tied(self.received[0], *after)
        elif after:
            self.kept = tied(self.kept, *after)

    def advance(self, *after):
        self.take(*after)
        if self.steps:
            axis, bits = self.steps.pop(0)
            if axis == "swap":
                kept = self.added(lambda part: part)
                sent = [(bits[0], kept)]
                axis = "space"
            elif axis == "chan":
                kept = self.added(lambda part: part[0::2])
                sent = [(bits[0], self.added(lambda part: part[1::2]))]
            else:
                size = self.kept.shape[1] >> len(bits)

                def piece(held):
                    at = 0
                    for bit, on in zip(bits[::-1], held[::-1]):
                        at = 2 * at + (self.mine(bit) if not on else 1 - self.mine(bit))
                    return self.added(lambda part: lax.dynamic_slice_in_dim(part, at * size, size, 1))

                kept = piece([0] * len(bits))
                sent = [(flip, piece(held)) for flip, held in self.flips(bits)]
            self.kept = kept
            self.received = [flipped(part, axis, flip) for flip, part in sent]
            return sent[0][1]
        bits = self.gathers.pop(0)
        whole = self.ordered() if self.gathering else self.added(lambda part: part)
        self.gathering = bits
        self.kept = whole
        self.received = [flipped(whole, "space", flip) for flip, _ in self.flips(bits)]
        return whole

    def ordered(self):
        parts = [self.kept] + self.received
        for bit in self.gathering:
            turned = self.mine(bit) == 0
            joined = []
            for i in range(0, len(parts), 2):
                low = jnp.concatenate(parts[i : i + 2], axis=1)
                high = jnp.concatenate(parts[i : i + 2][::-1], axis=1)
                joined.append(jnp.where(turned, low, high))
            parts = joined
        return parts[0]

    def halves(self, *after):
        while self.steps or self.gathers:
            self.advance(*after)
        self.take(*after)
        return self.kept[0], self.received[0][0]


def tiles(count, size):
    return [slice(i, i + size) for i in range(0, count, size)]


def logistic(u):
    return 1.0 / (1.0 + jnp.exp(-u))


def slope(u):
    g = logistic(u)
    return g * (1.0 + u * (1.0 - g))


def moments(stat, inv_count):
    mean = stat[0:1, :] * inv_count
    inverse = lax.rsqrt(stat[1:2, :] * inv_count - mean * mean + EPS)
    return mean, inverse


def dot(a, b):
    return lax.dot_general(a, b, (((1,), (0,)), ((), ())), preferred_element_type=FULL)


def dot_t(a, b):
    return lax.dot_general(a, b, (((1,), (1,)), ((), ())), preferred_element_type=FULL)


def unit(count):
    rows = lax.broadcasted_iota(jnp.int32, (count, count), 0)
    columns = lax.broadcasted_iota(jnp.int32, (count, count), 1)
    return jnp.where(rows == columns, 1.0, 0.0).astype(LOW)


def clear_gaps(ref, spots):
    zero = jnp.zeros((GAP, ref.shape[-1]), ref.dtype)
    ref[pl.ds(0, GAP), :] = zero
    ref[pl.ds(GAP + spots, GAP), :] = zero


def column_sum(x):
    return jnp.sum(x, axis=0, keepdims=True)


def start_shards(chan, shard_refs, w_ref, sems):
    size = shard_refs[0].shape[2]
    copies = []
    for rel, ref in enumerate(shard_refs):
        place = pl.ds(pl.multiple_of((chan ^ rel) * size, size), size)
        copy = pltpu.make_async_copy(ref, w_ref.at[:, :, place, :], sems.at[rel])
        copy.start()
        copies.append(copy)
    return copies


def matmul_tile(plan):
    for size in (288, 192, 144, 96, 64):
        if plan.spots % size == 0:
            return size
    return plan.spots


def vector_tile(plan):
    return 2 * plan.pitch // 4 if plan.pitch % 32 == 0 else plan.pitch


def feature_pick(plan, side, first, count):
    shape = (2 * MOST_SIDE * BLOCK, count)
    place = lax.broadcasted_iota(jnp.int32, shape, 0)
    cell = lax.broadcasted_iota(jnp.int32, shape, 1) + first
    row, column = place & (BLOCK - 1), place >> (BLOCK.bit_length() - 1)
    phase = jnp.where(column >= MOST_SIDE, 1, 0)
    column = column - MOST_SIDE * phase
    source = (2 * row + phase) * (2 * plan.width) + 2 * column + side
    return jnp.where(source == cell, 1.0, 0.0).astype(LOW)


def row_pick(plan, first, count, turned=False):
    spots = MOST_SIDE * ROW_BLOCK
    shape = (count, spots) if turned else (spots, count)
    place = lax.broadcasted_iota(jnp.int32, shape, 1 if turned else 0)
    cell = lax.broadcasted_iota(jnp.int32, shape, 0 if turned else 1) + first
    row, column = place & (ROW_BLOCK - 1), place >> (ROW_BLOCK.bit_length() - 1)
    return jnp.where(row * plan.width + column == cell, 1.0, 0.0).astype(LOW)


def spread_features_kernel(plan, chan_ref, x_ref, halo_ref, out_ref):
    chan = chan_ref[0]
    size, lanes = plan.chans_in, BLOCK * 4 * plan.width
    columns = MOST_SIDE

    def stacked(part):
        blank = jnp.zeros_like(part[0])
        even, odd = [], []
        for m in range(MICRO):
            even += [part[m], blank]
            odd += [blank, part[m]]
        return jnp.concatenate(even, 0), jnp.concatenate(odd, 0)

    have = x_ref.shape[2]
    own, extra = have % lanes, halo_ref.shape[2]
    picks = [feature_pick(plan, side, 0, lanes) for side in range(2)]
    left = [feature_pick(plan, side, 0, own) for side in range(2)]
    right = [feature_pick(plan, side, own, extra) for side in range(2)]
    for j in range(-(-(plan.rows_dev + EXTRA) // BLOCK)):
        start = j * lanes
        if start + lanes <= have:
            even, odd = stacked([x_ref[m, :, start : start + lanes] for m in range(MICRO)])
            result = dot_t(picks[0], even) + dot_t(picks[1], odd)
        else:
            even, odd = stacked([x_ref[m, :, start:have] for m in range(MICRO)])
            result = dot_t(left[0], even) + dot_t(left[1], odd)
            even, odd = stacked([halo_ref[m] for m in range(MICRO)])
            result += dot_t(right[0], even) + dot_t(right[1], odd)
        result = result.astype(LOW)
        for split, base in enumerate(plan.bases):
            row = j * BLOCK - base
            if row < 0 or row >= plan.pitch:
                continue
            for m in range(MICRO):
                to = chan ^ (m * plan.splits + split)
                for phase in range(2):
                    for c in range(columns):
                        at = (phase * columns + c) * BLOCK
                        part = result[at : at + BLOCK, m * 2 * size : (m + 1) * 2 * size]
                        spot = c * plan.pitch + row
                        out_ref[to, phase, spot : spot + BLOCK] = part


def spread_rows_kernel(plan, chan_ref, x_ref, halo_ref, out_ref):
    chan = chan_ref[0]
    size, spots = plan.chans_out, ROW_BLOCK * plan.width
    have = x_ref.shape[1]
    own, extra = have % spots, halo_ref.shape[1]
    pick, left = row_pick(plan, 0, spots), row_pick(plan, 0, own)
    right = row_pick(plan, own, extra)
    for j in range(-(-(plan.rows_dev + EXTRA) // ROW_BLOCK)):
        start = j * spots
        for m in range(MICRO):
            if start + spots <= have:
                result = dot(pick, x_ref[m, start : start + spots])
            else:
                result = dot(left, x_ref[m, start:have]) + dot(right, halo_ref[m])
            result = result.astype(LOW)
            for split, base in enumerate(plan.bases):
                low, high = max(j * ROW_BLOCK, base), min((j + 1) * ROW_BLOCK, base + plan.pitch)
                if low >= high:
                    continue
                to = chan ^ (m * plan.splits + split)
                for c in range(MOST_SIDE):
                    at = c * ROW_BLOCK + low - j * ROW_BLOCK
                    spot = c * plan.pitch + low - base
                    out_ref[to, spot : spot + high - low] = result[at : at + high - low]


def laid_rows(plan, whole_ref, m, c, low, high, phase=None):
    pieces = []
    for row in range(low, high, BLOCK):
        total = None
        for split, base in enumerate(plan.bases):
            if not base <= row < base + plan.pitch:
                continue
            spots = pl.ds(c * plan.pitch + row - base, BLOCK)
            at = m * plan.splits + split
            part = whole_ref[at, spots] if phase is None else whole_ref[at, phase, spots]
            total = part if total is None else total + part
        pieces.append(total)
    return pieces


def join_rows_kernel(plan, chan_ref, *refs):
    parts = refs[: plan.chans]
    out_ref, tail_ref, whole_ref = refs[plan.chans :]
    chan = chan_ref[0]
    for rel in range(plan.chans):
        whole_ref[chan ^ rel] = parts[rel][...]
    spots = ROW_BLOCK * plan.width
    have = out_ref.shape[1]
    own, extra = have % spots, tail_ref.shape[1]
    pick, left = row_pick(plan, 0, spots, True), row_pick(plan, 0, own, True)
    right = row_pick(plan, own, extra, True)
    limit = plan.rows_dev + EXTRA
    for j in range(-(-limit // ROW_BLOCK)):
        start = j * spots
        low, high = j * ROW_BLOCK, min((j + 1) * ROW_BLOCK, limit)
        for m in range(MICRO):
            pieces = []
            for c in range(MOST_SIDE):
                pieces += laid_rows(plan, whole_ref, m, c, low, high)
                if high - low < ROW_BLOCK:
                    blank = (ROW_BLOCK - high + low, plan.chans_out)
                    pieces.append(jnp.zeros(blank, LOW))
            rows = jnp.concatenate(pieces, 0)
            if start + spots <= have:
                out_ref[m, start : start + spots] = dot(pick, rows).astype(LOW)
            else:
                out_ref[m, start:have] = dot(left, rows).astype(LOW)
                tail_ref[m] = dot(right, rows).astype(LOW)


def join_features_kernel(plan, chan_ref, *refs):
    parts = refs[: plan.chans]
    out_ref, tail_ref, whole_ref = refs[plan.chans :]
    chan = chan_ref[0]
    for rel in range(plan.chans):
        whole_ref[chan ^ rel] = parts[rel][...]
    size = plan.chans_in
    one = unit(2 * size)
    lanes = BLOCK * 4 * plan.width
    have = out_ref.shape[2]
    own, extra = have % lanes, tail_ref.shape[2]
    picks = [feature_pick(plan, side, 0, lanes) for side in range(2)]
    left = [feature_pick(plan, side, 0, own) for side in range(2)]
    right = [feature_pick(plan, side, own, extra) for side in range(2)]
    for j in range(-(-(plan.rows_dev + EXTRA) // BLOCK)):
        start = j * lanes
        first, second = [], []
        for m in range(MICRO):
            pieces = []
            for phase in range(2):
                for c in range(MOST_SIDE):
                    row = j * BLOCK
                    pieces += laid_rows(plan, whole_ref, m, c, row, row + BLOCK, phase)
            turned = dot_t(one, jnp.concatenate(pieces, 0)).astype(LOW)
            first.append(turned[:size])
            second.append(turned[size:])
        first, second = jnp.concatenate(first, 0), jnp.concatenate(second, 0)
        if start + lanes <= have:
            result = dot(first, picks[0]) + dot(second, picks[1])
            for m in range(MICRO):
                out_ref[m, :, start : start + lanes] = result[m * size : (m + 1) * size]
        else:
            result = dot(first, left[0]) + dot(second, left[1])
            tail = dot(first, right[0]) + dot(second, right[1])
            for m in range(MICRO):
                out_ref[m, :, start:have] = result[m * size : (m + 1) * size]
                tail_ref[m] = tail[m * size : (m + 1) * size].astype(LOW)


def entry_copies(plan, shard_refs, w_ref, wp_ref, sems):
    copies = []
    for rel in range(plan.chans):
        for a in range(3):
            sem = sems.at[7 * rel + 2 * a]
            source = shard_refs[rel].at[pl.ds(3 * a + 1, 2)]
            copies.append(pltpu.make_async_copy(source, w_ref.at[a, 0, rel], sem))
            sem = sems.at[7 * rel + 2 * a + 1]
            source = shard_refs[rel].at[3 * a]
            copies.append(pltpu.make_async_copy(source, w_ref.at[a, 1, rel, 1], sem))
        source = shard_refs[rel].at[9]
        copies.append(pltpu.make_async_copy(source, wp_ref.at[rel, 0], sems.at[7 * rel + 6]))
    for copy in copies:
        copy.start()
    for rel in range(plan.chans):
        blank = jnp.zeros(wp_ref.shape[2:], LOW)
        wp_ref[rel, 1] = blank
        for a in range(3):
            w_ref[a, 1, rel, 0] = blank
    return copies


def entry_forward_kernel(plan, marks_ref, *refs):
    n = plan.chans
    x_refs, shard_refs = refs[:n], refs[n : 2 * n]
    e_ref, p_ref, stat_ref, xm_ref = refs[2 * n : 2 * n + 4]
    x_ref, w_ref, wp_ref, xs_ref, am_ref, sems, x_sems = refs[2 * n + 4 :]
    x_copies = []
    for rel in range(n):
        x_copies.append(pltpu.make_async_copy(x_refs[rel], x_ref.at[rel], x_sems.at[rel]))
        x_copies[-1].start()
    copies = entry_copies(plan, shard_refs, w_ref, wp_ref, sems)
    size = 2 * plan.chans_in
    deep = n * size
    pitch = plan.pitch
    for k in range(3):
        am_ref[k, 0:pitch] = jnp.zeros((pitch, deep), LOW)
    clear_gaps(xs_ref, plan.spots)
    for rel in range(n):
        x_copies[rel].wait()
        lanes = slice(rel * size, (rel + 1) * size)
        for t in tiles(plan.spots, vector_tile(plan)):
            own = marks_ref[t, 0:1]
            for row in range(2):
                value = x_ref[rel, row, t].astype(FULL) * own
                low = value.astype(LOW)
                xm_ref[row, t, lanes] = low
                am_ref[row, pitch + t.start : pitch + t.stop, lanes] = low
                if row == 1:
                    xs_ref[GAP + t.start : GAP + t.stop, lanes] = value
    for t in tiles(plan.spots, vector_tile(plan)):
        above = xs_ref[GAP + t.start - 1 : GAP + t.stop - 1] * marks_ref[t, 1:2]
        am_ref[2, pitch + t.start : pitch + t.stop] = above.astype(LOW)
    for copy in copies:
        copy.wait()
    weights = w_ref[...].reshape(6 * deep, plan.wide)
    proj = wp_ref[...].reshape(deep, plan.wide)
    sums = [0.0] * 4
    for t in tiles(plan.spots, matmul_tile(plan)):
        own = marks_ref[t, 0:1]
        pieces = []
        for k in (2, 0, 1):
            pieces.append(am_ref[k, pitch + t.start : pitch + t.stop])
            pieces.append(am_ref[k, t])
        z = dot(jnp.concatenate(pieces, 1), weights)
        e_ref[t] = z.astype(LOW)
        p = dot(pieces[2], proj)
        p_ref[t] = p.astype(LOW)
        zm, pm = z * own, p * own
        for i, term in enumerate((zm, zm * z, pm, pm * p)):
            sums[i] = sums[i] + column_sum(term)
    stat_ref[...] = jnp.concatenate(sums, 0)


def mid_forward_kernel(plan, layers, chan_ref, inv_ref, marks_ref, par_ref, *refs):
    k = len(layers)
    n = plan.chans
    z_refs, stat_refs, shard_refs = refs[:k], refs[k : 2 * k], refs[2 * k : 2 * k + n]
    outs = refs[2 * k + n :]
    if k == 2:
        z_ref, out_stat_ref, a_ref, h_ref, w_ref, xs_ref, xa_ref, sems = outs
    else:
        z_ref, out_stat_ref, a_ref, w_ref, xs_ref, xa_ref, sems = outs
        h_ref = None
    copies = start_shards(chan_ref[0], shard_refs, w_ref, sems)
    inv = inv_ref[0]
    norms = [moments(stat[...], inv) for stat in stat_refs]
    wide, pitch = plan.wide, plan.pitch
    clear_gaps(xs_ref, plan.spots)
    for i in range(3):
        blank = jnp.zeros((pitch, wide), LOW)
        xa_ref[i, 0:pitch] = blank
        xa_ref[i, pitch + plan.spots : 2 * pitch + plan.spots] = blank
    for t in tiles(plan.spots, vector_tile(plan)):
        own = marks_ref[t, 0:1]
        u = 0.0
        for (mean, inverse), src, j in zip(norms, z_refs, layers):
            u = u + (par_ref[j : j + 1] * ((src[t].astype(FULL) - mean) * inverse) + par_ref[5 + j : 6 + j])
        u = u * own
        a = u * logistic(u)
        if h_ref is not None:
            h_ref[t] = a.astype(LOW)
        xs_ref[GAP + t.start : GAP + t.stop] = a
        low = a.astype(LOW)
        a_ref[t] = low
        xa_ref[1, pitch + t.start : pitch + t.stop] = low
    for t in tiles(plan.spots, vector_tile(plan)):
        for i, step in ((0, -1), (2, 1)):
            part = xs_ref[GAP + t.start + step : GAP + t.stop + step]
            part = part * marks_ref[t, 1 + i // 2 : 2 + i // 2]
            xa_ref[i, pitch + t.start : pitch + t.stop] = part.astype(LOW)
    for copy in copies:
        copy.wait()
    weights = w_ref[...].reshape(9 * wide, wide)
    total, square = 0.0, 0.0
    for t in tiles(plan.spots, matmul_tile(plan)):
        own = marks_ref[t, 0:1]
        pieces = []
        for a in range(3):
            for b in range(3):
                pieces.append(xa_ref[a, t.start + b * pitch : t.stop + b * pitch])
        z = dot(jnp.concatenate(pieces, 1), weights)
        z_ref[t] = z.astype(LOW)
        zm = z * own
        total = total + column_sum(zm)
        square = square + column_sum(zm * z)
    out_stat_ref[...] = jnp.concatenate([total, square], 0)


def head_kernel(plan, chan_ref, inv_ref, marks_ref, par_ref, z_ref, stat_ref, h_ref, *refs):
    n = plan.chans
    og_refs = refs[:n]
    out_ref, g_ref, out_stat_ref, og_ref = refs[n:]
    chan = chan_ref[0]
    for rel in range(n):
        og_ref[chan ^ rel] = og_refs[rel][...]
    mean, inverse = moments(stat_ref[...], inv_ref[0])
    size = plan.chans_out
    for j in range(n):
        lanes = slice(j * size, (j + 1) * size)
        total, dotted = 0.0, 0.0
        for t in tiles(plan.spots, plan.pitch):
            own = marks_ref[t, 0:1]
            hat = (z_ref[t, lanes].astype(FULL) - mean[:, lanes]) * inverse[:, lanes]
            u = own * (par_ref[4:5, lanes] * hat + par_ref[9:10, lanes]) + h_ref[t, lanes].astype(FULL)
            s = logistic(u)
            out_ref[chan ^ j, t] = (u * s).astype(LOW)
            q = og_ref[j, t].astype(FULL) * (s * (1.0 + u * (1.0 - s))) * own
            g_ref[t, lanes] = q.astype(LOW)
            total = total + column_sum(q)
            dotted = dotted + column_sum(q * hat)
        out_stat_ref[0:1, lanes] = total
        out_stat_ref[1:2, lanes] = dotted


def norm_back(own, q, z, norm, gain, total, dotted, inv):
    mean, inverse = norm
    hat = (z - mean) * inverse
    return own * (gain * inverse) * (q - total * inv - hat * (dotted * inv))


def mid_backward_kernel(plan, j, kind, chan_ref, inv_ref, marks_ref, par_ref, *refs):
    n = plan.chans
    g_ref, z_ref, stat_ref, back_ref = refs[:4]
    shard_refs = refs[4 : 4 + n]
    refs = refs[4 + n :]
    add_ref = short_z_ref = None
    if kind == "join":
        src_refs, src_stats, add_ref = refs[:2], refs[2:4], refs[4]
        refs = refs[5:]
        layers = (1, 2)
    elif kind == "entry":
        src_refs, src_stats, short_z_ref, short_stat_ref = refs[:1], refs[1:2], refs[2], refs[3]
        refs = refs[4:]
        layers = (0,)
    else:
        src_refs, src_stats = refs[:1], refs[1:2]
        refs = refs[2:]
        layers = (3,)
    ga_ref, next_ref, out_stat_ref = refs[:3]
    refs = refs[3:]
    if kind == "entry":
        short_ref, refs = refs[0], refs[1:]
    w_ref, s0_ref, s2_ref, sems = refs
    copies = start_shards(chan_ref[0], shard_refs, w_ref, sems)
    inv = inv_ref[0]
    wide, pitch = plan.wide, plan.pitch
    norm = moments(stat_ref[...], inv)
    total, dotted = back_ref[0:1], back_ref[1:2]
    for ref in (s0_ref, s2_ref):
        clear_gaps(ref, plan.spots)
    for i in range(3):
        blank = jnp.zeros((pitch, wide), LOW)
        ga_ref[i, 0:pitch] = blank
        ga_ref[i, pitch + plan.spots : 2 * pitch + plan.spots] = blank
    if kind == "entry":
        short_norm = moments(short_stat_ref[...], inv)
    for t in tiles(plan.spots, vector_tile(plan)):
        own, upper, lower = (marks_ref[t, i : i + 1] for i in range(3))
        g = g_ref[t].astype(FULL)
        z = z_ref[t].astype(FULL)
        gz = norm_back(own, g, z, norm, par_ref[j : j + 1], total, dotted, inv)
        low = gz.astype(LOW)
        gz = low.astype(FULL)
        ga_ref[1, pitch + t.start : pitch + t.stop] = low
        s0_ref[GAP + t.start : GAP + t.stop] = gz * upper
        s2_ref[GAP + t.start : GAP + t.stop] = gz * lower
        if kind == "entry":
            back = norm_back(
                own, g, short_z_ref[t].astype(FULL), short_norm, par_ref[2:3], total,
                back_ref[2:3], inv,
            )
            short_ref[t] = back.astype(LOW)
    for t in tiles(plan.spots, vector_tile(plan)):
        first, last = GAP + t.start, GAP + t.stop
        to = slice(pitch + t.start, pitch + t.stop)
        ga_ref[0, to] = s0_ref[first + 1 : last + 1].astype(LOW)
        ga_ref[2, to] = s2_ref[first - 1 : last - 1].astype(LOW)
    for copy in copies:
        copy.wait()
    norms = [moments(stat[...], inv) for stat in src_stats]
    sums = [0.0] * (1 + len(layers))
    weights = jnp.concatenate([w_ref[a, b] for a in range(3) for b in range(3)], 1)
    for t in tiles(plan.spots, matmul_tile(plan)):
        own = marks_ref[t, 0:1]
        pieces = []
        for a in range(3):
            for b in range(3):
                back = (2 - b) * pitch
                pieces.append(ga_ref[a, t.start + back : t.stop + back])
        gx = dot_t(jnp.concatenate(pieces, 1), weights)
        u = 0.0
        hats = []
        for (mean, inverse), src, i in zip(norms, src_refs, layers):
            hat = (src[t].astype(FULL) - mean) * inverse
            hats.append(hat)
            u = u + (par_ref[i : i + 1] * hat + par_ref[5 + i : 6 + i])
        u = u * own
        if add_ref is not None:
            gx = gx + add_ref[t].astype(FULL)
        q = gx * slope(u) * own
        next_ref[t] = q.astype(LOW)
        sums[0] = sums[0] + column_sum(q)
        for i, hat in enumerate(hats):
            sums[1 + i] = sums[1 + i] + column_sum(q * hat)
    out_stat_ref[...] = jnp.concatenate(sums, 0)


def entry_norm_kernel(plan, inv_ref, marks_ref, par_ref, g_ref, e_ref, stat_ref, back_ref, gm_ref, s_ref):
    inv = inv_ref[0]
    norm = moments(stat_ref[...], inv)
    clear_gaps(s_ref, plan.spots)
    for k in range(2):
        gm_ref[k, plan.spots : plan.spots + plan.pitch] = jnp.zeros((plan.pitch, plan.wide), LOW)
    for t in tiles(plan.spots, vector_tile(plan)):
        own, upper = marks_ref[t, 0:1], marks_ref[t, 1:2]
        gz = norm_back(
            own, g_ref[t].astype(FULL), e_ref[t].astype(FULL), norm, par_ref[0:1], back_ref[0:1],
            back_ref[1:2], inv,
        )
        low = gz.astype(LOW)
        gm_ref[0, t] = low
        s_ref[GAP + t.start : GAP + t.stop] = low.astype(FULL) * upper
    for t in tiles(plan.spots, vector_tile(plan)):
        gm_ref[1, t] = s_ref[GAP + t.start + 1 : GAP + t.stop + 1].astype(LOW)


def entry_backward_kernel(plan, marks_ref, gm_ref, short_ref, *refs):
    n = plan.chans
    shard_refs = refs[:n]
    gx_ref, w_ref, wp_ref, sems = refs[n:]
    for copy in entry_copies(plan, shard_refs, w_ref, wp_ref, sems):
        copy.wait()
    size = 2 * plan.chans_in
    deep = n * size
    pitch, wide = plan.pitch, plan.wide

    def part(a, side):
        return w_ref[a, side].reshape(deep, wide)

    top_weights = [part(1, 0), part(1, 1), wp_ref[...].reshape(deep, wide)]
    top_weights = jnp.concatenate(top_weights, 1)
    low_weights = jnp.concatenate([part(2, 0), part(2, 1), part(0, 0), part(0, 1)], 1)
    for t in tiles(plan.spots, matmul_tile(plan)):
        own = marks_ref[t, 0:1]
        right = slice(t.start + pitch, t.stop + pitch)
        here = [gm_ref[0, t], gm_ref[0, right]]
        top = dot_t(jnp.concatenate(here + [short_ref[t]], 1), top_weights)
        here += [gm_ref[1, t], gm_ref[1, right]]
        low = dot_t(jnp.concatenate(here, 1), low_weights)
        for row, value in enumerate((top, low)):
            value = (value * own).astype(LOW)
            for rel in range(n):
                gx_ref[rel, row, t] = value[:, rel * size : (rel + 1) * size]


def mid_weight_kernel(plan, chan_ref, a_ref, ga_ref, keep_ref, send_ref, turned_ref, at_ref):
    wide, pitch = plan.wide, plan.pitch
    turned_ref[...] = dot_t(unit(wide), a_ref[...]).astype(LOW)
    chan = chan_ref[0]
    size = plan.chans_out
    for rel in range(plan.chans):
        place = pl.ds(pl.multiple_of((chan ^ rel) * size, size), size)
        at_ref[rel * size : (rel + 1) * size] = turned_ref[place]
    for a in range(3):
        for b in range(3):
            back = (2 - b) * pitch
            rows = slice((3 * a + b) * size, (3 * a + b + 1) * size)
            part = dot(at_ref[...], ga_ref[a, back : back + plan.spots]).astype(LOW)
            for rel in range(plan.chans):
                target = send_ref if rel & 1 else keep_ref
                target[rel // 2, rows] = part[rel * size : (rel + 1) * size]


def entry_weight_kernel(plan, xm_ref, gm_ref, short_ref, keep_ref, send_ref, xt_ref):
    n, size, wide, pitch = plan.chans, plan.chans_in, plan.wide, plan.pitch
    whole = unit(n * 2 * size)
    for row in range(2):
        xt_ref[row] = dot_t(whole, xm_ref[row]).astype(LOW)

    def put(tap, rel, value):
        target = send_ref if rel & 1 else keep_ref
        target[rel // 2, tap * size : (tap + 1) * size] = value

    def product(row, right):
        return dot(xt_ref[row], right).astype(LOW)

    for row, grad, a in ((0, 0, 1), (1, 0, 2), (1, 1, 0)):
        big = product(row, gm_ref[grad, 0 : plan.spots])
        side = product(row, gm_ref[grad, pitch : pitch + plan.spots])
        for rel in range(n):
            at = 2 * rel * size
            put(3 * a + 1, rel, big[at : at + size])
            put(3 * a + 2, rel, big[at + size : at + 2 * size])
            put(3 * a, rel, side[at + size : at + 2 * size])
    proj = product(0, short_ref[...])
    for rel in range(n):
        put(9, rel, proj[2 * rel * size : (2 * rel + 1) * size])


def mid_assembly_kernel(mine_ref, *refs):
    out_ref, hold_ref, sems = refs[6:]
    half = refs[0].shape[0]
    copies = []
    for layer in range(3):
        mine = mine_ref[layer]
        for i, part in enumerate(refs[2 * layer : 2 * layer + 2]):
            at = mine if i == 0 else 1 - mine
            rows = pl.ds(pl.multiple_of(at * half, 8), half)
            hold_ref[layer, rows] = part[...].astype(FULL)
        copies.append(pltpu.make_async_copy(hold_ref.at[layer], out_ref.at[layer], sems.at[layer]))
        copies[-1].start()
    for copy in copies:
        copy.wait()


def entry_assembly_kernel(mine_ref, own_ref, other_ref, conv_ref, proj_ref, hold_ref, sems):
    half = own_ref.shape[0]
    for i, part in enumerate((own_ref, other_ref)):
        at = mine_ref[3] if i == 0 else 1 - mine_ref[3]
        hold_ref[pl.ds(pl.multiple_of(at * half, 8), half)] = part[...].astype(FULL)
    cut = conv_ref.shape[0]
    copies = [
        pltpu.make_async_copy(hold_ref.at[pl.ds(0, cut)], conv_ref, sems.at[0]),
        pltpu.make_async_copy(hold_ref.at[pl.ds(cut, proj_ref.shape[0])], proj_ref, sems.at[1]),
    ]
    for copy in copies:
        copy.start()
    for copy in copies:
        copy.wait()


def call(kernel, operands, specs, outs, out_specs, scratch, name, flops=0):
    bytes_moved = sum(int(np.prod(o.shape)) * o.dtype.itemsize for o in operands)
    bytes_moved += sum(int(np.prod(s)) * jnp.dtype(d).itemsize for s, d in outs)
    bytes_moved = 1 if name in HIDERS else bytes_moved
    shapes = [jax.ShapeDtypeStruct(s, d) for s, d in outs]
    held = SLACK_BYTES
    for one in scratch:
        if one.memory_space == pltpu.VMEM:
            held += int(np.prod(one.shape)) * jnp.dtype(one.dtype).itemsize
    return pl.pallas_call(
        kernel,
        out_shape=shapes,
        in_specs=specs,
        out_specs=out_specs,
        scratch_shapes=scratch,
        compiler_params=pltpu.CompilerParams(vmem_limit_bytes=held),
        cost_estimate=pl.CostEstimate(
            flops=int(flops), bytes_accessed=int(bytes_moved), transcendentals=0
        ),
        name=name,
    )(*operands)


def marks_of(plan, sizes, top, first):
    sides = sizes // 2
    starts = jnp.cumsum(sides) - sides
    here = top + jnp.arange(plan.pitch, dtype=jnp.int32)
    inside = (
        (here[:, None] >= starts[None, :]) & (here[:, None] < (starts + sides)[None, :])
    ).astype(jnp.int32)
    begins = jnp.sum(inside * starts[None, :], axis=1)
    widths = jnp.sum(inside * sides[None, :], axis=1)
    local = here - begins
    owned = (widths > 0) & (begins >= first) & (begins < first + plan.own_rows)
    columns = jnp.arange(MOST_SIDE, dtype=jnp.int32)
    own = owned[None, :] & (columns[:, None] < widths[None, :])
    upper = jnp.broadcast_to((owned & (local > 0))[None, :], own.shape)
    lower = jnp.broadcast_to((owned & (local < widths - 1))[None, :], own.shape)
    marks = jnp.stack([own, upper, lower] + [jnp.zeros_like(own)] * 5, axis=-1)
    total = jnp.sum((sides * sides).astype(FULL))
    return marks.astype(FULL).reshape(plan.spots, 8), (1.0 / total).reshape(1)


def shards(features, image_sizes, conv_in_w, proj_w, conv_mid_w, norm_gain, norm_bias, out_grad):
    chans, spaces = lax.axis_size("chan"), lax.axis_size("space")
    splits = chans // MICRO
    width = WIN // 2
    rows_dev = features.shape[2] // (4 * width)
    own_rows = rows_dev // splits
    bases = tuple(split * own_rows // BLOCK * BLOCK for split in range(splits))
    need = max(split * own_rows - bases[split] for split in range(splits)) + own_rows + EXTRA
    pitch = -(-need // BLOCK) * BLOCK
    reach = -(-(rows_dev + EXTRA) // BLOCK) * BLOCK
    assert max(bases) + pitch <= reach and rows_dev + EXTRA == reach
    chans_in, chans_out = features.shape[1], norm_gain.shape[1]
    spots = MOST_SIDE * pitch
    plan = Plan(
        chans, spaces, splits, rows_dev, own_rows, bases, pitch, width, spots,
        chans_in, chans_out, chans * chans_out,
    )
    wide = plan.wide
    chan = lax.axis_index("chan")
    micro, split = chan // splits, chan % splits
    here = lax.axis_index("space") * rows_dev
    first = here + split * own_rows
    chan_at = chan.astype(jnp.int32).reshape(1)

    edge = features[:, :, : EXTRA * 4 * width]
    halo = from_next(edge)
    out_grad = jnp.swapaxes(out_grad, 1, 2)
    out_halo = from_next(out_grad[:, : EXTRA * width])
    (spread,) = call(
        functools.partial(spread_features_kernel, plan),
        (chan_at, features, tied(halo, out_halo)),
        [SMEM] + [VMEM] * 2,
        [((chans, 2, spots, 2 * chans_in), LOW)],
        [VMEM],
        [],
        "spread_features",
    )
    x_parts = swapped(spread, plan)
    slots = jnp.concatenate([norm_gain, norm_bias], axis=0)
    slots = lax.dynamic_update_slice(
        jnp.zeros((10, wide), FULL), slots, (jnp.int32(0), chan * chans_out)
    )
    bit = 1
    while bit < chans:
        slots = slots + flipped(slots, "chan", bit)
        bit *= 2
    pars = slots
    sizes = lax.dynamic_index_in_dim(image_sizes, micro, 0, keepdims=False)
    bases_at = jnp.asarray(bases, jnp.int32)[split]
    marks, inv = marks_of(plan, sizes, here + bases_at, first)

    (grad_spread,) = call(
        functools.partial(spread_rows_kernel, plan),
        (chan_at, out_grad, tied(out_halo, x_parts[1])),
        [SMEM] + [VMEM] * 2,
        [((chans, spots, chans_out), LOW)],
        [VMEM],
        [],
        "spread_rows",
    )

    entry_own = jnp.concatenate([conv_in_w.reshape(9, chans_in, wide), proj_w[None]], axis=0)
    entry_own = tied(entry_own, edge)
    entry_shards = gathered(entry_own, plan, (*x_parts[chans // 2 :], pars, grad_spread))
    mid_first = tied(conv_mid_w[0], *x_parts[chans // 2 :])

    conv_flops = 2 * spots * 9 * wide * wide
    field = ((spots, wide), LOW)
    deep = chans * 2 * chans_in
    entry_scratch = [
        pltpu.VMEM((3, 2, chans, 2, chans_in, wide), LOW),
        pltpu.VMEM((chans, 2, chans_in, wide), LOW),
    ]
    padded = pltpu.VMEM((spots + 2 * GAP, wide), FULL)
    z0, zp, stats, xm = call(
        functools.partial(entry_forward_kernel, plan),
        (marks, *x_parts, *entry_shards),
        [VMEM] + [ANY] * (2 * chans),
        [field, field, ((4, wide), FULL), ((2, spots, deep), LOW)],
        [VMEM] * 4,
        [pltpu.VMEM((chans, 2, spots, 2 * chans_in), LOW)]
        + entry_scratch
        + [
            pltpu.VMEM((spots + 2 * GAP, deep), FULL),
            pltpu.VMEM((3, spots + pitch, deep), LOW),
            pltpu.SemaphoreType.DMA((7 * chans,)),
            pltpu.SemaphoreType.DMA((chans,)),
        ],
        "entry_forward",
        conv_flops // 2,
    )
    mid_shards = []

    def second_hop(layer):
        return lambda value: mid_shards.append(gathered(layer, plan, (value,)))

    mid_second = tied(conv_mid_w[1], stats)
    stats = micro_sums(stats, plan, (), [("start", second_hop(mid_first))])
    mid_third = tied(conv_mid_w[2], stats)
    stat0, statp = stats[0:2], stats[2:4]

    weight_scratch = pltpu.VMEM((3, 3, wide, wide), LOW)
    shard_sems = pltpu.SemaphoreType.DMA((chans,))

    def mid_forward(layers, sources, source_stats, weights, name):
        outs = [field, ((2, wide), FULL), ((spots, wide), LOW)]
        if len(layers) == 2:
            outs.append(field)
        k = len(layers)
        return call(
            functools.partial(mid_forward_kernel, plan, layers),
            (chan_at, inv, marks, pars, *sources, *source_stats, *weights),
            [SMEM, SMEM] + [VMEM] * (2 + 2 * k) + [HBM] * chans,
            outs,
            [VMEM] * len(outs),
            [weight_scratch, padded, pltpu.VMEM((3, spots + 2 * pitch, wide), LOW), shard_sems],
            name,
            0 if name in HIDERS else conv_flops,
        )

    z2, stat1, a_first = mid_forward((0,), (z0,), (stat0,), mid_shards[0], "mid_forward_a")
    og_parts = swapped(tied(grad_spread, stat1), plan)
    stat1 = micro_sums(stat1, plan, (), [("start", second_hop(mid_second))])
    z3, stat3, a_second, h1 = mid_forward(
        (1, 2), (z2, zp), (stat1, statp), mid_shards[1], "mid_forward_b"
    )
    stat3 = micro_sums(stat3, plan, (), [("start", second_hop(mid_third))])
    z4, stat4, a_third = mid_forward((3,), (z3,), (stat3,), mid_shards[2], "mid_forward_c")
    stat4 = micro_sums(tied(stat4, *og_parts[1:]), plan)

    block, gh2, back4 = call(
        functools.partial(head_kernel, plan),
        (chan_at, inv, marks, pars, z4, stat4, h1, *og_parts),
        [SMEM, SMEM] + [VMEM] * (5 + chans),
        [((chans, spots, chans_out), LOW), field, ((2, wide), FULL)],
        [VMEM] * 3,
        [pltpu.VMEM((chans, spots, chans_out), LOW)],
        "head",
    )
    back4 = micro_sums(back4, plan)
    block_parts = swapped(block, plan)

    def mid_backward(j, kind, g, z, stat, back, weights, others, extra_outs, name):
        count = 3 if kind == "join" else 2
        outs = [((3, spots + 2 * pitch, wide), LOW), field, ((count, wide), FULL)] + extra_outs
        return call(
            functools.partial(mid_backward_kernel, plan, j, kind),
            (chan_at, inv, marks, pars, g, z, stat, back, *weights, *others),
            [SMEM, SMEM] + [VMEM] * 6 + [HBM] * chans + [VMEM] * len(others),
            outs,
            [VMEM] * len(outs),
            [weight_scratch, padded, padded, shard_sems],
            name,
            0 if name in HIDERS else conv_flops,
        )

    def mid_weight(a, ga, name):
        return call(
            functools.partial(mid_weight_kernel, plan),
            (chan_at, a, ga),
            [SMEM, VMEM, VMEM],
            [((chans // 2, 9 * chans_out, wide), LOW)] * 2,
            [VMEM, VMEM],
            [pltpu.VMEM((wide, spots), LOW)] * 2,
            name,
            0 if name in HIDERS else conv_flops,
        )
    ga_third, g3, back3 = mid_backward(
        4, "plain", gh2, z4, stat4, back4, mid_shards[2], (z3, stat3), [], "mid_backward_c"
    )
    sums_of = {}

    def weigh(key, a, ga, order, behind=()):
        def job(value, far):
            keep, send = mid_weight(tied(a, value), ga, "mid_weight_" + key)
            others = far + [part for other in behind for part in sums_of[other].received]
            if others:
                send = tied(send, *others)
            sums_of[key] = WeightSum(keep, send, plan, order)
            return [send] + [sums_of[other].advance(send) for other in behind]

        return job

    def step(key):
        return lambda value: sums_of[key].advance(value)

    back3 = micro_sums(
        tied(back3, *block_parts[1:]), plan,
        [weigh("c", a_third, ga_third, ["c", (0,), (1,), (2,)])],
        [("one", step("c"))],
    )
    ga_second, gh1, back12 = mid_backward(
        3, "join", g3, z3, stat3, back3, mid_shards[1], (z2, zp, stat1, statp, gh2), [],
        "mid_backward_b",
    )
    back12 = micro_sums(
        back12, plan, [weigh("b", a_second, ga_second, ["c", (1,), (0,), (2,)], "c")], [("one", step("b"))]
    )
    ga_first, g1, back0, gzp = mid_backward(
        1, "entry", gh1, z2, stat1, back12, mid_shards[0], (z0, stat0, zp, statp),
        [((spots, wide), LOW)], "mid_backward_a",
    )
    back0 = micro_sums(
        back0, plan,
        [weigh("a", a_first, ga_first, [(0,), "c", (1,), (2,)], "cb")],
        [("one", step("c"))],
    )
    (gm,) = call(
        functools.partial(entry_norm_kernel, plan),
        (inv, marks, pars, g1, z0, stat0, back0),
        [SMEM] + [VMEM] * 6,
        [((2, spots + pitch, wide), LOW)],
        [VMEM],
        [padded],
        "entry_norm",
    )
    token = sums_of["a"].advance(gm)
    (gx,) = call(
        functools.partial(entry_backward_kernel, plan),
        (marks, tied(gm, token), gzp, *entry_shards),
        [VMEM] * 3 + [ANY] * chans,
        [((chans, 2, spots, 2 * chans_in), LOW)],
        [VMEM],
        entry_scratch + [pltpu.SemaphoreType.DMA((7 * chans,))],
        "entry_backward",
    )
    gx_parts = swapped(gx, plan)
    keep, send = call(
        functools.partial(entry_weight_kernel, plan),
        (xm, tied(gm, gx), gzp),
        [VMEM] * 3,
        [((chans // 2, 10 * chans_in, wide), LOW)] * 2,
        [VMEM] * 2,
        [pltpu.VMEM((2, deep, spots), LOW)],
        "entry_weight",
    )
    send = tied(
        send, gx_parts[chans // 2], *[part for key in "abc" for part in sums_of[key].received]
    )
    sums_of["e"] = WeightSum(keep, send, plan, [(1,), (0,), "c", (2,)])

    def chain(last, keys):
        for key in keys:
            last = sums_of[key].advance(last)
        return last

    def joined(kernel, parts, shape, axis, extra, dtype, whole, name):
        edge = tuple(extra if i == axis else n for i, n in enumerate(shape))
        return call(
            functools.partial(kernel, plan),
            (chan_at, *parts),
            [SMEM] + [VMEM] * chans,
            [(shape, dtype), (edge, LOW)],
            [VMEM] * 2,
            [pltpu.VMEM(whole, LOW)],
            name,
        )

    def topped(main, tail, axis):
        first = lax.slice_in_dim(main, 0, tail.shape[axis], axis=axis) + tail.astype(main.dtype)
        return lax.dynamic_update_slice(main, first, (0, 0, 0))

    token = chain(send, "cab")
    token = chain(tied(token, gx_parts[-1]), "e")
    gx_parts[0] = tied(gx_parts[0], token)
    feature_grad, feature_tail = joined(
        join_features_kernel, gx_parts, features.shape, 2, EXTRA * 4 * width, FULL,
        (chans, 2, spots, 2 * chans_in), "join_features",
    )
    token = feature_tail
    feature_tail = to_next(feature_tail)
    token = chain(token, "be")
    block_parts[0] = tied(block_parts[0], token)
    block_out, block_tail = joined(
        join_rows_kernel, block_parts, out_grad.shape, 1, EXTRA * width, LOW,
        (chans, spots, chans_out), "join_rows",
    )
    token = block_tail
    block_tail = to_next(block_tail)
    token = chain(token, "aecb")
    feature_grad = topped(feature_grad, tied(feature_tail, token), 2)
    block_out = jnp.swapaxes(topped(block_out, tied(block_tail, token), 1), 1, 2)
    token = chain(token, "eabeaea")

    def mine(key):
        return sums_of[key].mine(sums_of[key].last[0])

    last = jnp.stack([mine(key) for key in "abce"]).astype(jnp.int32)
    (conv_mid_grad,) = call(
        mid_assembly_kernel,
        (last, *[part for key in "abc" for part in sums_of[key].halves(token)]),
        [SMEM] + [VMEM] * 6,
        [((3, 9 * chans_out, wide), FULL)],
        [HBM],
        [pltpu.VMEM((3, 9 * chans_out, wide), FULL), pltpu.SemaphoreType.DMA((3,))],
        "mid_assembly",
    )
    entry_own, entry_other = sums_of["e"].halves(token)
    entry_own = tied(entry_own, conv_mid_grad)
    conv_mid_grad = conv_mid_grad.reshape(3, 3, 3, chans_out, wide)
    conv_in_grad, proj_grad = call(
        entry_assembly_kernel,
        (last, entry_own, entry_other),
        [SMEM] + [VMEM] * 2,
        [((9 * chans_in, wide), FULL), ((chans_in, wide), FULL)],
        [HBM] * 2,
        [pltpu.VMEM((10 * chans_in, wide), FULL), pltpu.SemaphoreType.DMA((2,))],
        "entry_assembly",
    )
    conv_in_grad = conv_in_grad.reshape(3, 3, chans_in, wide)

    sums = jnp.stack(
        [back0[1], back12[1], back12[2], back3[1], back4[1]]
        + [back0[0], back12[0], back12[0], back3[0], back4[0]]
    )
    sums = sums + flipped(sums, "chan", splits)
    sums = lax.dynamic_slice_in_dim(sums, chan * chans_out, chans_out, 1)
    return (
        block_out, feature_grad, conv_in_grad, proj_grad, conv_mid_grad, sums[:5], sums[5:],
    )


def solution(mesh):
    placed = (
        P(None, "chan", "space"),
        P(),
        P(None, None, "chan", None),
        P("chan", None),
        P(None, None, None, "chan", None),
        P(None, "chan"),
        P(None, "chan"),
        P(None, "chan", "space"),
    )
    return jax.shard_map(
        shards,
        mesh=mesh,
        in_specs=placed,
        out_specs=(
            P(None, "chan", "space"),
            P(None, "chan", "space"),
            P(None, None, "chan", None),
            P("chan", None),
            P(None, None, None, "chan", None),
            P(None, "chan"),
            P(None, "chan"),
        ),
        check_vma=False,
    )
```
